32 devices in a mesh: fsdp: 8 (over y, x, core), sp: 4 (over z).
Axes of the slice: x: 2, y: 2, z: 4, core: 2. Of those that a mesh axis runs over, the one named last changes fastest.
Arguments:
- land: bfloat16 [8, 32, 64, 512], P('fsdp', 'sp'), may hold values from -20 to 20
- port: bfloat16 [8, 64, 32, 512], P('fsdp', 'sp'), may hold values from -20 to 20
- to_local: bfloat16 [2, 9, 512, 128], P(None, None, ('fsdp', 'sp')), may hold values from -0.09375 to 0.09375
- to_global: bfloat16 [2, 9, 128, 384], P(None, None, None, ('fsdp', 'sp')), may hold values from -0.1875 to 0.1875
- reduce_weight: bfloat16 [2, 384, 192], P(None, ('fsdp', 'sp')), may hold values from -0.3125 to 0.3125
- freq_weight: bfloat16 [2, 384, 384], P(None, ('fsdp', 'sp')), may hold values from -0.3125 to 0.3125
- expand_weight: bfloat16 [2, 192, 384], P(None, None, ('fsdp', 'sp')), may hold values from -0.4375 to 0.4375
- spec_gain: float32 [2, 192], replicated, may hold values from 0.1 to 1.9
- spec_bias: float32 [2, 192], replicated, may hold values from -3 to 3
- freq_gain: float32 [2, 384], replicated, may hold values from 0.1 to 1.9
- freq_bias: float32 [2, 384], replicated, may hold values from -3 to 3
- out_gain: float32 [2, 512], replicated, may hold values from 0.1 to 1.9
- out_bias: float32 [2, 512], replicated, may hold values from -3 to 3
- cot_land: bfloat16 [8, 32, 64, 512], P('fsdp', 'sp'), may hold values from -6 to 6
- cot_port: bfloat16 [8, 64, 32, 512], P('fsdp', 'sp'), may hold values from -6 to 6
Outputs:
- land_out: bfloat16 [8, 32, 64, 512], P('fsdp', 'sp')
- port_out: bfloat16 [8, 64, 32, 512], P('fsdp', 'sp')
- land_grad: bfloat16 [8, 32, 64, 512], P('fsdp', 'sp')
- port_grad: bfloat16 [8, 64, 32, 512], P('fsdp', 'sp')
- to_local_grad: float32 [2, 9, 512, 128], P(None, None, ('fsdp', 'sp'))
- to_global_grad: float32 [2, 9, 128, 384], P(None, None, None, ('fsdp', 'sp'))
- reduce_grad: float32 [2, 384, 192], P(None, ('fsdp', 'sp'))
- freq_grad: float32 [2, 384, 384], P(None, ('fsdp', 'sp'))
- expand_grad: float32 [2, 192, 384], P(None, None, ('fsdp', 'sp'))
- spec_gain_grad: float32 [2, 192], replicated
- spec_bias_grad: float32 [2, 192], replicated
- freq_gain_grad: float32 [2, 384], replicated
- freq_bias_grad: float32 [2, 384], replicated
- out_gain_grad: float32 [2, 512], replicated
- out_bias_grad: float32 [2, 512], replicated
The draws below stay inside these ranges and needn't reach their ends.
All inputs are finite; a program needn't handle non-finite values.
Results may differ from the reference program's by a relative error of at most 0.018.
Values may be sent and summed in bfloat16 or wider, within the bound.
No kernel may reach another device: no remote copies, remote signals or barrier semaphores. Data moves between devices by JAX's collectives and lax.ppermute only.
A program may use at most 192 MiB of HBM per device.

```python
import jax
import jax.numpy as jnp
from jax import lax

LOCAL = 128
GLOBAL = 384
HALF = 192
SHORT = 32
LONG = 64
SECTIONS = 2
IMGS = 8


def rising(length):
    return 3.0 ** (lax.iota(jnp.float32, length) / (length - 1) - 0.5)


def combine(base, rows_scale, shift_key, channels):
    offset = 0.5 * jax.random.truncated_normal(shift_key, -2.0, 2.0, (1, 1, 1, channels), jnp.float32)
    image_scale = rising(base.shape[0]).reshape(base.shape[0], 1, 1, 1)
    return image_scale * rows_scale * (base + offset)


def draw_land(key, part):
    key = jax.random.fold_in(key, 11)
    base_key = jax.random.fold_in(key, 0)
    shift_key = jax.random.fold_in(key, 2)
    channels = LOCAL + GLOBAL
    full_shape = (IMGS, SHORT, LONG, channels)
    base = jax.random.truncated_normal(base_key, -4.0, 4.0, full_shape, jnp.float32)
    rows_scale = rising(SHORT).reshape(1, SHORT, 1, 1)
    return combine(base, rows_scale, shift_key, channels).astype(jnp.bfloat16)


def draw_port(key, part):
    key = jax.random.fold_in(key, 23)
    base_key = jax.random.fold_in(key, 0)
    shift_key = jax.random.fold_in(key, 2)
    channels = LOCAL + GLOBAL
    full_shape = (IMGS, LONG, SHORT, channels)
    base = jax.random.truncated_normal(base_key, -4.0, 4.0, full_shape, jnp.float32)
    rows_scale = rising(LONG).reshape(1, LONG, 1, 1)
    return combine(base, rows_scale, shift_key, channels).astype(jnp.bfloat16)


def level_of(key, extent, cuts, low, high):
    factor_of = 1.0
    for position, blocks in cuts:
        steps = jax.random.uniform(jax.random.fold_in(jax.random.fold_in(key, 6), position), (blocks,), jnp.float32, low / len(cuts), high / len(cuts))
        factor_of = factor_of * jnp.repeat(jnp.exp(steps), extent[position] // blocks).reshape((-1,) + (1,) * (len(extent) - 1 - position))
    return factor_of


def bell_draw(rng, shape, width, reach, pieces=(), kind=jnp.bfloat16):
    entries = jax.random.normal(rng, shape, jnp.float32) * width
    if len(pieces) > 0:
        entries = level_of(rng, shape, pieces, -0.22, 0.18) * entries
    return jnp.clip(entries, min=-reach, max=reach).astype(kind)


def setup_inputs(seed: int = 0) -> dict:
    splits = jax.random.split(jax.random.key(seed), 16)
    return {
        "land": draw_land(jax.random.fold_in(splits[15], 71), 0),
        "port": draw_port(jax.random.fold_in(splits[15], 71), 0),
        "to_local": bell_draw(splits[2], (SECTIONS, 9, LOCAL + GLOBAL, LOCAL), (9 * (LOCAL + GLOBAL)) ** -0.5, 0.09375, ((2, 32),)),
        "to_global": bell_draw(splits[3], (SECTIONS, 9, LOCAL, GLOBAL), (9 * LOCAL) ** -0.5, 0.1875, ((3, 32),)),
        "reduce_weight": bell_draw(splits[4], (SECTIONS, GLOBAL, HALF), GLOBAL ** -0.5, 0.3125, ((1, 32),)),
        "freq_weight": bell_draw(splits[5], (SECTIONS, GLOBAL, GLOBAL), GLOBAL ** -0.5, 0.3125, ((1, 32),)),
        "expand_weight": bell_draw(splits[6], (SECTIONS, HALF, GLOBAL), HALF ** -0.5, 0.4375, ((2, 32),)),
        "spec_gain": jnp.clip(1.0 + 0.18 * jax.random.normal(splits[7], (SECTIONS, HALF), jnp.float32), 0.1, 1.9),
        "spec_bias": bell_draw(splits[8], (SECTIONS, HALF), 0.5, 3.0, (), jnp.float32),
        "freq_gain": jnp.clip(1.0 + 0.18 * jax.random.normal(splits[9], (SECTIONS, GLOBAL), jnp.float32), 0.1, 1.9),
        "freq_bias": bell_draw(splits[10], (SECTIONS, GLOBAL), 0.5, 3.0, (), jnp.float32),
        "out_gain": jnp.clip(1.0 + 0.18 * jax.random.normal(splits[11], (SECTIONS, LOCAL + GLOBAL), jnp.float32), 0.1, 1.9),
        "out_bias": bell_draw(splits[12], (SECTIONS, LOCAL + GLOBAL), 0.5, 3.0, (), jnp.float32),
        "cot_land": bell_draw(splits[13], (IMGS, SHORT, LONG, LOCAL + GLOBAL), 1.0, 6.0, ((0, 8), (1, 4))),
        "cot_port": bell_draw(splits[14], (IMGS, LONG, SHORT, LOCAL + GLOBAL), 1.0, 6.0, ((0, 8), (1, 4))),
    }


epsilon = 1e-05
highest = lax.Precision.HIGHEST

@jax.custom_vjp
def low(v):
    return lax.optimization_barrier(v.astype(jnp.bfloat16)).astype(jnp.float32)

@jax.custom_vjp
def low_back(v):
    return v

def low_keep(v):
    return (low(v), None)

def low_pass(kept, grad):
    return (grad,)

def back_keep(v):
    return (v, None)

def back_low(kept, grad):
    return (low(grad),)
low.defvjp(low_keep, low_pass)
low_back.defvjp(back_keep, back_low)

def mixing(values, matrix):
    return jnp.einsum('bhwc,cd->bhwd', values, matrix, precision=highest)

def conv_three(values, kernel):
    shaped = kernel.reshape(3, 3, kernel.shape[1], kernel.shape[2])
    return lax.conv_general_dilated(values, shaped, (1, 1), ((1, 1), (1, 1)), dimension_numbers=('NHWC', 'HWIO', 'NHWC'), precision=highest)

def batch_norm(values, gain, bias):
    center = lax.optimization_barrier(jnp.mean(values, axis=(0, 1, 2)))
    centered = values - center
    spread = lax.optimization_barrier(jnp.mean(centered * centered, axis=(0, 1, 2)))
    return centered * lax.rsqrt(spread + epsilon) * gain + bias

def section_forward(values, weights):
    local_kernel, global_kernel, reduce_kernel, freq_kernel, expand_kernel, spec_gain, spec_bias, freq_gain, freq_bias, out_gain, out_bias = weights
    narrow = local_kernel.shape[2]
    map_rows = values.shape[1]
    map_cols = values.shape[2]
    rounded = low(values)
    local_pre = conv_three(rounded, local_kernel)
    global_pre = conv_three(rounded[..., :narrow], global_kernel)
    reduced = low_back(mixing(rounded[..., narrow:], reduce_kernel))
    hidden = jax.nn.gelu(batch_norm(reduced, spec_gain, spec_bias))
    spectrum = jnp.fft.rfft2(hidden, axes=(1, 2), norm='ortho')
    spectrum_low = low(jnp.concatenate([spectrum.real, spectrum.imag], axis=3))
    mixed = low_back(mixing(spectrum_low, freq_kernel))
    freq_act = jax.nn.gelu(batch_norm(mixed, freq_gain, freq_bias))
    half_width = freq_act.shape[3] // 2
    returned = jnp.fft.irfft2(freq_act[..., :half_width] + 1j * freq_act[..., half_width:], s=(map_rows, map_cols), axes=(1, 2), norm='ortho')
    summed_low = low(hidden + returned)
    both_pre = low_back(jnp.concatenate([local_pre, global_pre + mixing(summed_low, expand_kernel)], axis=3))
    return jax.nn.gelu(batch_norm(both_pre, out_gain, out_bias))

def reference(land, port, to_local, to_global, reduce_weight, freq_weight, expand_weight, spec_gain, spec_bias, freq_gain, freq_bias, out_gain, out_bias, cot_land, cot_port):
    params = tuple((item.astype(jnp.float32) for item in (to_local, to_global, reduce_weight, freq_weight, expand_weight, spec_gain, spec_bias, freq_gain, freq_bias, out_gain, out_bias)))
    checked = jax.checkpoint(section_forward)

    def forward(weights, land_in, port_in):
        results = []
        for source in (land_in, port_in):
            current = source
            for section_index in range(SECTIONS):
                current = checked(current, tuple((item[section_index] for item in weights)))
            results.append(source + current)
        return (results[0], results[1])
    (land_out, port_out), pullback = jax.vjp(forward, params, land.astype(jnp.float32), port.astype(jnp.float32))
    param_grads, land_grad, port_grad = pullback((cot_land.astype(jnp.float32), cot_port.astype(jnp.float32)))
    return (land_out.astype(jnp.bfloat16), port_out.astype(jnp.bfloat16), land_grad.astype(jnp.bfloat16), port_grad.astype(jnp.bfloat16), param_grads[0], param_grads[1], param_grads[2], param_grads[3], param_grads[4], param_grads[5], param_grads[6], param_grads[7], param_grads[8], param_grads[9], param_grads[10])
```

```python
import math

import jax
import jax.numpy as jnp
import numpy as np
from jax import lax
from jax.sharding import Mesh, PartitionSpec as P

EPS = 1e-05
LINE = ("c", "k", "z", "e")
KIND = ("g", "c", "z", "e")
PART = ("c", "e")
ALL = ("g", "c", "k", "z", "e")
f32 = jnp.float32
bf16 = jnp.bfloat16


def routes(e_n):
    s_n = 4 * e_n
    count = 2 * s_n
    edges = []
    for c in range(2):
        for s in range(s_n):
            src = c * s_n + s
            for half in range(2):
                target = half * s_n + (0 * 2 + c) * e_n + s // 4
                edges.append((src, half, target, s % 4))
            part = s // 2
            for half in range(2):
                target = (part // e_n) * s_n + (1 * 2 + c) * e_n + part % e_n
                edges.append((src, 2 + half, target, (s % 2) * 2 + half))
    rounds = []
    left = list(edges)
    for _ in range(4):
        owner = {}

        def augment(src, seen):
            for edge in left:
                if edge[0] == src and edge[2] not in seen:
                    seen.add(edge[2])
                    if edge[2] not in owner or augment(owner[edge[2]][0], seen):
                        owner[edge[2]] = edge
                        return True
            return False

        for src in range(count):
            assert augment(src, set())
        chosen = list(owner.values())
        for edge in chosen:
            left.remove(edge)
        pairs = [(edge[0], edge[2]) for edge in chosen]
        sent = np.zeros(count, np.int32)
        slot = np.zeros(count, np.int32)
        for edge in chosen:
            sent[edge[0]] = edge[1]
            slot[edge[2]] = edge[3]
        rounds.append((pairs, sent, slot))
    return rounds


def transform_tables(e_n, land_shape, port_shape):
    parts = 2 * e_n
    shapes = (land_shape, port_shape)
    most = max(rows * (cols // 2 + 1) for rows, cols in shapes)
    per_part = -(-most // (16 * parts)) * 16
    forward, inverse, weight, counts = [], [], [], []
    for kind, (rows, cols) in enumerate(shapes):
        half = cols // 2 + 1
        total = rows * half
        point = np.arange(per_part * parts)
        valid = point < total
        kr, f = point // half, point % half
        tiles = []
        for part in range(parts):
            c, e = part // e_n, part % e_n
            if kind == 0:
                h = np.arange(rows // e_n) + e * (rows // e_n)
                w = np.arange(cols // 2) + c * (cols // 2)
            else:
                h = np.arange(rows // parts) + part * (rows // parts)
                w = np.arange(cols)
            tiles.append((np.repeat(h, len(w)), np.tile(w, len(h))))
        cell_h = np.concatenate([tile[0] for tile in tiles])
        cell_w = np.concatenate([tile[1] for tile in tiles])
        size = rows * cols
        phase = (kr[:, None] * cell_h[None, :] * cols + f[:, None] * cell_w[None, :] * rows) % size
        angle = phase * (2.0 * math.pi / size)
        table = np.stack([np.cos(angle), -np.sin(angle)]) * valid[None, :, None]
        table = table.astype(np.float32).astype(jnp.bfloat16)
        cells = size // parts
        factor = np.where((f == 0) | (2 * f == cols), 1.0, 2.0) * valid
        counts.append([int(valid[p * per_part : (p + 1) * per_part].sum()) for p in range(parts)])
        for part in range(parts):
            order = [(part + step) % parts for step in range(parts)]
            own_points = slice(part * per_part, (part + 1) * per_part)
            own_cells = slice(part * cells, (part + 1) * cells)
            forward.append(
                np.concatenate([table[:, own_points, q * cells : (q + 1) * cells] for q in order], axis=2)
            )
            back = np.concatenate([table[:, q * per_part : (q + 1) * per_part, own_cells] for q in order], axis=1)
            inverse.append(np.ascontiguousarray(back.transpose(0, 2, 1)))
            weight.append(factor[own_points].astype(np.float32))
    return np.stack(forward), np.stack(inverse), np.stack(weight), np.asarray(counts, np.int32)


def pick(table, index):
    return lax.dynamic_index_in_dim(jnp.asarray(table), index, 0, keepdims=False)


def to_tile(land, port, rounds):
    rows = land.shape[1]
    wide = port.shape[2]
    units = jnp.stack([land[0, :, :wide], land[0, :, wide:], port[0, :rows], port[0, rows:]])
    me = lax.axis_index(LINE)
    got = []
    for pairs, sent, _ in rounds:
        got.append(lax.ppermute(pick(units, pick(sent, me)), LINE, pairs))
    got = jnp.stack(got)
    slots = np.stack([slot for _, _, slot in rounds], axis=1)
    order = pick(np.argsort(slots, axis=1).astype(np.int32), me)
    return jnp.concatenate([pick(got, order[i]) for i in range(4)], axis=0)


def from_tile(tile, rounds):
    rows = tile.shape[0] // 4
    units = tile.reshape((4, rows) + tile.shape[1:])
    me = lax.axis_index(LINE)
    got = []
    for pairs, _, slot in rounds:
        got.append(lax.ppermute(pick(units, pick(slot, me)), LINE, [(b, a) for a, b in pairs]))
    got = jnp.stack(got)
    sents = np.stack([sent for _, sent, _ in rounds], axis=1)
    order = pick(np.argsort(sents, axis=1).astype(np.int32), me)
    parts = [pick(got, order[i]) for i in range(4)]
    land = jnp.concatenate(parts[:2], axis=1)
    port = jnp.concatenate(parts[2:], axis=0)
    return land[None], port[None]


def share(block):
    parts = lax.axis_size(PART)
    pieces = [block]
    for step in range(1, parts):
        pieces.append(lax.ppermute(block, PART, [((p + step) % parts, p) for p in range(parts)]))
    return jnp.concatenate(pieces, axis=0)


def with_halo(tile):
    rows, cols, channels = tile.shape
    c, k = lax.axis_index("c"), lax.axis_index("k")
    e_n = lax.axis_size("e")
    swap = [(0, 1), (1, 0)]
    zero = jnp.zeros((), tile.dtype)
    col_edge = jnp.where(c == 0, tile[:, -1], tile[:, 0])
    if e_n == 1:
        row_edge = jnp.where(c == 0, tile[-1], tile[0])
        got = lax.ppermute(jnp.where(k == 0, col_edge, row_edge), "c", swap)
        left = jnp.where((k == 0) & (c == 1), got, zero)
        right = jnp.where((k == 0) & (c == 0), got, zero)
        top = jnp.where((k == 1) & (c == 1), got, zero)
        bottom = jnp.where((k == 1) & (c == 0), got, zero)
        top = jnp.pad(top, ((1, 1), (0, 0)))
        bottom = jnp.pad(bottom, ((1, 1), (0, 0)))
        wide = jnp.concatenate([left[:, None], tile, right[:, None]], axis=1)
    else:
        got = lax.ppermute(col_edge, "c", swap)
        left = jnp.where((k == 0) & (c == 1), got, zero)
        right = jnp.where((k == 0) & (c == 0), got, zero)
        wide = jnp.concatenate([left[:, None], tile, right[:, None]], axis=1)
        ahead = []
        for cc in range(2):
            for e in range(e_n):
                if e + 1 < e_n:
                    ahead.append(((cc * 2 + 0) * e_n + e, (cc * 2 + 0) * e_n + e + 1))
                p = cc * e_n + e + 1
                if p < 2 * e_n:
                    ahead.append(((cc * 2 + 1) * e_n + e, ((p // e_n) * 2 + 1) * e_n + p % e_n))
        axes = ("c", "k", "e")
        top = lax.ppermute(wide[-1], axes, ahead)
        bottom = lax.ppermute(wide[0], axes, [(b, a) for a, b in ahead])
    return jnp.concatenate([top[None], wide, bottom[None]], axis=0)


def spread(values, axes):
    count = lax.axis_size(axes)
    return lax.all_to_all(jnp.broadcast_to(values[None], (count,) + values.shape), axes, 0, 0, tiled=True)


def norm_stats(values, counts, mask=None):
    me = lax.axis_index(KIND)
    own = counts[me]
    local_sum = jnp.sum(values, axis=0)
    centered = values - local_sum / own
    if mask is not None:
        centered = centered * mask
    local_square = jnp.sum(centered * centered, axis=0)
    every = spread(jnp.stack([local_sum, local_square]), KIND)
    total = jnp.sum(counts)
    mean = jnp.sum(every[:, 0], axis=0) / total
    apart = every[:, 0] / counts[:, None] - mean
    square = jnp.sum(every[:, 1] + counts[:, None] * apart * apart, axis=0)
    return mean, lax.rsqrt(square / total + EPS)


def gelu(v):
    return 0.5 * v * (1.0 + jnp.tanh(math.sqrt(2.0 / math.pi) * (v + 0.044715 * v * v * v)))


def gelu_slope(v):
    k = math.sqrt(2.0 / math.pi)
    t = jnp.tanh(k * (v + 0.044715 * v * v * v))
    return 0.5 * (1.0 + t) + 0.5 * v * (1.0 - t * t) * (k * (1.0 + 3.0 * 0.044715 * v * v))


def norm_back(q, normed, gain, inv, total):
    every = spread(jnp.stack([jnp.sum(q, axis=0), jnp.sum(q * normed, axis=0)]), KIND)
    sums = jnp.sum(every, axis=0)
    return gain * inv * (q - sums[0] / total - normed * (sums[1] / total)), sums


def dot(a, b):
    return lax.dot_general(a, b, (((1,), (0,)), ((), ())), preferred_element_type=f32)


def dot_t(a, b):
    return lax.dot_general(a, b, (((1,), (1,)), ((), ())), preferred_element_type=f32)


def outer(a, b):
    return lax.dot_general(a, b, (((0,), (0,)), ((), ())), preferred_element_type=f32)


def unfold(padded):
    rows, cols, channels = padded.shape[0] - 2, padded.shape[1] - 2, padded.shape[2]
    return jnp.concatenate(
        [padded[t // 3 : t // 3 + rows, t % 3 : t % 3 + cols].reshape(rows * cols, channels) for t in range(9)],
        axis=1,
    )


def gather_rows(shard):
    return lax.all_gather(shard, ALL, tiled=True)


def per_device(plan, *args):
    (
        land,
        port,
        to_local,
        to_global,
        reduce_weight,
        freq_weight,
        expand_weight,
        spec_gain,
        spec_bias,
        freq_gain,
        freq_bias,
        out_gain,
        out_bias,
        cot_land,
        cot_port,
    ) = args
    rounds, forward_table, inverse_table, weight_table, point_counts, cells_of_kind = plan
    sections = to_local.shape[0]
    devices = lax.axis_size(ALL)
    own_in = to_local.shape[2]
    own_out = to_global.shape[3]
    narrow = to_local.shape[3]
    channels = own_in * devices
    broad = channels - narrow
    half = reduce_weight.shape[2]
    k, part = lax.axis_index("k"), lax.axis_index(PART)
    variant = k * lax.axis_size(PART) + part
    g_n, z_n, e_n = lax.axis_size("g"), lax.axis_size("z"), lax.axis_size("e")

    x = to_tile(land, port, rounds)
    rows, cols = x.shape[:2]
    cells = rows * cols
    size = cells * lax.axis_size(PART)
    scale = 1.0 / math.sqrt(size)
    maps = g_n * z_n

    small, kernels = [], []
    for s in range(sections):
        packed = jnp.concatenate(
            [freq_weight[s], reduce_weight[s], jnp.transpose(expand_weight[s])], axis=1
        )
        full = gather_rows(packed)
        wide = full.shape[1] - 2 * half
        small.append((full[:, wide : wide + half], full[:, :wide], full[:, wide + half :]))
    for s in range(sections):
        taps_local = jnp.reshape(to_local[s], (1, 9 * own_in, narrow))
        taps_global = jnp.transpose(to_global[s], (2, 0, 1)).reshape(1, own_out * 9, narrow)
        full = gather_rows(jnp.concatenate([taps_local, taps_global], axis=1))
        local_kernel = full[:, : 9 * own_in].reshape(devices, 9, own_in, narrow)
        local_kernel = jnp.transpose(local_kernel, (1, 0, 2, 3)).reshape(9, channels, narrow)
        global_kernel = full[:, 9 * own_in :].reshape(devices * own_out, 9 * narrow)
        kernels.append((local_kernel, global_kernel))
    cot = to_tile(cot_land, cot_port, rounds)

    forward = pick(forward_table, variant)
    inverse = pick(inverse_table, variant)
    factor = pick(weight_table, variant)[:, None]
    mask = jnp.where(factor > 0.0, 1.0, 0.0)
    cell_counts = jnp.full((maps * 2 * e_n,), cells, f32)
    by_part = pick(point_counts, k).astype(f32)
    freq_counts = jnp.broadcast_to(by_part.reshape(1, 2, 1, e_n), (g_n, 2, z_n, e_n)).reshape(-1)
    cell_total = float(maps * size)
    freq_total = jnp.sum(freq_counts)

    def to_spectrum(values):
        whole = share(values.astype(bf16))
        return dot(forward[0], whole) * scale, dot(forward[1], whole) * scale

    def from_spectrum(values):
        whole = share(values.astype(bf16))
        return (dot(inverse[0], whole[:, :half]) + dot(inverse[1], whole[:, half:])) * scale

    state = x
    kept = []
    for s in range(sections):
        reduce_kernel, freq_kernel, expand_t = small[s]
        local_kernel, global_t = kernels[s]
        low = state.astype(bf16)
        flat = low.reshape(cells, channels)
        padded = with_halo(low)
        reduced = dot(flat[:, narrow:], reduce_kernel)
        mean_1, inv_1 = norm_stats(reduced, cell_counts)
        normed_1 = (reduced - mean_1) * inv_1
        act_1 = normed_1 * spec_gain[s] + spec_bias[s]
        hidden = gelu(act_1)
        real, imag = to_spectrum(hidden)
        real, imag = real.astype(bf16), imag.astype(bf16)
        mixed = dot(real, freq_kernel[:half]) + dot(imag, freq_kernel[half:])
        mean_2, inv_2 = norm_stats(mixed, freq_counts, mask)
        normed_2 = (mixed - mean_2) * inv_2
        act_2 = normed_2 * freq_gain[s] + freq_bias[s]
        returned = from_spectrum(gelu(act_2) * factor)
        summed = (hidden + returned).astype(bf16)
        local_pre = dot(unfold(padded), local_kernel.reshape(9 * channels, narrow))
        global_pre = dot_t(unfold(padded[..., :narrow]), global_t)
        both = jnp.concatenate([local_pre, global_pre + dot_t(summed, expand_t)], axis=1)
        mean_3, inv_3 = norm_stats(both, cell_counts)
        normed_3 = (both - mean_3) * inv_3
        act_3 = normed_3 * out_gain[s] + out_bias[s]
        state = gelu(act_3).reshape(rows, cols, channels)
        kept.append(
            (padded, flat, normed_1, inv_1, act_1, real, imag, normed_2, inv_2, act_2, summed, normed_3, inv_3, act_3)
        )
    land_out, port_out = from_tile((x.astype(f32) + state).astype(bf16), rounds)

    grad = cot.astype(f32).reshape(cells, channels)
    weight_shares = [None] * sections
    norm_sums = [None] * sections
    for s in reversed(range(sections)):
        (padded, flat, normed_1, inv_1, act_1, real, imag, normed_2, inv_2, act_2, summed, normed_3, inv_3, act_3) = kept[s]
        reduce_kernel, freq_kernel, expand_t = small[s]
        local_kernel, global_t = kernels[s]
        grad_pre, sums_3 = norm_back(gelu_slope(act_3) * grad, normed_3, out_gain[s], inv_3, cell_total)
        grad_low = grad_pre.astype(bf16)
        grad_local, grad_global = grad_low[:, :narrow], grad_low[:, narrow:]
        grad_summed = dot(grad_global, expand_t)
        freq_real, freq_imag = to_spectrum(grad_summed)
        grad_freq = jnp.concatenate([freq_real, freq_imag], axis=1) * factor
        grad_mixed, sums_2 = norm_back(gelu_slope(act_2) * grad_freq, normed_2, freq_gain[s], inv_2, freq_total)
        mixed_low = grad_mixed.astype(bf16)
        grad_hidden = grad_summed + from_spectrum(dot_t(mixed_low, freq_kernel) * mask)
        grad_reduced, sums_1 = norm_back(gelu_slope(act_1) * grad_hidden, normed_1, spec_gain[s], inv_1, cell_total)
        reduced_low = grad_reduced.astype(bf16)
        into_global = dot_t(reduced_low, reduce_kernel)

        grad_padded = with_halo(grad_low.reshape(rows, cols, channels))
        back_local = jnp.transpose(local_kernel[::-1], (0, 2, 1)).reshape(9 * narrow, channels)
        taps_t = global_t.reshape(broad, 9, narrow)
        back_global = jnp.transpose(taps_t[:, ::-1], (1, 0, 2)).reshape(9 * broad, narrow)
        grad_input = dot(unfold(grad_padded[..., :narrow]), back_local)
        into_local = dot(unfold(grad_padded[..., narrow:]), back_global)
        grad = grad_input + jnp.concatenate([into_local, into_global], axis=1)

        local_grad = outer(unfold(padded), grad_local)
        global_grad = outer(grad_global, unfold(padded[..., :narrow]))
        expand_grad = outer(grad_global, summed)
        freq_grad = jnp.concatenate([outer(real, mixed_low), outer(imag, mixed_low)], axis=0)
        reduce_grad = outer(flat[:, narrow:], reduced_low)
        local_grad = jnp.transpose(local_grad.reshape(9, devices, own_in, narrow), (1, 0, 2, 3))
        local_grad = local_grad.reshape(devices, 9 * own_in, narrow)
        global_grad = global_grad.reshape(devices, own_out * 9, narrow)
        others = jnp.concatenate([freq_grad, reduce_grad, expand_grad], axis=1)
        others = others.reshape(devices, own_out, others.shape[1])
        owned_kernels = owned(jnp.concatenate([local_grad, global_grad], axis=1))
        owned_others = owned(others)
        weight_shares[s] = (
            owned_kernels[: 9 * own_in].reshape(9, own_in, narrow),
            jnp.transpose(owned_kernels[9 * own_in :].reshape(own_out, 9, narrow), (1, 2, 0)),
            owned_others[:, 2 * half : 3 * half],
            owned_others[:, : 2 * half],
            jnp.transpose(owned_others[:, 3 * half :]),
        )
        norm_sums[s] = (sums_1, sums_2, sums_3)
    land_grad, port_grad = from_tile(
        (cot.astype(f32) + grad.reshape(rows, cols, channels)).astype(bf16), rounds
    )
    flat_sums = jnp.concatenate([item.reshape(-1) for s in range(sections) for item in norm_sums[s]])
    flat_sums = flat_sums + lax.ppermute(flat_sums, "k", [(0, 1), (1, 0)])
    gains = [[] for _ in range(6)]
    offset = 0
    for s in range(sections):
        for index, width in enumerate((half, 2 * half, channels)):
            bias_sum = flat_sums[offset : offset + width]
            gain_sum = flat_sums[offset + width : offset + 2 * width]
            offset += 2 * width
            gains[2 * index].append(gain_sum)
            gains[2 * index + 1].append(bias_sum)
    stacked = [jnp.stack([weight_shares[s][i] for s in range(sections)]) for i in range(5)]
    return (land_out, port_out, land_grad, port_grad, *stacked, *[jnp.stack(item) for item in gains])


def owned(shares):
    shape = shares.shape[1:]
    g_n, c_n = lax.axis_size("g"), lax.axis_size("c")
    rest = lax.axis_size(("k", "z", "e"))
    low = shares.astype(bf16).reshape((g_n * c_n, rest) + shape)
    first = lax.all_to_all(low, ("g", "c"), 0, 0, tiled=True)
    first = jnp.sum(first.astype(f32), axis=0).astype(bf16)
    second = lax.all_to_all(first, ("k", "z", "e"), 0, 0, tiled=True)
    return jnp.sum(second.astype(f32), axis=0)


def solution(mesh):
    f_n, s_n = mesh.shape["fsdp"], mesh.shape["sp"]
    e_n = s_n // 4
    fine = Mesh(np.asarray(mesh.devices).reshape(f_n // 2, 2, 2, 2, e_n), ALL)
    maps = P(("g", "c"), ("k", "z", "e"), None, None)
    split = ALL

    def whole(*args):
        land, port = args[0], args[1]
        plan = (
            routes(e_n),
            *transform_tables(e_n, land.shape[1:3], port.shape[1:3]),
            land.shape[1] * land.shape[2],
        )
        weights = (
            P(None, None, split, None),
            P(None, None, None, split),
            P(None, split, None),
            P(None, split, None),
            P(None, None, split),
        )
        return jax.shard_map(
            lambda *local: per_device(plan, *local),
            mesh=fine,
            in_specs=(maps, maps, *weights, P(), P(), P(), P(), P(), P(), maps, maps),
            out_specs=(maps, maps, maps, maps, *weights, P(), P(), P(), P(), P(), P()),
            check_vma=False,
        )(*args)

    return whole
```

```python
import math

import jax
import jax.numpy as jnp
import numpy as np
from jax import lax
from jax.experimental import pallas as pl
from jax.experimental.pallas import tpu as pltpu
from jax.sharding import Mesh, PartitionSpec as P

EPS = 1e-05
LINE = ("c", "k", "z", "e")
KIND = ("g", "c", "z", "e")
PART = ("c", "e")
ALL = ("g", "c", "k", "z", "e")
f32 = jnp.float32
bf16 = jnp.bfloat16


def routes(e_n):
    s_n = 4 * e_n
    count = 2 * s_n
    edges = []
    for c in range(2):
        for s in range(s_n):
            src = c * s_n + s
            for half in range(2):
                target = half * s_n + (0 * 2 + c) * e_n + s // 4
                edges.append((src, half, target, s % 4))
            part = s // 2
            for half in range(2):
                target = (part // e_n) * s_n + (1 * 2 + c) * e_n + part % e_n
                edges.append((src, 2 + half, target, (s % 2) * 2 + half))
    rounds = []
    left = list(edges)
    for _ in range(4):
        owner = {}

        def augment(src, seen):
            for edge in left:
                if edge[0] == src and edge[2] not in seen:
                    seen.add(edge[2])
                    if edge[2] not in owner or augment(owner[edge[2]][0], seen):
                        owner[edge[2]] = edge
                        return True
            return False

        for src in range(count):
            assert augment(src, set())
        chosen = list(owner.values())
        for edge in chosen:
            left.remove(edge)
        pairs = [(edge[0], edge[2]) for edge in chosen]
        sent = np.zeros(count, np.int32)
        slot = np.zeros(count, np.int32)
        for edge in chosen:
            sent[edge[0]] = edge[1]
            slot[edge[2]] = edge[3]
        rounds.append((pairs, sent, slot))
    return rounds


def transform_tables(e_n, land_shape, port_shape):
    parts = 2 * e_n
    shapes = (land_shape, port_shape)
    most = max(rows * (cols // 2 + 1) for rows, cols in shapes)
    per_part = -(-most // (16 * parts)) * 16
    forward, inverse, weight, counts = [], [], [], []
    for kind, (rows, cols) in enumerate(shapes):
        half = cols // 2 + 1
        total = rows * half
        point = np.arange(per_part * parts)
        valid = point < total
        kr, f = point // half, point % half
        tiles = []
        for part in range(parts):
            c, e = part // e_n, part % e_n
            if kind == 0:
                h = np.arange(rows // e_n) + e * (rows // e_n)
                w = np.arange(cols // 2) + c * (cols // 2)
            else:
                h = np.arange(rows // parts) + part * (rows // parts)
                w = np.arange(cols)
            tiles.append((np.repeat(h, len(w)), np.tile(w, len(h))))
        cell_h = np.concatenate([tile[0] for tile in tiles])
        cell_w = np.concatenate([tile[1] for tile in tiles])
        size = rows * cols
        phase = (kr[:, None] * cell_h[None, :] * cols + f[:, None] * cell_w[None, :] * rows) % size
        angle = phase * (2.0 * math.pi / size)
        table = np.stack([np.cos(angle), -np.sin(angle)]) * valid[None, :, None]
        table = table.astype(np.float32).astype(jnp.bfloat16)
        cells = size // parts
        factor = np.where((f == 0) | (2 * f == cols), 1.0, 2.0) * valid
        counts.append([int(valid[p * per_part : (p + 1) * per_part].sum()) for p in range(parts)])
        for part in range(parts):
            order = [(part + step) % parts for step in range(parts)]
            own_points = slice(part * per_part, (part + 1) * per_part)
            own_cells = slice(part * cells, (part + 1) * cells)
            forward.append(
                np.concatenate([table[:, own_points, q * cells : (q + 1) * cells] for q in order], axis=2)
            )
            back = np.concatenate([table[:, q * per_part : (q + 1) * per_part, own_cells] for q in order], axis=1)
            inverse.append(np.ascontiguousarray(back.transpose(0, 2, 1)))
            weight.append(factor[own_points].astype(np.float32))
    return np.stack(forward), np.stack(inverse), np.stack(weight), np.asarray(counts, np.int32)


def pick(table, index):
    return lax.dynamic_index_in_dim(jnp.asarray(table), index, 0, keepdims=False)


def to_tile(land, port, rounds):
    rows = land.shape[1]
    wide = port.shape[2]
    units = jnp.stack([land[0, :, :wide], land[0, :, wide:], port[0, :rows], port[0, rows:]])
    me = lax.axis_index(LINE)
    got = []
    for pairs, sent, _ in rounds:
        got.append(lax.ppermute(pick(units, pick(sent, me)), LINE, pairs))
    got = jnp.stack(got)
    slots = np.stack([slot for _, _, slot in rounds], axis=1)
    order = pick(np.argsort(slots, axis=1).astype(np.int32), me)
    return jnp.concatenate([pick(got, order[i]) for i in range(4)], axis=0)


def from_tile(tile, rounds):
    rows = tile.shape[0] // 4
    units = tile.reshape((4, rows) + tile.shape[1:])
    me = lax.axis_index(LINE)
    got = []
    for pairs, _, slot in rounds:
        got.append(lax.ppermute(pick(units, pick(slot, me)), LINE, [(b, a) for a, b in pairs]))
    got = jnp.stack(got)
    sents = np.stack([sent for _, sent, _ in rounds], axis=1)
    order = pick(np.argsort(sents, axis=1).astype(np.int32), me)
    parts = [pick(got, order[i]) for i in range(4)]
    land = jnp.concatenate(parts[:2], axis=1)
    port = jnp.concatenate(parts[2:], axis=0)
    return land[None], port[None]


def shared(block):
    parts = lax.axis_size(PART)
    pieces = [
        lax.ppermute(block, PART, [((p + step) % parts, p) for p in range(parts)]) for step in range(1, parts)
    ]
    return pieces[0] if parts == 2 else jnp.concatenate(pieces, axis=0)


def edges(tile):
    rows, cols, channels = tile.shape
    c, k = lax.axis_index("c"), lax.axis_index("k")
    e_n = lax.axis_size("e")
    swap = [(0, 1), (1, 0)]
    zero = jnp.zeros((), tile.dtype)
    col_edge = jnp.where(c == 0, tile[:, -1], tile[:, 0])
    if e_n == 1:
        row_edge = jnp.where(c == 0, tile[-1], tile[0])
        got = lax.ppermute(jnp.where(k == 0, col_edge, row_edge), "c", swap)
        left = jnp.pad(jnp.where((k == 0) & (c == 1), got, zero), ((1, 1), (0, 0)))
        right = jnp.pad(jnp.where((k == 0) & (c == 0), got, zero), ((1, 1), (0, 0)))
        top = jnp.where((k == 1) & (c == 1), got, zero)
        bottom = jnp.where((k == 1) & (c == 0), got, zero)
        return top, bottom, left, right
    got = lax.ppermute(col_edge, "c", swap)
    left = jnp.where((k == 0) & (c == 1), got, zero)
    right = jnp.where((k == 0) & (c == 0), got, zero)
    wide = jnp.concatenate([left[:, None], tile, right[:, None]], axis=1)
    ahead = []
    for cc in range(2):
        for e in range(e_n):
            if e + 1 < e_n:
                ahead.append(((cc * 2 + 0) * e_n + e, (cc * 2 + 0) * e_n + e + 1))
            p = cc * e_n + e + 1
            if p < 2 * e_n:
                ahead.append(((cc * 2 + 1) * e_n + e, ((p // e_n) * 2 + 1) * e_n + p % e_n))
    axes = ("c", "k", "e")
    top = lax.ppermute(wide[-1], axes, ahead)
    bottom = lax.ppermute(wide[0], axes, [(b, a) for a, b in ahead])
    left = jnp.concatenate([top[:1], left, bottom[:1]], axis=0)
    right = jnp.concatenate([top[-1:], right, bottom[-1:]], axis=0)
    return top[1:-1], bottom[1:-1], left, right


def spread(values, axes):
    count = lax.axis_size(axes)
    return lax.all_to_all(jnp.broadcast_to(values[None], (count,) + values.shape), axes, 0, 0, tiled=True)


def gelu_parts(v):
    k = math.sqrt(2.0 / math.pi)
    square = v * v
    t = jnp.tanh(k * v * (1.0 + 0.044715 * square))
    half = 0.5 * (1.0 + t)
    return v * half, half + 0.5 * v * (1.0 - t * t) * (k * (1.0 + 3.0 * 0.044715 * square))


def gelu(v):
    return 0.5 * v * (1.0 + jnp.tanh(math.sqrt(2.0 / math.pi) * v * (1.0 + 0.044715 * (v * v))))


def dot(a, b):
    return lax.dot_general(a, b, (((1,), (0,)), ((), ())), preferred_element_type=f32)


def dot_t(a, b):
    return lax.dot_general(a, b, (((1,), (1,)), ((), ())), preferred_element_type=f32)


def outer(a, b):
    return lax.dot_general(a, b, (((0,), (0,)), ((), ())), preferred_element_type=f32)


def moments(every, counts):
    sums, squares = every[:, 0, :], every[:, 1, :]
    total = jnp.sum(counts)
    mean = jnp.sum(sums, axis=0, keepdims=True) / total
    apart = sums / counts - mean
    square = jnp.sum(squares + counts * apart * apart, axis=0, keepdims=True)
    return mean, lax.rsqrt(square / total + EPS)


def emit(out_ref, first, second):
    both = jnp.concatenate([first, second], axis=0)
    out_ref[...] = jnp.broadcast_to(both[None], out_ref.shape)


def emit_moments(out_ref, values, count, mask=None):
    local_sum = jnp.sum(values, axis=0, keepdims=True)
    centered = values - local_sum / count
    if mask is not None:
        centered = centered * mask
    emit(out_ref, local_sum, jnp.sum(centered * centered, axis=0, keepdims=True))


def emit_sums(out_ref, q, normed):
    emit(out_ref, jnp.sum(q, axis=0, keepdims=True), jnp.sum(q * normed, axis=0, keepdims=True))


def back_terms(every_ref, total):
    sums = jnp.sum(every_ref[...], axis=0)
    return sums, sums[0:1] / total, sums[1:2] / total


def run(body, outs, ins, name):
    return pl.pallas_call(
        body,
        out_shape=outs,
        compiler_params=pltpu.CompilerParams(vmem_limit_bytes=40 * 1024 * 1024),
        name=name,
    )(*ins)


def shape(dims, kind=f32):
    return jax.ShapeDtypeStruct(tuple(dims), kind)


def row_block(rows, most):
    block = rows
    while block > most or rows % block or block % 16:
        block -= 1
    return block


def whole_spec(array):
    zeros = (0,) * array.ndim
    return pl.BlockSpec(array.shape, lambda i, v: zeros)


def run_table(body, table, block, variant, outs, ins, name):
    rows = table.shape[2]
    spec = pl.BlockSpec((1, 2, block, table.shape[3]), lambda i, v: (v[0], 0, i, 0))
    return pl.pallas_call(
        body,
        out_shape=outs,
        grid_spec=pltpu.PrefetchScalarGridSpec(
            num_scalar_prefetch=1,
            grid=(rows // block,),
            in_specs=[spec] + [whole_spec(item) for item in ins],
            out_specs=[whole_spec(item) for item in outs],
        ),
        compiler_params=pltpu.CompilerParams(vmem_limit_bytes=40 * 1024 * 1024),
        name=name,
    )(variant, table, *ins)


def reduce_first(x, reduce_kernel, width, narrow):
    cells, channels = x.shape
    half = reduce_kernel.shape[1]

    def body(x_ref, r_ref, reduced_ref, stats_ref):
        reduced = dot(x_ref[:, narrow:], r_ref[...])
        reduced_ref[...] = reduced
        emit_moments(stats_ref, reduced, float(cells))

    return run(body, [shape((cells, half)), shape((width, 2, half))], (x, reduce_kernel), "reduce_first")


def reduce_next(both, every, counts, gain, bias, s, reduce_kernel, narrow):
    cells, channels = both.shape
    half = reduce_kernel.shape[1]
    width = every.shape[0]

    def body(both_ref, every_ref, counts_ref, g_ref, b_ref, r_ref, low_ref, reduced_ref, stats_ref, mi_ref):
        mean, inv = moments(every_ref[...], counts_ref[...])
        mi_ref[...] = jnp.concatenate([mean, inv], axis=0)
        state = gelu((both_ref[...] - mean) * inv * g_ref[s : s + 1] + b_ref[s : s + 1])
        low = state.astype(bf16)
        low_ref[...] = low
        reduced = dot(low[:, narrow:], r_ref[...])
        reduced_ref[...] = reduced
        emit_moments(stats_ref, reduced, float(cells))

    outs = [shape((cells, channels), bf16), shape((cells, half)), shape((width, 2, half)), shape((2, channels))]
    return run(body, outs, (both, every, counts, gain, bias, reduce_kernel), "reduce_next")


def activate(values, every, counts, gain, bias, s, factor, keep, name):
    rows, channels = values.shape

    def body(v_ref, every_ref, counts_ref, g_ref, b_ref, factor_ref, *out_refs):
        mean, inv = moments(every_ref[...], counts_ref[...])
        out_refs[0][...] = jnp.concatenate([mean, inv], axis=0)
        act = gelu((v_ref[...] - mean) * inv * g_ref[s : s + 1] + b_ref[s : s + 1])
        if keep:
            out_refs[2][...] = act
        else:
            act = act * factor_ref[...]
        out_refs[1][...] = act.astype(bf16)

    outs = [shape((2, channels)), shape((rows, channels), bf16)]
    if keep:
        outs.append(shape((rows, channels)))
    return run(body, outs, (values, every, counts, gain, bias, factor), name)


def spectrum_forward(table, variant, own, others, freq_kernel, factor, scale, width):
    points = table.shape[2]
    half = own.shape[1]
    wide = freq_kernel.shape[1]
    block = row_block(points, 272)
    cells = own.shape[0]

    def body(v_ref, t_ref, own_ref, others_ref, w_ref, factor_ref, real_ref, imag_ref, mixed_ref, stats_ref):
        i = pl.program_id(0)
        t = t_ref[0].reshape(2 * block, t_ref.shape[3])
        z = (dot(t[:, :cells], own_ref[...]) + dot(t[:, cells:], others_ref[...])) * scale
        real, imag = z[:block].astype(bf16), z[block:].astype(bf16)
        rows = pl.ds(pl.multiple_of(i * block, block), block)
        real_ref[rows] = real
        imag_ref[rows] = imag
        mixed_ref[rows] = dot(real, w_ref[:half]) + dot(imag, w_ref[half:])

        @pl.when(i == pl.num_programs(0) - 1)
        def _():
            mask = jnp.where(factor_ref[...] > 0.0, 1.0, 0.0)
            emit_moments(stats_ref, mixed_ref[...], jnp.sum(mask), mask)

    outs = [shape((points, half), bf16), shape((points, half), bf16), shape((points, wide)), shape((width, 2, wide))]
    return run_table(body, table, block, variant, outs, (own, others, freq_kernel, factor), "spectrum_forward")


def inverse_forward(table, variant, own, others, hidden, pre, expand_t, scale, width):
    cells = table.shape[2]
    half = hidden.shape[1]
    channels = pre.shape[1]
    narrow = channels - expand_t.shape[0]
    block = row_block(cells, 256)

    def body(v_ref, t_ref, own_ref, others_ref, hidden_ref, pre_ref, e_ref, summed_ref, both_ref, stats_ref):
        i = pl.program_id(0)
        rows = pl.ds(pl.multiple_of(i * block, block), block)
        freq = jnp.concatenate([own_ref[...], others_ref[...]], axis=0)
        returned = (dot(t_ref[0, 0], freq[:, :half]) + dot(t_ref[0, 1], freq[:, half:])) * scale
        summed = (hidden_ref[rows] + returned).astype(bf16)
        summed_ref[rows] = summed
        both_ref[rows, :narrow] = pre_ref[rows, :narrow]
        both_ref[rows, narrow:] = pre_ref[rows, narrow:] + dot_t(summed, e_ref[...])

        @pl.when(i == pl.num_programs(0) - 1)
        def _():
            emit_moments(stats_ref, both_ref[...], float(cells))

    outs = [shape((cells, half), bf16), shape((cells, channels)), shape((width, 2, channels))]
    return run_table(body, table, block, variant, outs, (own, others, hidden, pre, expand_t), "inverse_forward")


def turn(both, every, counts, gain, bias, s, x, cot, width):
    cells, channels = both.shape

    def body(both_ref, every_ref, counts_ref, g_ref, b_ref, x_ref, cot_ref, out_ref, q_ref, sums_ref, mi_ref):
        mean, inv = moments(every_ref[...], counts_ref[...])
        mi_ref[...] = jnp.concatenate([mean, inv], axis=0)
        normed = (both_ref[...] - mean) * inv
        state, slope = gelu_parts(normed * g_ref[s : s + 1] + b_ref[s : s + 1])
        out_ref[...] = (x_ref[...].astype(f32) + state).astype(bf16)
        q = slope * cot_ref[...].astype(f32)
        q_ref[...] = q
        emit_sums(sums_ref, q, normed)

    outs = [shape((cells, channels), bf16), shape((cells, channels)), shape((width, 2, channels)), shape((2, channels))]
    return run(body, outs, (both, every, counts, gain, bias, x, cot), "turn")


def grad_pre(q, both, mi, every, gain, s, expand_t, total):
    cells, channels = both.shape
    broad, half = expand_t.shape
    narrow = channels - broad

    def body(q_ref, both_ref, mi_ref, every_ref, g_ref, e_ref, low_ref, summed_ref, summed_low_ref, sums_ref):
        sums, bias_term, gain_term = back_terms(every_ref, total)
        sums_ref[...] = sums
        inv = mi_ref[1:2]
        normed = (both_ref[...] - mi_ref[0:1]) * inv
        low = (g_ref[s : s + 1] * inv * (q_ref[...] - bias_term - normed * gain_term)).astype(bf16)
        low_ref[...] = low
        summed = dot(low[:, narrow:], e_ref[...])
        summed_ref[...] = summed
        summed_low_ref[...] = summed.astype(bf16)

    outs = [shape((cells, channels), bf16), shape((cells, half)), shape((cells, half), bf16), shape((2, channels))]
    return run(body, outs, (q, both, mi, every, gain, expand_t), "grad_pre")


def spectrum_backward(table, variant, own, others, mixed, mi, gain, bias, s, factor, scale, width):
    points, wide = mixed.shape
    block = row_block(points, 272)
    cells = own.shape[0]

    def body(v_ref, t_ref, own_ref, others_ref, mixed_ref, mi_ref, g_ref, b_ref, factor_ref, q_ref, sums_ref, n_ref):
        i = pl.program_id(0)
        t = t_ref[0].reshape(2 * block, t_ref.shape[3])
        z = dot(t[:, :cells], own_ref[...]) + dot(t[:, cells:], others_ref[...])
        rows = pl.ds(pl.multiple_of(i * block, block), block)
        grad = jnp.concatenate([z[:block], z[block:]], axis=1) * (factor_ref[rows] * scale)
        normed = (mixed_ref[rows] - mi_ref[0:1]) * mi_ref[1:2]
        _, slope = gelu_parts(normed * g_ref[s : s + 1] + b_ref[s : s + 1])
        q_ref[rows] = slope * grad
        n_ref[rows] = normed

        @pl.when(i == pl.num_programs(0) - 1)
        def _():
            emit_sums(sums_ref, q_ref[...], n_ref[...])

    outs = [shape((points, wide)), shape((width, 2, wide)), shape((points, wide))]
    ins = (own, others, mixed, mi, gain, bias, factor)
    return run_table(body, table, block, variant, outs, ins, "spectrum_backward")


def grad_mixed(q, normed, mi, every, gain, s, freq_kernel, counts):
    points, wide = q.shape

    def body(q_ref, n_ref, mi_ref, every_ref, g_ref, w_ref, counts_ref, low_ref, back_ref, sums_ref):
        sums, bias_term, gain_term = back_terms(every_ref, jnp.sum(counts_ref[...]))
        sums_ref[...] = sums
        low = (g_ref[s : s + 1] * mi_ref[1:2] * (q_ref[...] - bias_term - n_ref[...] * gain_term)).astype(bf16)
        low_ref[...] = low
        back_ref[...] = dot_t(low, w_ref[...]).astype(bf16)

    outs = [shape((points, wide), bf16), shape((points, wide), bf16), shape((2, wide))]
    return run(body, outs, (q, normed, mi, every, gain, freq_kernel, counts), "grad_mixed")


def inverse_backward(table, variant, own, others, summed, reduced, mi, gain, bias, s, scale, width):
    cells = table.shape[2]
    half = summed.shape[1]
    block = row_block(cells, 256)

    def body(v_ref, t_ref, own_ref, others_ref, summed_ref, reduced_ref, mi_ref, g_ref, b_ref, q_ref, sums_ref, n_ref):
        i = pl.program_id(0)
        rows = pl.ds(pl.multiple_of(i * block, block), block)
        freq = jnp.concatenate([own_ref[...], others_ref[...]], axis=0)
        back = (dot(t_ref[0, 0], freq[:, :half]) + dot(t_ref[0, 1], freq[:, half:])) * scale
        normed = (reduced_ref[rows] - mi_ref[0:1]) * mi_ref[1:2]
        _, slope = gelu_parts(normed * g_ref[s : s + 1] + b_ref[s : s + 1])
        q_ref[rows] = slope * (summed_ref[rows] + back)
        n_ref[rows] = normed

        @pl.when(i == pl.num_programs(0) - 1)
        def _():
            emit_sums(sums_ref, q_ref[...], n_ref[...])

    outs = [shape((cells, half)), shape((width, 2, half)), shape((cells, half))]
    ins = (own, others, summed, reduced, mi, gain, bias)
    return run_table(body, table, block, variant, outs, ins, "inverse_backward")


def grad_reduced(q, normed, mi, every, gain, s, reduce_kernel, total, conv_back, both, mi_3, gain_3, bias_3, width):
    cells, half = q.shape
    channels = both.shape[1]
    narrow = channels - reduce_kernel.shape[0]

    def body(q_ref, n_ref, mi_ref, every_ref, g_ref, r_ref, conv_ref, both_ref, mi3_ref, g3_ref, b3_ref, low_ref, out_ref, sums3_ref, sums_ref):
        sums, bias_term, gain_term = back_terms(every_ref, total)
        sums_ref[...] = sums
        low = (g_ref[s : s + 1] * mi_ref[1:2] * (q_ref[...] - bias_term - n_ref[...] * gain_term)).astype(bf16)
        low_ref[...] = low
        grad = conv_ref[...]
        grad = jnp.concatenate([grad[:, :narrow], grad[:, narrow:] + dot_t(low, r_ref[...])], axis=1)
        normed_3 = (both_ref[...] - mi3_ref[0:1]) * mi3_ref[1:2]
        _, slope = gelu_parts(normed_3 * g3_ref[s - 1 : s] + b3_ref[s - 1 : s])
        grad = grad * slope
        out_ref[...] = grad
        emit_sums(sums3_ref, grad, normed_3)

    outs = [shape((cells, half), bf16), shape((cells, channels)), shape((width, 2, channels)), shape((2, half))]
    ins = (q, normed, mi, every, gain, reduce_kernel, conv_back, both, mi_3, gain_3, bias_3)
    return run(body, outs, ins, "grad_reduced")


def grad_input(q, normed, mi, every, gain, s, reduce_kernel, total, conv_back, cot):
    cells, half = q.shape
    channels = cot.shape[1]
    narrow = channels - reduce_kernel.shape[0]

    def body(q_ref, n_ref, mi_ref, every_ref, g_ref, r_ref, conv_ref, cot_ref, low_ref, out_ref, sums_ref):
        sums, bias_term, gain_term = back_terms(every_ref, total)
        sums_ref[...] = sums
        low = (g_ref[s : s + 1] * mi_ref[1:2] * (q_ref[...] - bias_term - n_ref[...] * gain_term)).astype(bf16)
        low_ref[...] = low
        grad = conv_ref[...] + cot_ref[...].astype(f32)
        out_ref[:, :narrow] = grad[:, :narrow].astype(bf16)
        out_ref[:, narrow:] = (grad[:, narrow:] + dot_t(low, r_ref[...])).astype(bf16)

    outs = [shape((cells, half), bf16), shape((cells, channels), bf16), shape((2, half))]
    return run(body, outs, (q, normed, mi, every, gain, reduce_kernel, conv_back, cot), "grad_input")


def padded_columns(tile_ref, top_ref, bottom_ref, left_ref, right_ref, out_ref, cols, lanes):
    wide = jnp.concatenate([top_ref[:, lanes], tile_ref[:, lanes], bottom_ref[:, lanes]], axis=0)
    rows = wide.shape[0] // cols
    out_ref[1] = wide
    wide = wide.astype(f32)
    column = lax.broadcasted_iota(jnp.int32, (rows, cols, 1), 1)
    for j, edge_ref, at in ((0, left_ref, 0), (2, right_ref, cols - 1)):
        moved = pltpu.roll(wide, 1 if j == 0 else wide.shape[0] - 1, 0).reshape(rows, cols, wide.shape[1])
        edge = edge_ref[:, lanes].astype(f32)[:, None, :]
        moved = jnp.where(column == at, edge, moved)
        out_ref[j] = moved.reshape(rows * cols, wide.shape[1]).astype(bf16)


def conv_forward(low, sides, cols, local_kernel, global_t):
    cells, channels = low.shape
    narrow = local_kernel.shape[2]
    padded = cells + 2 * cols

    def body(x_ref, top_ref, bottom_ref, left_ref, right_ref, l_ref, g_ref, pre_ref, cols_ref, wide_ref):
        padded_columns(x_ref, top_ref, bottom_ref, left_ref, right_ref, wide_ref, cols, slice(None))
        cols_ref[...] = wide_ref[:, :, :narrow]
        local = jnp.zeros((cells, narrow), f32)
        for t in range(9):
            i, j = t // 3, t % 3
            local = local + dot(wide_ref[j, i * cols : i * cols + cells], l_ref[t])
        pre_ref[:, :narrow] = local
        patches = jnp.concatenate([wide_ref[t % 3, t // 3 * cols : t // 3 * cols + cells, :narrow] for t in range(9)], axis=1)
        pre_ref[:, narrow:] = dot_t(patches, g_ref[...])

    return pl.pallas_call(
        body,
        out_shape=[shape((cells, channels)), shape((3, padded, narrow), bf16)],
        scratch_shapes=[pltpu.VMEM((3, padded, channels), bf16)],
        compiler_params=pltpu.CompilerParams(vmem_limit_bytes=40 * 1024 * 1024),
        name="conv_forward",
    )(low, *sides, local_kernel, global_t)


def conv_backward(low, sides, cols, local_kernel, global_t):
    cells, channels = low.shape
    narrow = local_kernel.shape[2]
    broad = channels - narrow
    padded = cells + 2 * cols

    def body(x_ref, top_ref, bottom_ref, left_ref, right_ref, l_ref, g_ref, grad_ref, patches_ref, wide_ref):
        padded_columns(x_ref, top_ref, bottom_ref, left_ref, right_ref, wide_ref, cols, slice(None))
        grad = jnp.zeros((cells, channels), f32)
        into = jnp.zeros((cells, narrow), f32)
        for t in range(9):
            i, j = 2 - t // 3, 2 - t % 3
            rows = slice(i * cols, i * cols + cells)
            patches_ref[:, t * narrow : (t + 1) * narrow] = wide_ref[j, rows, :narrow]
            grad = grad + dot_t(wide_ref[j, rows, :narrow], l_ref[t])
            into = into + dot(wide_ref[j, rows, narrow:], g_ref[:, t * narrow : (t + 1) * narrow])
        grad_ref[:, :narrow] = grad[:, :narrow] + into
        grad_ref[:, narrow:] = grad[:, narrow:]

    return pl.pallas_call(
        body,
        out_shape=[shape((cells, channels)), shape((cells, 9 * narrow), bf16)],
        scratch_shapes=[pltpu.VMEM((3, padded, channels), bf16)],
        compiler_params=pltpu.CompilerParams(vmem_limit_bytes=40 * 1024 * 1024),
        name="conv_backward",
    )(low, *sides, local_kernel, global_t)


def gathered(shard):
    line = ("k", "z", "e")
    block = spread(shard, line)
    block = spread(block, "g")
    other = lax.ppermute(block, "c", [(0, 1), (1, 0)])
    first = jnp.where(lax.axis_index("c") == 0, block, other)
    second = jnp.where(lax.axis_index("c") == 0, other, block)
    both = jnp.stack([first, second], axis=1)
    return both.reshape((-1,) + shard.shape)


def per_device(plan, *args):
    (
        land,
        port,
        to_local,
        to_global,
        reduce_weight,
        freq_weight,
        expand_weight,
        spec_gain,
        spec_bias,
        freq_gain,
        freq_bias,
        out_gain,
        out_bias,
        cot_land,
        cot_port,
    ) = args
    rounds, forward_table, inverse_table, weight_table, point_counts = plan
    sections = to_local.shape[0]
    devices = lax.axis_size(ALL)
    own_in = to_local.shape[2]
    own_out = to_global.shape[3]
    narrow = to_local.shape[3]
    channels = own_in * devices
    broad = channels - narrow
    half = reduce_weight.shape[2]
    k, part = lax.axis_index("k"), lax.axis_index(PART)
    variant = k * lax.axis_size(PART) + part
    g_n, z_n, e_n = lax.axis_size("g"), lax.axis_size("z"), lax.axis_size("e")
    width = lax.axis_size(KIND)

    packed = jnp.concatenate([freq_weight, reduce_weight, jnp.transpose(expand_weight, (0, 2, 1))], axis=2)
    small = gathered(packed)
    x = to_tile(land, port, rounds)
    rows, cols = x.shape[:2]
    cells = rows * cols
    x = x.reshape(cells, channels)
    size = cells * lax.axis_size(PART)
    scale = 1.0 / math.sqrt(size)
    maps = g_n * z_n
    taps_local = jnp.reshape(to_local, (sections, 9 * own_in, narrow))
    taps_global = jnp.transpose(to_global, (0, 3, 1, 2)).reshape(sections, own_out * 9, narrow)
    kernels = gathered(jnp.concatenate([taps_local, taps_global], axis=1))
    weights = []
    for s in range(sections):
        full = small[:, s].reshape(broad, -1)
        wide = full.shape[1] - 2 * half
        local_kernel = kernels[:, s, : 9 * own_in].reshape(devices, 9, own_in, narrow)
        local_kernel = jnp.transpose(local_kernel, (1, 0, 2, 3)).reshape(9, channels, narrow)
        global_t = kernels[:, s, 9 * own_in :].reshape(broad, 9 * narrow)
        weights.append((full[:, wide : wide + half], full[:, :wide], full[:, wide + half :], local_kernel, global_t))
    cot = to_tile(cot_land, cot_port, rounds).reshape(cells, channels)

    factor = pick(weight_table, variant)[:, None]
    cell_counts = jnp.full((width, 1), cells, f32)
    by_part = pick(point_counts, k).astype(f32)
    freq_counts = jnp.broadcast_to(by_part.reshape(1, 2, 1, e_n), (g_n, 2, z_n, e_n)).reshape(width, 1)
    cell_total = float(maps * size)
    variant = variant.reshape(1)
    forward_table, inverse_table = jnp.asarray(forward_table), jnp.asarray(inverse_table)

    def exchange(stats):
        return lax.all_to_all(stats, KIND, 0, 0, tiled=True)

    kept = []
    both = every_3 = None
    for s in range(sections):
        reduce_kernel, freq_kernel, expand_t, local_kernel, global_t = weights[s]
        if s == 0:
            low = x
            reduced, stats = reduce_first(x, reduce_kernel, width, narrow)
        else:
            low, reduced, stats, mi_3 = reduce_next(both, every_3, cell_counts, out_gain, out_bias, s - 1, reduce_kernel, narrow)
            kept[-1]["mi_3"] = mi_3
        every_1 = exchange(stats)
        sides = edges(low.reshape(rows, cols, channels))
        pre, shifted = conv_forward(low, sides, cols, local_kernel, global_t)
        mi_1, hidden_low, hidden = activate(reduced, every_1, cell_counts, spec_gain, spec_bias, s, factor, True, "hidden")
        real, imag, mixed, stats = spectrum_forward(
            forward_table, variant, hidden_low, shared(hidden_low), freq_kernel, factor, scale, width
        )
        every_2 = exchange(stats)
        mi_2, freq_act = activate(mixed, every_2, freq_counts, freq_gain, freq_bias, s, factor, False, "freq_act")
        summed, both, stats = inverse_forward(
            inverse_table, variant, freq_act, shared(freq_act), hidden, pre, expand_t, scale, width
        )
        every_3 = exchange(stats)
        kept.append(
            dict(low=low, shifted=shifted, reduced=reduced, mi_1=mi_1, real=real, imag=imag, mixed=mixed, mi_2=mi_2, summed=summed, both=both)
        )
    out, q_3, sums, mi_3 = turn(both, every_3, cell_counts, out_gain, out_bias, sections - 1, x, cot, width)
    kept[-1]["mi_3"] = mi_3
    land_out, port_out = from_tile(out.reshape(rows, cols, channels), rounds)

    weight_shares = [None] * sections
    norm_sums = [None] * sections
    for s in reversed(range(sections)):
        reduce_kernel, freq_kernel, expand_t, local_kernel, global_t = weights[s]
        item = kept[s]
        every = exchange(sums)
        low, summed, summed_low, sums_3 = grad_pre(q_3, item["both"], item["mi_3"], every, out_gain, s, expand_t, cell_total)
        q, sums, normed = spectrum_backward(
            forward_table, variant, summed_low, shared(summed_low), item["mixed"], item["mi_2"], freq_gain, freq_bias, s, factor, scale, width
        )
        every = exchange(sums)
        sides = edges(low.reshape(rows, cols, channels))
        conv_back, patches = conv_backward(low, sides, cols, local_kernel, global_t)
        mixed_low, back, sums_2 = grad_mixed(q, normed, item["mi_2"], every, freq_gain, s, freq_kernel, freq_counts)
        q, sums, normed = inverse_backward(
            inverse_table, variant, back, shared(back), summed, item["reduced"], item["mi_1"], spec_gain, spec_bias, s, scale, width
        )
        every = exchange(sums)
        if s > 0:
            below = kept[s - 1]
            reduced_low, q_3, sums, sums_1 = grad_reduced(
                q, normed, item["mi_1"], every, spec_gain, s, reduce_kernel, cell_total,
                conv_back, below["both"], below["mi_3"], out_gain, out_bias, width,
            )
        else:
            reduced_low, grad, sums_1 = grad_input(
                q, normed, item["mi_1"], every, spec_gain, s, reduce_kernel, cell_total, conv_back, cot
            )
            land_grad, port_grad = from_tile(grad.reshape(rows, cols, channels), rounds)
        grad_global = low[:, narrow:]
        local_grad = outer(item["low"], patches)
        taps = jnp.concatenate(
            [item["shifted"][t % 3, t // 3 * cols : t // 3 * cols + cells] for t in range(9)], axis=1
        )
        global_grad = outer(grad_global, taps)
        expand_grad = outer(grad_global, item["summed"])
        freq_grad = jnp.concatenate([outer(item["real"], mixed_low), outer(item["imag"], mixed_low)], axis=0)
        reduce_grad = outer(item["low"][:, narrow:], reduced_low)
        local_grad = jnp.transpose(local_grad.reshape(devices, own_in, 9, narrow), (0, 2, 1, 3))
        local_grad = local_grad.reshape(devices, 9 * own_in, narrow)
        global_grad = global_grad.reshape(devices, own_out * 9, narrow)
        others = jnp.concatenate([freq_grad, reduce_grad, expand_grad], axis=1)
        others = others.reshape(devices, own_out, others.shape[1])
        owned_kernels = owned(jnp.concatenate([local_grad, global_grad], axis=1))
        owned_others = owned(others)
        weight_shares[s] = (
            owned_kernels[: 9 * own_in].reshape(9, own_in, narrow),
            jnp.transpose(owned_kernels[9 * own_in :].reshape(own_out, 9, narrow), (1, 2, 0)),
            owned_others[:, 2 * half : 3 * half],
            owned_others[:, : 2 * half],
            jnp.transpose(owned_others[:, 3 * half :]),
        )
        norm_sums[s] = (sums_1, sums_2, sums_3)
    flat_sums = jnp.concatenate([item for s in range(sections) for item in norm_sums[s]], axis=1)
    flat_sums = flat_sums + lax.ppermute(flat_sums, "k", [(0, 1), (1, 0)])
    gains = [[] for _ in range(6)]
    offset = 0
    for s in range(sections):
        for index, wide in enumerate((half, 2 * half, channels)):
            gains[2 * index].append(flat_sums[1, offset : offset + wide])
            gains[2 * index + 1].append(flat_sums[0, offset : offset + wide])
            offset += wide
    stacked = [jnp.stack([weight_shares[s][i] for s in range(sections)]) for i in range(5)]
    return (land_out, port_out, land_grad, port_grad, *stacked, *[jnp.stack(item) for item in gains])


def owned(shares):
    shape = shares.shape[1:]
    g_n, c_n = lax.axis_size("g"), lax.axis_size("c")
    rest = lax.axis_size(("k", "z", "e"))
    low = shares.astype(bf16).reshape((g_n * c_n, rest) + shape)
    first = lax.all_to_all(low, ("g", "c"), 0, 0, tiled=True)
    first = jnp.sum(first.astype(f32), axis=0).astype(bf16)
    second = lax.all_to_all(first, ("k", "z", "e"), 0, 0, tiled=True)
    return jnp.sum(second.astype(f32), axis=0)


def solution(mesh):
    f_n, s_n = mesh.shape["fsdp"], mesh.shape["sp"]
    e_n = s_n // 4
    fine = Mesh(np.asarray(mesh.devices).reshape(f_n // 2, 2, 2, 2, e_n), ALL)
    maps = P(("g", "c"), ("k", "z", "e"), None, None)
    split = ALL

    def whole(*args):
        land, port = args[0], args[1]
        plan = (
            routes(e_n),
            *transform_tables(e_n, land.shape[1:3], port.shape[1:3]),
        )
        weights = (
            P(None, None, split, None),
            P(None, None, None, split),
            P(None, split, None),
            P(None, split, None),
            P(None, None, split),
        )
        return jax.shard_map(
            lambda *local: per_device(plan, *local),
            mesh=fine,
            in_specs=(maps, maps, *weights, P(), P(), P(), P(), P(), P(), maps, maps),
            out_specs=(maps, maps, maps, maps, *weights, P(), P(), P(), P(), P(), P()),
            check_vma=False,
        )(*args)

    return whole
```

```python
import math

import jax
import jax.numpy as jnp
import numpy as np
from jax import lax
from jax.experimental import pallas as pl
from jax.experimental.pallas import tpu as pltpu
from jax.sharding import Mesh, PartitionSpec as P

EPS = 1e-05
LINE = ("c", "k", "z", "e")
KIND = ("g", "c", "z", "e")
PART = ("c", "e")
ALL = ("g", "c", "k", "z", "e")
f32 = jnp.float32
bf16 = jnp.bfloat16


def routes(e_n):
    s_n = 4 * e_n
    count = 2 * s_n
    left = []
    for c in range(2):
        for s in range(s_n):
            for unit in range(4):
                kind, half = unit // 2, unit % 2
                left.append((c * s_n + s, unit, half * s_n + (kind * 2 + c) * e_n + s // 4, s % 4))
    rounds = []
    for _ in range(4):
        owner = {}

        def augment(src, seen):
            for edge in left:
                if edge[0] == src and edge[2] not in seen:
                    seen.add(edge[2])
                    if edge[2] not in owner or augment(owner[edge[2]][0], seen):
                        owner[edge[2]] = edge
                        return True
            return False

        for src in range(count):
            assert augment(src, set())
        chosen = list(owner.values())
        for edge in chosen:
            left.remove(edge)
        sent = np.zeros(count, np.int32)
        slot = np.zeros(count, np.int32)
        for edge in chosen:
            sent[edge[0]] = edge[1]
            slot[edge[2]] = edge[3]
        rounds.append(([(edge[0], edge[2]) for edge in chosen], sent, slot))
    return rounds


def transform_tables(e_n, land_shape, port_shape):
    parts = 2 * e_n
    shapes = (land_shape, port_shape)
    most = max(rows * (cols // 2 + 1) for rows, cols in shapes)
    per_part = -(-most // (16 * parts)) * 16
    forward, inverse, weight, counts = [], [], [], []
    for rows, cols in shapes:
        half = cols // 2 + 1
        point = np.arange(per_part * parts)
        valid = point < rows * half
        kr, f = point // half, point % half
        tiles = []
        for part in range(parts):
            c, e = part // e_n, part % e_n
            h = np.arange(rows // e_n) + e * (rows // e_n)
            w = np.arange(cols // 2) + c * (cols // 2)
            tiles.append((np.repeat(h, len(w)), np.tile(w, len(h))))
        cell_h = np.concatenate([tile[0] for tile in tiles])
        cell_w = np.concatenate([tile[1] for tile in tiles])
        size = rows * cols
        phase = (kr[:, None] * cell_h[None, :] * cols + f[:, None] * cell_w[None, :] * rows) % size
        angle = phase * (2.0 * math.pi / size)
        table = np.stack([np.cos(angle), -np.sin(angle)]) * valid[None, :, None]
        table = table.astype(np.float32).astype(jnp.bfloat16)
        cells = size // parts
        factor = np.where((f == 0) | (2 * f == cols), 1.0, 2.0) * valid
        counts.append([int(valid[p * per_part : (p + 1) * per_part].sum()) for p in range(parts)])
        for part in range(parts):
            order = [(part + step) % parts for step in range(parts)]
            own_points = slice(part * per_part, (part + 1) * per_part)
            own_cells = slice(part * cells, (part + 1) * cells)
            forward.append(
                np.concatenate([table[:, own_points, q * cells : (q + 1) * cells] for q in order], axis=2)
            )
            back = np.concatenate([table[:, q * per_part : (q + 1) * per_part, own_cells] for q in order], axis=1)
            inverse.append(np.ascontiguousarray(back.transpose(0, 2, 1)))
            weight.append(factor[own_points].astype(np.float32))
    return np.stack(forward), np.stack(inverse), np.stack(weight), np.asarray(counts, np.int32)


SWAP = [(0, 1), (1, 0)]


def pick(table, index):
    return lax.dynamic_index_in_dim(jnp.asarray(table), index, 0, keepdims=False)


def partners(pieces, axes, step):
    count = lax.axis_size(axes)
    return lax.ppermute(pieces, axes, [(i, i ^ step) for i in range(count)])


def split_halves(land, port, place):
    channels = land.shape[3]
    shapes = [maps.shape[1:3] for maps in (land, port)]
    cells = shapes[0][0] * shapes[0][1] // 2

    def body(land_ref, port_ref, place_ref, mine_ref, theirs_ref):
        c = place_ref[1]
        for kind, ref in enumerate((land_ref, port_ref)):
            half = shapes[kind][1] // 2
            for out_ref, core in ((mine_ref, c), (theirs_ref, 1 - c)):
                at = pl.ds(pl.multiple_of(core * half, half), half)
                out_ref[kind] = ref[0, :, at, :].reshape(cells, channels)

    outs = [shape((2, cells, channels), land.dtype)] * 2
    return run(body, outs, (land, port, place), "split_halves", scalars=1)


def join_halves(mine, theirs, like, place):
    def body(mine_ref, theirs_ref, place_ref, *out_refs):
        c = place_ref[1]
        for kind, out_ref in enumerate(out_refs):
            _, rows, cols, channels = out_ref.shape
            half = cols // 2
            for ref, core in ((mine_ref, c), (theirs_ref, 1 - c)):
                at = pl.ds(pl.multiple_of(core * half, half), half)
                out_ref[0, :, at, :] = ref[kind].reshape(rows, half, channels)

    return run(body, [shape(maps.shape, maps.dtype) for maps in like], (mine, theirs, place), "join_halves", scalars=1)


def to_slots(mine, theirs, place, lanes):
    channels = lanes.stop - lanes.start

    def body(mine_ref, theirs_ref, place_ref, *out_refs):
        here, c = place_ref[2], place_ref[1]
        for step, out_ref in enumerate(out_refs):
            there = here ^ step
            kind, core = there // 2, there % 2

            @pl.when(core == c)
            def _():
                out_ref[...] = mine_ref[kind, :, lanes]

            @pl.when(core != c)
            def _():
                out_ref[...] = theirs_ref[kind, :, lanes]

    outs = [shape((mine.shape[1], channels), mine.dtype)] * 4
    return run(body, outs, (mine, theirs, place), "to_slots", scalars=1)


def from_slots(pieces, place):
    def body(*refs):
        place_ref, mine_ref, theirs_ref = refs[-3:]
        here, c = place_ref[2], place_ref[1]
        for step in range(4):
            there = here ^ step
            kind, core = there // 2, there % 2

            @pl.when(core == c)
            def _():
                mine_ref[kind] = refs[step][...]

            @pl.when(core != c)
            def _():
                theirs_ref[kind] = refs[step][...]

    outs = [shape((2,) + pieces[0].shape, pieces[0].dtype)] * 2
    return run(body, outs, (*pieces, place), "from_slots", scalars=1)


def in_order(pieces, here):
    rows = pieces[0].shape[0]

    def body(*refs):
        here_ref, out_ref = refs[-2:]
        for step in range(len(pieces)):
            out_ref[here_ref[0] ^ step] = refs[step][...]

    outs = [shape((len(pieces),) + pieces[0].shape, pieces[0].dtype)]
    out = run(body, outs, (*pieces, here), "in_order", scalars=1)[0]
    return out.reshape((len(pieces) * rows,) + pieces[0].shape[1:])


def join_lanes(pieces, rest, here):
    rows, first = pieces[0].shape
    channels = first + rest.shape[1]
    count = len(pieces)

    def body(*refs):
        rest_ref, here_ref, out_ref = refs[count:]
        out_ref[:, first:] = rest_ref[...]
        for step in range(count):
            at = pl.ds(pl.multiple_of((here_ref[0] ^ step) * rows, 16), rows)
            out_ref[at, :first] = refs[step][...]

    return run(body, [shape((count * rows, channels), rest.dtype)], (*pieces, rest, here), "join_lanes", scalars=1)[0]


def for_partners(blocks, here, lanes):
    count, rows = blocks.shape[:2]

    def body(blocks_ref, here_ref, *out_refs):
        for step in range(count):
            out_refs[step][...] = blocks_ref[here_ref[0] ^ step, :, lanes]

    outs = [shape((rows, lanes.stop - lanes.start), blocks.dtype)] * count
    return run(body, outs, (blocks, here), "for_partners", scalars=1)


def advance(steps):
    return next(steps)


def finish(steps):
    while True:
        try:
            next(steps)
        except StopIteration as stop:
            return stop.value


def over_line(pieces):
    axes = ("k", "z", "e")
    return [pieces[0]] + [partners(pieces[step], axes, step) for step in range(1, lax.axis_size(axes))]


def over_plane(pieces):
    return [pieces[0]] + [partners(pieces[step], "g", step) for step in range(1, lax.axis_size("g"))]


def to_tile(land, port, rounds, place, here, narrow=0):
    channels = land.shape[3]
    if lax.axis_size("e") == 1:
        mine, theirs = split_halves(land, port, place)
        theirs = lax.ppermute(theirs, "c", SWAP)
        yield
        pieces = over_line(to_slots(mine, theirs, place, slice(narrow, channels)))
        if narrow:
            first = over_line(to_slots(mine, theirs, place, slice(0, narrow)))
        yield
        broad = in_order(pieces, here[0])
        if not narrow:
            return broad
        yield broad
        return join_lanes(first, broad, here[0])
    me = lax.axis_index(LINE)
    units = []
    for maps in (land, port):
        cols = maps.shape[2] // 2
        units += [maps[0, :, :cols].reshape(-1, channels), maps[0, :, cols:].reshape(-1, channels)]
    units = jnp.stack(units)
    got = [lax.ppermute(pick(units, pick(sent, me)), LINE, pairs) for pairs, sent, _ in rounds]
    yield
    slots = np.stack([slot for _, _, slot in rounds], axis=1)
    order = pick(np.argsort(slots, axis=1).astype(np.int32), me)
    yield
    tile = jnp.concatenate([pick(jnp.stack(got), order[i]) for i in range(4)], axis=0)
    if narrow:
        yield tile[:, narrow:]
    return tile


def from_tile(tile, rounds, place, here, lanes=None):
    lanes = lanes or slice(0, tile.shape[1])
    units = tile.reshape(4, -1, tile.shape[1])
    if lax.axis_size("e") == 1:
        pieces = over_line(for_partners(units, here[0], lanes))
        yield
        mine, theirs = from_slots(pieces, place)
        return mine, lax.ppermute(theirs, "c", SWAP)
    units = units[:, :, lanes]
    me = lax.axis_index(LINE)
    got = [lax.ppermute(pick(units, pick(slot, me)), LINE, [(b, a) for a, b in pairs]) for pairs, _, slot in rounds]
    yield
    sents = np.stack([sent for _, sent, _ in rounds], axis=1)
    order = pick(np.argsort(sents, axis=1).astype(np.int32), me)
    both = jnp.stack([pick(jnp.stack(got), order[i]) for i in range(4)]).reshape((2, 2) + units.shape[1:])
    c = lax.axis_index("c")
    return (
        lax.dynamic_index_in_dim(both, c, 1, keepdims=False),
        lax.dynamic_index_in_dim(both, 1 - c, 1, keepdims=False),
    )


def shared(block):
    parts = lax.axis_size(PART)
    pieces = [
        lax.ppermute(block, PART, [((p + step) % parts, p) for p in range(parts)]) for step in range(1, parts)
    ]
    return pieces[0] if parts == 2 else jnp.concatenate(pieces, axis=0)


def gelu_parts(v):
    k = math.sqrt(2.0 / math.pi)
    square = v * v
    t = jnp.tanh(k * v * (1.0 + 0.044715 * square))
    half = 0.5 * (1.0 + t)
    return v * half, half + 0.5 * v * (1.0 - t * t) * (k * (1.0 + 3.0 * 0.044715 * square))


def gelu(v):
    return 0.5 * v * (1.0 + jnp.tanh(math.sqrt(2.0 / math.pi) * v * (1.0 + 0.044715 * (v * v))))


def dot(a, b):
    return lax.dot_general(a, b, (((1,), (0,)), ((), ())), preferred_element_type=f32)


def dot_t(a, b):
    return lax.dot_general(a, b, (((1,), (1,)), ((), ())), preferred_element_type=f32)


def outer(a, b):
    return lax.dot_general(a, b, (((0,), (0,)), ((), ())), preferred_element_type=f32)


def device_counts(counts, kind, width, e_n, z_n):
    row = lax.broadcasted_iota(jnp.int32, (width, 1), 0)
    part = row // (e_n * z_n) % 2 * e_n + row % e_n
    out = jnp.zeros((width, 1), f32)
    for p in range(len(counts[0])):
        out = jnp.where(part == p, jnp.where(kind == 0, float(counts[0][p]), float(counts[1][p])), out)
    return out


def moments(every, counts, total):
    sums, squares = every[:, 0, :], every[:, 1, :]
    mean = jnp.sum(sums, axis=0, keepdims=True) / total
    apart = sums / counts - mean
    square = jnp.sum(squares + counts * apart * apart, axis=0, keepdims=True)
    return mean, lax.rsqrt(square / total + EPS)


def emit(out_ref, first, second):
    both = jnp.concatenate([first, second], axis=0)
    out_ref[...] = jnp.broadcast_to(both[None], out_ref.shape)


def row_step(rows):
    return next(step for step in (64, 32, 16, 8) if rows % step == 0)


def sweep(rows, body, carry=0, step=None):
    step = step or row_step(rows)
    if rows == step:
        return body(slice(0, rows), carry)
    return lax.fori_loop(0, rows // step, lambda i, carry: body(pl.ds(pl.multiple_of(i * step, step), step), carry), carry)


def folded(values):
    return jnp.sum(values.reshape(values.shape[0] // 8, 8, values.shape[1]), axis=0)


def column(values):
    return jnp.sum(values, axis=0, keepdims=True)


def emit_moments(out_ref, ref, count, factor_ref=None):
    rows, columns = ref.shape
    zero = jnp.zeros((8, columns), f32)
    local_sum = column(sweep(rows, lambda at, acc: acc + folded(ref[at, :]), zero))
    mean = local_sum / count

    def squares(at, acc):
        centered = ref[at, :] - mean
        if factor_ref is not None:
            centered = jnp.where(factor_ref[at, :] > 0.0, centered, 0.0)
        return acc + folded(centered * centered)

    emit(out_ref, local_sum, column(sweep(rows, squares, zero)))


def pair(columns):
    return jnp.zeros((8, columns), f32), jnp.zeros((8, columns), f32)


def add_sums(sums, q, normed):
    return sums[0] + folded(q), sums[1] + folded(q * normed)


def emit_sums(out_ref, sums):
    emit(out_ref, column(sums[0]), column(sums[1]))


def back_terms(every_ref, total):
    sums = jnp.sum(every_ref[...], axis=0)
    return sums, sums[0:1] / total, sums[1:2] / total


VMEM = pl.BlockSpec(memory_space=pltpu.VMEM)
SMEM = pl.BlockSpec(memory_space=pltpu.SMEM)
ANY = pl.BlockSpec(memory_space=pl.ANY)
HBM = pl.BlockSpec(memory_space=pltpu.HBM)


class Order:
    last = ()


def run(body, outs, ins, name, scratch=(), limit=8, scalars=0):
    vectors = len(ins) - scalars
    waits = len(Order.last)

    def ordered(*refs):
        body(*refs[:vectors], *refs[vectors + waits :])

    result = pl.pallas_call(
        ordered,
        out_shape=outs,
        in_specs=[HBM if item is None else VMEM for item in _spaces(ins[:vectors])] + [ANY] * waits + [SMEM] * scalars,
        out_specs=[VMEM] * len(outs),
        scratch_shapes=list(scratch),
        cost_estimate=pl.CostEstimate(flops=1, bytes_accessed=1, transcendentals=0),
        compiler_params=pltpu.CompilerParams(vmem_limit_bytes=limit * 1024 * 1024),
        name=name,
    )(*[item.array if isinstance(item, InPlace) else item for item in ins[:vectors]], *Order.last, *ins[vectors:])
    Order.last = (result[0],)
    return result


class InPlace:
    def __init__(self, array):
        self.array = array


def _spaces(items):
    return [None if isinstance(item, InPlace) else item for item in items]


def shape(dims, kind=f32):
    return jax.ShapeDtypeStruct(tuple(dims), kind)


def reduce_first(x, reduce_kernel, width):
    cells = x.shape[0]
    half = reduce_kernel.shape[1]

    def body(x_ref, r_ref, reduced_ref, stats_ref):
        reduced_ref[...] = dot(x_ref[...], r_ref[...])
        emit_moments(stats_ref, reduced_ref, float(cells))

    return run(body, [shape((cells, half)), shape((width, 2, half))], (x, reduce_kernel), "reduce_first")


def reduce_next(both, every, gain, bias, s, reduce_kernel, narrow):
    cells, channels = both.shape
    half = reduce_kernel.shape[1]
    width = every.shape[0]

    def body(both_ref, every_ref, g_ref, b_ref, r_ref, low_ref, reduced_ref, stats_ref, mi_ref):
        mean, inv = moments(every_ref[...], float(cells), float(cells * width))
        mi_ref[...] = jnp.concatenate([mean, inv], axis=0)
        gain_row, bias_row = g_ref[s : s + 1], b_ref[s : s + 1]

        def apply(at, carry):
            low_ref[at, :] = gelu((both_ref[at, :] - mean) * inv * gain_row + bias_row).astype(bf16)
            return carry

        sweep(cells, apply, step=32)
        reduced_ref[...] = dot(low_ref[:, narrow:], r_ref[...])
        emit_moments(stats_ref, reduced_ref, float(cells))

    outs = [shape((cells, channels), bf16), shape((cells, half)), shape((width, 2, half)), shape((2, channels))]
    return run(body, outs, (both, every, gain, bias, reduce_kernel), "reduce_next")


def hidden_act(reduced, every, gain, bias, s):
    cells, channels = reduced.shape
    width = every.shape[0]

    def body(v_ref, every_ref, g_ref, b_ref, low_ref, hidden_ref, mi_ref):
        mean, inv = moments(every_ref[...], float(cells), float(cells * width))
        mi_ref[...] = jnp.concatenate([mean, inv], axis=0)
        gain_row, bias_row = g_ref[s : s + 1], b_ref[s : s + 1]

        def apply(at, carry):
            act = gelu((v_ref[at, :] - mean) * inv * gain_row + bias_row)
            hidden_ref[at, :] = act
            low_ref[at, :] = act.astype(bf16)
            return carry

        sweep(cells, apply)

    outs = [shape((cells, channels), bf16), shape((cells, channels)), shape((2, channels))]
    return run(body, outs, (reduced, every, gain, bias), "hidden_act")


def freq_act(mixed, every, gain, bias, s, factor, place, counts, e_n, z_n):
    points, channels = mixed.shape
    width = every.shape[0]

    def body(v_ref, every_ref, g_ref, b_ref, factor_ref, place_ref, low_ref, mi_ref):
        by_device = device_counts(counts, place_ref[0], width, e_n, z_n)
        mean, inv = moments(every_ref[...], by_device, jnp.sum(by_device))
        mi_ref[...] = jnp.concatenate([mean, inv], axis=0)
        gain_row, bias_row = g_ref[s : s + 1], b_ref[s : s + 1]

        def apply(at, carry):
            act = gelu((v_ref[at, :] - mean) * inv * gain_row + bias_row)
            low_ref[at, :] = (act * factor_ref[at, :]).astype(bf16)
            return carry

        sweep(points, apply)

    outs = [shape((points, channels), bf16), shape((2, channels))]
    return run(body, outs, (mixed, every, gain, bias, factor, place), "freq_act", scalars=1)


def blocks_of(rows, most):
    count = -(-rows // most)
    while rows % (16 * count):
        count += 1
    return [slice(i * rows // count, (i + 1) * rows // count) for i in range(count)]


def spectrum_forward(table, own, others, freq_kernel, factor, scale, width):
    points = table.shape[1]
    cells, half = own.shape
    wide = freq_kernel.shape[1]

    def body(t_ref, own_ref, others_ref, w_ref, factor_ref, real_ref, imag_ref, mixed_ref, stats_ref):
        for side, out_ref in enumerate((real_ref, imag_ref)):
            for at in blocks_of(points, 272):
                z = dot(t_ref[side, at, :cells], own_ref[...]) + dot(t_ref[side, at, cells:], others_ref[...])
                out_ref[at, :] = (z * scale).astype(bf16)
        mixed_ref[...] = dot(real_ref[...], w_ref[:half]) + dot(imag_ref[...], w_ref[half:])
        count = jnp.sum(jnp.where(factor_ref[...] > 0.0, 1.0, 0.0))
        emit_moments(stats_ref, mixed_ref, count, factor_ref)

    outs = [shape((points, half), bf16), shape((points, half), bf16), shape((points, wide)), shape((width, 2, wide))]
    return run(body, outs, (table, own, others, freq_kernel, factor), "spectrum_forward")


def inverse_forward(table, own, others, hidden, pre, expand_t, scale, width):
    cells = table.shape[1]
    half = hidden.shape[1]
    channels = pre.shape[1]
    narrow = channels - expand_t.shape[0]

    def body(t_ref, own_ref, others_ref, hidden_ref, pre_ref, e_ref, summed_ref, both_ref, stats_ref):
        freq = jnp.concatenate([own_ref[...], others_ref[...]], axis=0)
        real, imag = freq[:, :half], freq[:, half:]
        for at in blocks_of(cells, 256):
            returned = dot(t_ref[0, at, :], real) + dot(t_ref[1, at, :], imag)
            summed_ref[at, :] = (hidden_ref[at, :] + returned * scale).astype(bf16)
        both_ref[:, :narrow] = pre_ref[:, :narrow]
        for at in blocks_of(cells, 256):
            both_ref[at, narrow:] = pre_ref[at, narrow:] + dot_t(summed_ref[at, :], e_ref[...])
        emit_moments(stats_ref, both_ref, float(cells))

    outs = [shape((cells, half), bf16), shape((cells, channels)), shape((width, 2, channels))]
    return run(body, outs, (table, own, others, hidden, pre, expand_t), "inverse_forward")


def turn(both, every, gain, bias, s, x, cot):
    cells, channels = both.shape

    width = every.shape[0]

    def body(both_ref, every_ref, g_ref, b_ref, x_ref, cot_ref, out_ref, q_ref, sums_ref, mi_ref):
        mean, inv = moments(every_ref[...], float(cells), float(cells * width))
        mi_ref[...] = jnp.concatenate([mean, inv], axis=0)
        gain_row, bias_row = g_ref[s : s + 1], b_ref[s : s + 1]

        def apply(at, sums):
            normed = (both_ref[at, :] - mean) * inv
            state, slope = gelu_parts(normed * gain_row + bias_row)
            out_ref[at, :] = (x_ref[at, :].astype(f32) + state).astype(bf16)
            q = slope * cot_ref[at, :].astype(f32)
            q_ref[at, :] = q
            return add_sums(sums, q, normed)

        emit_sums(sums_ref, sweep(cells, apply, pair(channels), step=32))

    outs = [shape((cells, channels), bf16), shape((cells, channels)), shape((width, 2, channels)), shape((2, channels))]
    return run(body, outs, (both, every, gain, bias, x, cot), "turn")


def grad_pre(q, both, mi, every, gain, s, expand_t, total):
    cells, channels = both.shape
    broad, half = expand_t.shape
    narrow = channels - broad

    def body(q_ref, both_ref, mi_ref, every_ref, g_ref, e_ref, *refs):
        low_ref, summed_ref, summed_low_ref, sums_ref = refs
        sums, bias_term, gain_term = back_terms(every_ref, total)
        sums_ref[...] = sums
        mean, inv = mi_ref[0:1], mi_ref[1:2]
        gain_row = g_ref[s : s + 1] * inv

        def apply(at, carry):
            normed = (both_ref[at, :] - mean) * inv
            low_ref[at, :] = (gain_row * (q_ref[at, :] - bias_term - normed * gain_term)).astype(bf16)
            return carry

        sweep(cells, apply, step=32)
        summed_ref[...] = dot(low_ref[:, narrow:], e_ref[...])
        summed_low_ref[...] = summed_ref[...].astype(bf16)

    outs = [shape((cells, channels), bf16), shape((cells, half)), shape((cells, half), bf16), shape((2, channels))]
    return run(body, outs, (q, both, mi, every, gain, expand_t), "grad_pre")


def spectrum_backward(table, own, others, mixed, mi, gain, bias, s, factor, scale, width):
    points, wide = mixed.shape
    cells, half = own.shape

    def body(t_ref, own_ref, others_ref, mixed_ref, mi_ref, g_ref, b_ref, factor_ref, *refs):
        q_ref, sums_ref, n_ref = refs
        mean, inv = mi_ref[0:1], mi_ref[1:2]
        gain_row, bias_row = g_ref[s : s + 1], b_ref[s : s + 1]
        for side in range(2):
            for at in blocks_of(points, 272):
                z = dot(t_ref[side, at, :cells], own_ref[...]) + dot(t_ref[side, at, cells:], others_ref[...])
                q_ref[at, side * half : (side + 1) * half] = z * (factor_ref[at, :] * scale)

        def apply(at, sums):
            normed = (mixed_ref[at, :] - mean) * inv
            q = gelu_parts(normed * gain_row + bias_row)[1] * q_ref[at, :]
            q_ref[at, :] = q
            n_ref[at, :] = normed
            return add_sums(sums, q, normed)

        emit_sums(sums_ref, sweep(points, apply, pair(wide)))

    outs = [shape((points, wide)), shape((width, 2, wide)), shape((points, wide))]
    return run(body, outs, (table, own, others, mixed, mi, gain, bias, factor), "spectrum_backward")


def norm_low(low_ref, q_ref, n_ref, mi_ref, gain_row, bias_term, gain_term):
    gain_row = gain_row * mi_ref[1:2]

    def apply(at, carry):
        low_ref[at, :] = (gain_row * (q_ref[at, :] - bias_term - n_ref[at, :] * gain_term)).astype(bf16)
        return carry

    sweep(q_ref.shape[0], apply)


def grad_mixed(q, normed, mi, every, gain, s, freq_kernel, place, totals):
    points, wide = q.shape

    def body(q_ref, n_ref, mi_ref, every_ref, g_ref, w_ref, place_ref, low_ref, back_ref, sums_ref):
        total = jnp.where(place_ref[0] == 0, float(totals[0]), float(totals[1]))
        sums, bias_term, gain_term = back_terms(every_ref, total)
        sums_ref[...] = sums
        norm_low(low_ref, q_ref, n_ref, mi_ref, g_ref[s : s + 1], bias_term, gain_term)
        back_ref[...] = dot_t(low_ref[...], w_ref[...]).astype(bf16)

    outs = [shape((points, wide), bf16), shape((points, wide), bf16), shape((2, wide))]
    return run(body, outs, (q, normed, mi, every, gain, freq_kernel, place), "grad_mixed", scalars=1)


def inverse_backward(table, own, others, summed, reduced, mi, gain, bias, s, scale, width):
    cells = table.shape[1]
    half = summed.shape[1]

    def body(t_ref, own_ref, others_ref, summed_ref, reduced_ref, mi_ref, g_ref, b_ref, *refs):
        q_ref, sums_ref, n_ref = refs
        mean, inv = mi_ref[0:1], mi_ref[1:2]
        gain_row, bias_row = g_ref[s : s + 1], b_ref[s : s + 1]
        freq = jnp.concatenate([own_ref[...], others_ref[...]], axis=0)
        real, imag = freq[:, :half], freq[:, half:]
        for at in blocks_of(cells, 256):
            back = dot(t_ref[0, at, :], real) + dot(t_ref[1, at, :], imag)
            q_ref[at, :] = summed_ref[at, :] + back * scale

        def apply(at, sums):
            normed = (reduced_ref[at, :] - mean) * inv
            q = gelu_parts(normed * gain_row + bias_row)[1] * q_ref[at, :]
            q_ref[at, :] = q
            n_ref[at, :] = normed
            return add_sums(sums, q, normed)

        emit_sums(sums_ref, sweep(cells, apply, pair(half)))

    outs = [shape((cells, half)), shape((width, 2, half)), shape((cells, half))]
    return run(body, outs, (table, own, others, summed, reduced, mi, gain, bias), "inverse_backward")


def grad_reduced(q, normed, mi, every, gain, s, reduce_kernel, total, conv_back, both, mi_3, gain_3, bias_3, width):
    cells, half = q.shape
    channels = both.shape[1]
    narrow = channels - reduce_kernel.shape[0]

    def body(q_ref, n_ref, mi_ref, every_ref, g_ref, r_ref, conv_ref, both_ref, mi3_ref, g3_ref, b3_ref, *refs):
        low_ref, out_ref, sums3_ref, sums_ref = refs
        sums, bias_term, gain_term = back_terms(every_ref, total)
        sums_ref[...] = sums
        norm_low(low_ref, q_ref, n_ref, mi_ref, g_ref[s : s + 1], bias_term, gain_term)
        out_ref[:, :narrow] = conv_ref[:, :narrow]
        for at in blocks_of(cells, 256):
            out_ref[at, narrow:] = conv_ref[at, narrow:] + dot_t(low_ref[at, :], r_ref[...])
        mean, inv = mi3_ref[0:1], mi3_ref[1:2]
        gain_row, bias_row = g3_ref[s - 1 : s], b3_ref[s - 1 : s]

        def apply(at, sums):
            normed_3 = (both_ref[at, :] - mean) * inv
            grad = gelu_parts(normed_3 * gain_row + bias_row)[1] * out_ref[at, :]
            out_ref[at, :] = grad
            return add_sums(sums, grad, normed_3)

        emit_sums(sums3_ref, sweep(cells, apply, pair(channels), step=32))

    outs = [shape((cells, half), bf16), shape((cells, channels)), shape((width, 2, channels)), shape((2, half))]
    ins = (q, normed, mi, every, gain, reduce_kernel, conv_back, both, mi_3, gain_3, bias_3)
    return run(body, outs, ins, "grad_reduced")


def grad_last(q, normed, mi, every, gain, s, total):
    cells, half = q.shape

    def body(q_ref, n_ref, mi_ref, every_ref, g_ref, *refs):
        low_ref, sums_ref = refs
        sums, bias_term, gain_term = back_terms(every_ref, total)
        sums_ref[...] = sums
        norm_low(low_ref, q_ref, n_ref, mi_ref, g_ref[s : s + 1], bias_term, gain_term)

    outs = [shape((cells, half), bf16), shape((2, half))]
    return run(body, outs, (q, normed, mi, every, gain), "grad_last")


def input_grad(cots, conv, late, reduce_kernel, place):
    channels = cots[0].shape[3]
    narrow = channels - reduce_kernel.shape[0]

    def body(cot0_ref, cot1_ref, *refs):
        conv_refs, late_refs, (r_ref, place_ref), out_refs = refs[:4], refs[4:6], refs[6:8], refs[8:]
        c = place_ref[1]
        for kind, (cot_ref, out_ref) in enumerate(zip((cot0_ref, cot1_ref), out_refs)):
            _, rows, cols, _ = cot_ref.shape
            half = cols // 2
            for side, core in enumerate((c, 1 - c)):
                at = pl.ds(pl.multiple_of(core * half, half), half)
                into = dot_t(late_refs[side][kind], r_ref[...]).reshape(rows, half, channels - narrow)
                base = jnp.concatenate([conv_refs[side][kind], conv_refs[2 + side][kind]], axis=1)
                base = base.astype(f32).reshape(rows, half, channels) + cot_ref[0, :, at, :].astype(f32)
                out_ref[0, :, at, :narrow] = base[..., :narrow].astype(bf16)
                out_ref[0, :, at, narrow:] = (base[..., narrow:] + into).astype(bf16)

    outs = [shape(cot.shape, bf16) for cot in cots]
    ins = (*cots, *conv[0], *conv[1], *late, reduce_kernel, place)
    return run(body, outs, ins, "input_grad", limit=12, scalars=1)


def edge_cells(low, above, place, unit):
    cells, channels = low.shape
    blocks = cells // unit + 4

    def body(*refs):
        x_ref, place_ref, out_ref = refs[0], refs[-2], refs[-1]
        if above is None:
            zeros = jnp.zeros((2, channels), f32)
            ends = x_ref[...].astype(f32).reshape(blocks - 4, unit, channels)
            first = jnp.concatenate([zeros, ends[:, 0], zeros], axis=0)
            last = jnp.concatenate([zeros, ends[:, unit - 1], zeros], axis=0)
        else:
            wide = jnp.concatenate([refs[1][...], x_ref[...], refs[2][...]], axis=0)
            ends = wide.astype(f32).reshape(blocks, unit, channels)
            first, last = ends[:, 0], ends[:, unit - 1]
        land, left = place_ref[0] == 0, place_ref[1] == 0
        last = jnp.where(land, jnp.concatenate([last[1:], last[:1]], axis=0), last)
        first = jnp.where(land, jnp.concatenate([first[-1:], first[:-1]], axis=0), first)
        out_ref[...] = jnp.where(left, last, first).astype(bf16)

    ins = (low, place) if above is None else (low, *above, place)
    return run(body, [shape((blocks, channels), bf16)], ins, "edge_cells", scalars=1)[0]


def surroundings(low, place, unit):
    e_n = lax.axis_size("e")
    above = None
    if e_n > 1:
        ahead = [(e, e + 1) for e in range(e_n - 1)]
        above = (
            lax.ppermute(low[-2 * unit :], "e", ahead),
            lax.ppermute(low[: 2 * unit], "e", [(b, a) for a, b in ahead]),
        )
    beside = lax.ppermute(edge_cells(low, above, place, unit), "c", SWAP)
    return above, beside


def shifted_columns(x_ref, above_refs, beside_ref, land, left, out_ref, unit):
    cells, channels = x_ref.shape
    blocks = cells // unit + 4
    block = lax.broadcasted_iota(jnp.int32, (blocks, unit, 1), 0)
    cell = lax.broadcasted_iota(jnp.int32, (blocks, unit, 1), 1)
    for lane in range(0, channels, 128):
        at = slice(lane, lane + 128)
        if above_refs:
            top, bottom = above_refs[0][:, at], above_refs[1][:, at]
        else:
            top = bottom = jnp.zeros((2 * unit, 128), bf16)
        wide = jnp.concatenate([top, x_ref[:, at], bottom], axis=0)
        out_ref[1, :, at] = wide
        wide = wide.astype(f32)
        beside = beside_ref[:, at].astype(f32)[:, None, :]
        for j, edge, odd in ((0, 0, 0), (2, unit - 1, 1)):
            moved = pltpu.roll(wide, 1 if j == 0 else blocks * unit - 1, 0).reshape(blocks, unit, 128)
            outer_side = (cell == edge) & (jnp.logical_not(land) | (block % 2 == odd))
            fill = jnp.where(left if j == 2 else jnp.logical_not(left), beside, 0.0)
            out_ref[j, :, at] = jnp.where(outer_side, fill, moved).reshape(blocks * unit, 128).astype(bf16)


def rows_at(i, first, count, land, unit):
    if i == 1:
        return slice(2 * unit + first, 2 * unit + first + count)
    step = jnp.where(land, 2 * unit, unit)
    return pl.ds(pl.multiple_of(2 * unit + first + (i - 1) * step, unit), count)


def conv_forward(low, above, beside, place, unit, local_kernel, global_t):
    cells, channels = low.shape
    narrow = local_kernel.shape[1] // 9
    padded = cells + 4 * unit
    extra = () if above is None else above
    start = 4 + len(extra)

    def body(*refs):
        x_ref, beside_ref, l_ref, g_ref = refs[0], *refs[1 + len(extra) : 4 + len(extra)]
        place_ref, pre_ref, cols_ref, wide_ref = refs[start:]
        land, left = place_ref[0] == 0, place_ref[1] == 0
        shifted_columns(x_ref, refs[1 : 1 + len(extra)], beside_ref, land, left, wide_ref, unit)
        cols_ref[...] = wide_ref[:, :, :narrow]
        for at in blocks_of(cells, 512):
            count = at.stop - at.start
            local = jnp.zeros((count, narrow), f32)
            patches = []
            for t in range(9):
                block = wide_ref[t % 3, rows_at(t // 3, at.start, count, land, unit), :]
                local = local + dot(block, l_ref[:, t * narrow : (t + 1) * narrow])
                patches.append(block[:, :narrow])
            pre_ref[at, :narrow] = local
            pre_ref[at, narrow:] = dot_t(jnp.concatenate(patches, axis=1), g_ref[...])

    outs = [shape((cells, channels)), shape((3, padded, narrow), bf16)]
    ins = (low, *extra, beside, local_kernel, global_t, place)
    return run(body, outs, ins, "conv_forward", [pltpu.VMEM((3, padded, channels), bf16)], 12, 1)


def conv_backward(low, above, beside, place, unit, local_kernel, global_t, kind):
    cells, channels = low.shape
    narrow = local_kernel.shape[1] // 9
    padded = cells + 4 * unit
    extra = () if above is None else above
    start = 4 + len(extra)

    def body(*refs):
        x_ref, beside_ref, l_ref, g_ref = refs[0], *refs[1 + len(extra) : 4 + len(extra)]
        place_ref, grad_ref, patches_ref, wide_ref = refs[start:]
        land, left = place_ref[0] == 0, place_ref[1] == 0
        shifted_columns(x_ref, refs[1 : 1 + len(extra)], beside_ref, land, left, wide_ref, unit)
        for at in blocks_of(cells, 512):
            count = at.stop - at.start
            into = jnp.zeros((count, narrow), f32)
            for t in range(9):
                block = wide_ref[2 - t % 3, rows_at(2 - t // 3, at.start, count, land, unit), :]
                patches_ref[at, t * narrow : (t + 1) * narrow] = block[:, :narrow]
                into = into + dot(block[:, narrow:], g_ref[:, t * narrow : (t + 1) * narrow])
            grad = dot_t(patches_ref[at, :], l_ref[...])
            grad_ref[at, :narrow] = (grad[:, :narrow] + into).astype(kind)
            grad_ref[at, narrow:] = grad[:, narrow:].astype(kind)

    outs = [shape((cells, channels), kind), shape((cells, 9 * narrow), bf16)]
    ins = (low, *extra, beside, local_kernel, global_t, place)
    return run(body, outs, ins, "conv_backward", [pltpu.VMEM((3, padded, channels), bf16)], 12, 1)


def spaced(rows, own, pad):
    row = lax.broadcasted_iota(jnp.int32, (rows, rows // own * pad), 0)
    place = lax.broadcasted_iota(jnp.int32, (rows, rows // own * pad), 1)
    return jnp.where(place == row // own * pad + row % own, 1.0, 0.0).astype(bf16)


def gathered(shard, here):
    pieces = over_line([shard] * lax.axis_size(("k", "z", "e")))
    yield
    block = in_order(pieces, here[0]).reshape((-1,) + shard.shape)
    pieces = over_plane([block] * lax.axis_size("g"))
    others = [lax.ppermute(piece, "c", SWAP) for piece in pieces]
    yield
    return pieces + others


def assemble(full_ref, piece_refs, g, c):
    count = len(piece_refs) // 2
    for step in range(count):
        full_ref[g ^ step, c] = piece_refs[step][...]
        full_ref[g ^ step, 1 - c] = piece_refs[count + step][...]


def unpack_small(pieces, here, own, half):
    count = len(pieces)
    line_n, sections, pad, columns = pieces[0].shape
    devices = line_n * count
    wide = columns - 2 * half

    def body(*refs):
        g_ref, c_ref, *out_refs = refs[count:-1]
        full_ref = refs[-1]
        assemble(full_ref, refs[:count], g_ref[0], c_ref[0])
        place = spaced(devices * own, own, pad)
        for s in range(sections):
            full = dot(place, full_ref[:, :, :, s].reshape(devices * pad, columns)).astype(bf16)
            out_refs[3 * s][...] = full[:, :wide]
            out_refs[3 * s + 1][...] = full[:, wide : wide + half]
            out_refs[3 * s + 2][...] = full[:, wide + half :]

    outs = [shape((devices * own, width), bf16) for width in (wide, half, half)] * sections
    scratch = [pltpu.VMEM((count // 2, 2) + pieces[0].shape, bf16)]
    return run(body, outs, (*pieces, *here[1:]), "unpack_small", scratch, scalars=2)


def unpack_kernels(full, sections, own_in, pad_in, own_out):
    devices, _, rows, columns = full.shape
    pad = rows - pad_in
    plain = own_in == pad_in

    def body(full_ref, *refs):
        out_refs, local_ref, global_ref, sems = refs[: 2 * sections], *refs[2 * sections :]
        copies = []
        for s in range(sections):
            target = out_refs[2 * s] if plain else local_ref.at[s]
            copies.append(pltpu.make_async_copy(full_ref.at[:, s, :pad_in, :], target, sems.at[2 * s]))
            copies.append(pltpu.make_async_copy(full_ref.at[:, s, pad_in:, :], global_ref.at[s], sems.at[2 * s + 1]))
        for copy in copies:
            copy.start()
        for copy in copies:
            copy.wait()
        for s in range(sections):
            if not plain:
                block = local_ref[s].reshape(devices * pad_in, columns)
                out_refs[2 * s][...] = dot(spaced(devices * own_in, own_in, pad_in), block).astype(bf16)
            block = global_ref[s].reshape(devices * pad, columns)
            out_refs[2 * s + 1][...] = dot(spaced(devices * own_out, own_out, pad), block).astype(bf16)

    local = (devices, pad_in, columns) if plain else (devices * own_in, columns)
    outs = [shape(dims, bf16) for dims in (local, (devices * own_out, columns))] * sections
    scratch = [
        pltpu.VMEM((8,) * 4 if plain else (sections, devices, pad_in, columns), bf16),
        pltpu.VMEM((sections, devices, pad, columns), bf16),
        pltpu.SemaphoreType.DMA((2 * sections,)),
    ]
    limit = 12 if plain else 48
    out = run(body, outs, (InPlace(full),), "unpack_kernels", scratch, limit)
    return [(out[2 * s].reshape(devices * own_in, columns), out[2 * s + 1]) for s in range(sections)]


def early_grads(x_low, patches, grad_low, shifted, summed, place, unit, own, pad):
    cells, channels = x_low.shape
    narrow = shifted.shape[2]
    broad = channels - narrow
    half = summed.shape[1]

    def body(x_ref, p_ref, g_ref, s_ref, m_ref, *refs):
        place_ref, local_ref, other_ref = refs
        land = place_ref[0] == 0
        for i in range(3):
            at = slice(3 * i * narrow, 3 * (i + 1) * narrow)
            local_ref[:, at] = outer(x_ref[...], p_ref[:, at]).astype(bf16)
        grad = dot(g_ref[:, narrow:], spaced(broad, own, pad)).astype(bf16)
        for i in range(3):
            taps = [s_ref[j, rows_at(i, 0, cells, land, unit), :] for j in range(3)]
            at = slice(3 * i * narrow, 3 * (i + 1) * narrow)
            other_ref[:, at] = outer(grad, jnp.concatenate(taps, axis=1)).astype(bf16)
        other_ref[:, 9 * narrow :] = outer(grad, m_ref[...]).astype(bf16)

    outs = [shape((channels, 9 * narrow), bf16), shape((broad // own * pad, 9 * narrow + half), bf16)]
    ins = (x_low, patches, grad_low, shifted, summed, place)
    return run(body, outs, ins, "early_grads", limit=12, scalars=1)


def late_grads(x_low, reduced_low, real, imag, mixed_low, own, pad):
    channels = x_low.shape[1]
    wide = mixed_low.shape[1]
    half = reduced_low.shape[1]
    narrow = channels - wide

    def body(x_ref, r_ref, real_ref, imag_ref, m_ref, out_ref):
        freq = jnp.concatenate([outer(real_ref[...], m_ref[...]), outer(imag_ref[...], m_ref[...])], axis=0)
        reduce = outer(x_ref[:, narrow:], r_ref[...])
        place = spaced(wide, own, pad)
        out_ref[:, :wide] = outer(place, freq.astype(bf16)).astype(bf16)
        out_ref[:, wide:] = outer(place, reduce.astype(bf16)).astype(bf16)

    outs = [shape((wide // own * pad, wide + half), bf16)]
    return run(body, outs, (x_low, reduced_low, real, imag, mixed_low), "late_grads")[0]


def core_parts(shares, here, g_n):
    parts = [part.reshape((g_n, 2, -1) + part.shape[1:]) for part in shares]
    rows, widths = parts[0].shape[2], [part.shape[3] for part in parts]
    starts = [sum(widths[:i]) for i in range(len(widths) + 1)]

    def body(*refs):
        c = refs[len(parts)][0]
        theirs_ref, mine_ref = refs[len(parts) + 1 :]
        for i, ref in enumerate(refs[: len(parts)]):
            at = slice(starts[i], starts[i + 1])
            for g in range(g_n):
                theirs_ref[g, :, at] = ref[g, 1 - c]
                mine_ref[g, :, at] = ref[g, c]

    outs = [shape((g_n, rows, starts[-1]), bf16)] * 2
    return run(body, outs, (*parts, here[2]), "core_parts", scalars=1)


def add_parts(mine, theirs, here):
    g_n = mine.shape[0]

    def body(mine_ref, theirs_ref, *refs):
        for step in range(g_n):
            g = refs[0][0] ^ step
            total = mine_ref[g].astype(f32) + theirs_ref[g].astype(f32)
            refs[1 + step][...] = total if step == 0 else total.astype(bf16)

    outs = [shape(mine.shape[1:], f32 if step == 0 else bf16) for step in range(g_n)]
    return run(body, outs, (mine, theirs, here[1]), "add_parts", scalars=1)


def add_plane(pieces, here, line_n):
    rows, columns = pieces[0].shape
    block = rows // line_n

    def body(*refs):
        here_ref, *out_refs = refs[len(pieces) :]
        for step in range(line_n):
            there = here_ref[0] ^ step
            total = None
            for ref in refs[: len(pieces)]:
                part = ref[there].astype(f32)
                total = part if total is None else total + part
            out_refs[step][...] = total if step == 0 else total.astype(bf16)

    ins = [piece.reshape(line_n, block, columns) for piece in pieces]
    outs = [shape((block, columns), f32 if step == 0 else bf16) for step in range(line_n)]
    return run(body, outs, (*ins, here[0]), "add_plane", scalars=1)


def owned(shares, here):
    g_n = lax.axis_size("g")
    line_n = lax.axis_size(("k", "z", "e"))
    theirs, mine = core_parts(shares, here, g_n)
    theirs = lax.ppermute(theirs, "c", SWAP)
    yield
    pieces = over_plane(add_parts(mine, theirs, here))
    yield
    pieces = over_line(add_plane(pieces, here, line_n))
    yield
    return pieces


def owned_groups(grads, here, alike):
    return [owned(grads, here)] if alike else [owned((grad,), here) for grad in grads]


def settle(groups):
    flat = [piece for group in groups for piece in group]

    def body(*refs):
        at = 0
        for group, out_ref in zip(groups, refs[len(flat) :]):
            total = refs[at][...]
            for ref in refs[at + 1 : at + len(group)]:
                total = total + ref[...].astype(f32)
            out_ref[...] = total
            at += len(group)

    return run(body, [shape(group[0].shape) for group in groups], flat, "settle")


def pack_sums(sums):
    widths = [item.shape[1] for item in sums]

    def body(*refs):
        refs[-1][...] = jnp.concatenate([ref[...] for ref in refs[:-1]], axis=1)

    return run(body, [shape((2, sum(widths)))], sums, "pack_sums")[0]


def results(totals, sums, other_sums, own_in, own_out, narrow, half, channels):
    sections = len(totals)
    flat = [item for group in totals for item in group]
    widths = [[item.shape[1] for item in group] for group in totals]

    def body(*refs):
        sums_ref, other_ref, local_ref, global_ref, reduce_ref, freq_ref, expand_ref, *norm_refs = refs[len(flat) :]
        first = 0
        for s in range(sections):
            group = refs[first : first + len(widths[s])]
            first += len(widths[s])

            def columns(start, count, rows):
                for ref, wide in zip(group, widths[s]):
                    if start < wide:
                        return ref[:rows, start : start + count]
                    start -= wide

            for t in range(9):
                local_ref[s, t] = columns(t * narrow, narrow, own_in)
                global_ref[t, :, s, :] = columns((9 + t) * narrow, narrow, own_out)
            expand_ref[:, s, :] = columns(18 * narrow, half, own_out)
            freq_ref[:, s, :] = columns(18 * narrow + half, 2 * half, own_out)
            reduce_ref[:, s, :] = columns(18 * narrow + 3 * half, half, own_out)
        both = sums_ref[...] + other_ref[...]
        at = 0
        for s in range(sections):
            for index, wide in enumerate((half, 2 * half, channels)):
                norm_refs[2 * index][s : s + 1, :] = both[1:2, at : at + wide]
                norm_refs[2 * index + 1][s : s + 1, :] = both[0:1, at : at + wide]
                at += wide

    outs = [
        shape((sections, 9, own_in, narrow)),
        shape((9, own_out, sections, narrow)),
        shape((own_out, sections, half)),
        shape((own_out, sections, 2 * half)),
        shape((own_out, sections, half)),
    ]
    outs += [shape((sections, wide)) for wide in (half, half, 2 * half, 2 * half, channels, channels)]
    out = run(body, outs, (*flat, sums, other_sums), "results")
    return (
        out[0],
        jnp.transpose(out[1], (2, 0, 3, 1)),
        jnp.transpose(out[2], (1, 0, 2)),
        jnp.transpose(out[3], (1, 0, 2)),
        jnp.transpose(out[4], (1, 2, 0)),
        *out[5:],
    )


def pick_tables(tables, variant):
    count = len(tables)

    def body(*refs):
        v = refs[count][0]
        copies = [
            pltpu.make_async_copy(refs[i].at[v], refs[count + 1 + i], refs[-1].at[i]) for i in range(count)
        ]
        for copy in copies:
            copy.start()
        for copy in copies:
            copy.wait()

    outs = [shape(table.shape[1:], table.dtype) for table in tables]
    scratch = [pltpu.SemaphoreType.DMA((count,))]
    return run(body, outs, (*[InPlace(table) for table in tables], variant), "pick_tables", scratch, 44, 1)


def per_device(plan, *args):
    (
        land,
        port,
        to_local,
        to_global,
        reduce_weight,
        freq_weight,
        expand_weight,
        spec_gain,
        spec_bias,
        freq_gain,
        freq_bias,
        out_gain,
        out_bias,
        cot_land,
        cot_port,
    ) = args
    rounds, forward_table, inverse_table, weight_table, point_counts = plan
    sections = to_local.shape[0]
    devices = lax.axis_size(ALL)
    own_in = to_local.shape[2]
    own_out = to_global.shape[3]
    pad = -(-own_out // 16) * 16
    narrow = to_local.shape[3]
    channels = own_in * devices
    half = reduce_weight.shape[2]
    unit = port.shape[2] // 2
    k, c, part = lax.axis_index("k"), lax.axis_index("c"), lax.axis_index(PART)
    line_here = lax.axis_index(("k", "z", "e"))
    place = jnp.stack([k, c, line_here]).astype(jnp.int32)
    here = tuple(index.astype(jnp.int32).reshape(1) for index in (line_here, lax.axis_index("g"), c))
    variant = k * lax.axis_size(PART) + part
    g_n, z_n, e_n = lax.axis_size("g"), lax.axis_size("z"), lax.axis_size("e")
    width = lax.axis_size(KIND)

    pad_in = -(-own_in // 16) * 16
    Order.last = ()

    grow = ((0, 0), (0, pad - own_out), (0, 0))
    taps_local = jnp.transpose(to_local, (0, 2, 1, 3)).reshape(sections, own_in, 9 * narrow)
    taps_local = jnp.pad(taps_local, ((0, 0), (0, pad_in - own_in), (0, 0)))
    taps_global = jnp.pad(jnp.transpose(to_global, (0, 3, 1, 2)).reshape(sections, own_out, 9 * narrow), grow)
    taps = lax.all_gather(jnp.concatenate([taps_local, taps_global], axis=1), ALL)
    x_steps = to_tile(land, port, rounds, place, here, narrow)
    advance(x_steps)
    advance(x_steps)
    packed = jnp.concatenate([freq_weight, reduce_weight, jnp.transpose(expand_weight, (0, 2, 1))], axis=2)
    small_steps = gathered(jnp.pad(packed, grow), here)
    advance(small_steps)
    tables = (jnp.asarray(forward_table), jnp.asarray(inverse_table), jnp.asarray(weight_table)[..., None])
    forward, inverse, factor = pick_tables(tables, variant.reshape(1))
    advance(small_steps)
    small = unpack_small(finish(small_steps), here, own_out, half)
    x_broad = advance(x_steps)

    cells = x_broad.shape[0]
    size = cells * lax.axis_size(PART)
    scale = 1.0 / math.sqrt(size)
    cell_total = float(g_n * z_n * size)
    point_totals = [int(item.sum()) * g_n * z_n for item in point_counts]

    def exchange(stats):
        every = lax.all_to_all(stats, KIND, 0, 0, tiled=True)
        Order.last = (every,)
        return every

    kept = []
    for s in range(sections):
        freq_kernel, reduce_kernel, expand_t = small[3 * s : 3 * s + 3]
        if s == 0:
            reduced, stats = reduce_first(x_broad, reduce_kernel, width)
        else:
            low, reduced, stats, kept[-1]["mi_3"] = reduce_next(both, every, out_gain, out_bias, s - 1, reduce_kernel, narrow)
        every = exchange(stats)
        if s == 0:
            x = low = finish(x_steps)
            cot_steps = to_tile(cot_land, cot_port, rounds, place, here)
            advance(cot_steps)
        above, beside = surroundings(low, place, unit)
        hidden_low, hidden, mi_1 = hidden_act(reduced, every, spec_gain, spec_bias, s)
        others = shared(hidden_low)
        if s > 0:
            pre, shifted = conv_forward(low, above, beside, place, unit, *kernels[s])
        else:
            advance(cot_steps)
        real, imag, mixed, stats = spectrum_forward(forward, hidden_low, others, freq_kernel, factor, scale, width)
        every = exchange(stats)
        freq_low, mi_2 = freq_act(mixed, every, freq_gain, freq_bias, s, factor, place, point_counts, e_n, z_n)
        others = shared(freq_low)
        if s == 0:
            kernels = unpack_kernels(taps, sections, own_in, pad_in, own_out)
            pre, shifted = conv_forward(low, above, beside, place, unit, *kernels[s])
        summed, both, stats = inverse_forward(inverse, freq_low, others, hidden, pre, expand_t, scale, width)
        if s == 0:
            cot = finish(cot_steps)
        every = exchange(stats)
        kept.append(
            dict(low=low, shifted=shifted, reduced=reduced, mi_1=mi_1, real=real, imag=imag, mixed=mixed, mi_2=mi_2, summed=summed, both=both)
        )
    out, q_3, sums, kept[-1]["mi_3"] = turn(both, every, out_gain, out_bias, sections - 1, x, cot)

    totals = [None] * sections
    norm_sums = [None] * sections
    out_steps = None
    grads = ()
    for s in reversed(range(sections)):
        freq_kernel, reduce_kernel, expand_t = small[3 * s : 3 * s + 3]
        item = kept[s]
        above_steps = []
        every = exchange(sums)
        low, summed, summed_low, sums_3 = grad_pre(
            q_3, item["both"], item["mi_3"], every, out_gain, s, expand_t, cell_total
        )
        others = shared(summed_low)
        if out_steps is None:
            out_steps = from_tile(out, rounds, place, here)
            advance(out_steps)
        above, beside = surroundings(low, place, unit)
        if s + 1 < sections:
            last = kept[s + 1]
            late_grad = late_grads(last["low"], reduced_low, last["real"], last["imag"], mixed_low, own_out, pad)
            above_steps = owned_groups((*grads, late_grad), here, own_in == pad)
            for steps in above_steps:
                advance(steps)

        def convolve():
            back, patches = conv_backward(low, above, beside, place, unit, *kernels[s], f32 if s > 0 else bf16)
            return back, early_grads(item["low"], patches, low, item["shifted"], item["summed"], place, unit, own_out, pad)

        if s == 0:
            conv_back, grads = convolve()
            conv_steps = [from_tile(conv_back, rounds, place, here, lanes) for lanes in (slice(0, channels // 2), slice(channels // 2, channels))]
            for steps in conv_steps:
                advance(steps)
            early_steps = owned_groups(grads, here, own_in == pad)
            for steps in early_steps + above_steps:
                advance(steps)
        q, sums, normed = spectrum_backward(
            forward, summed_low, others, item["mixed"], item["mi_2"], freq_gain, freq_bias, s, factor, scale, width
        )
        every = exchange(sums)
        mixed_low, back, sums_2 = grad_mixed(
            q, normed, item["mi_2"], every, freq_gain, s, freq_kernel, place, point_totals
        )
        others = shared(back)
        if s > 0:
            conv_back, grads = convolve()
            if s == sections - 1:
                out_parts = finish(out_steps)
        else:
            for steps in above_steps:
                advance(steps)
            conv_parts = [finish(conv_steps[0])]
            for steps in early_steps:
                advance(steps)
        q, sums, normed = inverse_backward(
            inverse, back, others, summed, item["reduced"], item["mi_1"], spec_gain, spec_bias, s, scale, width
        )
        every = exchange(sums)
        if s > 0:
            if s == sections - 1:
                land_out, port_out = join_halves(*out_parts, (land, port), place)
            below = kept[s - 1]
            reduced_low, q_3, sums, sums_1 = grad_reduced(
                q, normed, item["mi_1"], every, spec_gain, s, reduce_kernel, cell_total,
                conv_back, below["both"], below["mi_3"], out_gain, out_bias, width,
            )
        else:
            reduced_low, sums_1 = grad_last(q, normed, item["mi_1"], every, spec_gain, s, cell_total)
        norm_sums[s] = (sums_1, sums_2, sums_3)
        if above_steps:
            totals[s + 1] = above_steps

    end_steps = from_tile(reduced_low, rounds, place, here)
    advance(end_steps)
    late_grad = late_grads(kept[0]["low"], reduced_low, kept[0]["real"], kept[0]["imag"], mixed_low, own_out, pad)
    late_steps = owned((late_grad,), here)
    advance(late_steps)
    packed_sums = pack_sums([item for s in range(sections) for item in norm_sums[s]])
    other_sums = lax.ppermute(packed_sums, "k", SWAP)
    for steps in early_steps:
        advance(steps)
    advance(late_steps)
    conv_parts.append(finish(conv_steps[1]))
    end_parts = finish(end_steps)
    advance(late_steps)
    land_grad, port_grad = input_grad((cot_land, cot_port), conv_parts, end_parts, small[1], place)
    for s in range(1, sections):
        totals[s] = settle([finish(steps) for steps in totals[s]])
    totals[0] = settle([finish(steps) for steps in early_steps] + [finish(late_steps)])
    rest = results(totals, packed_sums, other_sums, own_in, own_out, narrow, half, channels)
    return (land_out, port_out, land_grad, port_grad, *rest)


def solution(mesh):
    f_n, s_n = mesh.shape["fsdp"], mesh.shape["sp"]
    e_n = s_n // 4
    fine = Mesh(np.asarray(mesh.devices).reshape(f_n // 2, 2, 2, 2, e_n), ALL)
    maps = P(("g", "c"), ("k", "z", "e"), None, None)
    split = ALL

    def whole(*args):
        land, port = args[0], args[1]
        plan = (
            routes(e_n),
            *transform_tables(e_n, land.shape[1:3], port.shape[1:3]),
        )
        weights = (
            P(None, None, split, None),
            P(None, None, None, split),
            P(None, split, None),
            P(None, split, None),
            P(None, None, split),
        )
        return jax.shard_map(
            lambda *local: per_device(plan, *local),
            mesh=fine,
            in_specs=(maps, maps, *weights, P(), P(), P(), P(), P(), P(), maps, maps),
            out_specs=(maps, maps, maps, maps, *weights, P(), P(), P(), P(), P(), P()),
            check_vma=False,
        )(*args)

    return whole
```

```python
import math

import jax
import jax.numpy as jnp
import numpy as np
from jax import lax
from jax.experimental import pallas as pl
from jax.experimental.pallas import tpu as pltpu
from jax.sharding import Mesh, PartitionSpec as P

EPS = 1e-05
LINE = ("c", "k", "z", "e")
KIND = ("g", "c", "z", "e")
PART = ("c", "e")
ALL = ("g", "c", "k", "z", "e")
f32 = jnp.float32
bf16 = jnp.bfloat16


def routes(e_n):
    s_n = 4 * e_n
    count = 2 * s_n
    left = []
    for c in range(2):
        for s in range(s_n):
            for unit in range(4):
                kind, half = unit // 2, unit % 2
                left.append((c * s_n + s, unit, half * s_n + (kind * 2 + c) * e_n + s // 4, s % 4))
    rounds = []
    for _ in range(4):
        owner = {}

        def augment(src, seen):
            for edge in left:
                if edge[0] == src and edge[2] not in seen:
                    seen.add(edge[2])
                    if edge[2] not in owner or augment(owner[edge[2]][0], seen):
                        owner[edge[2]] = edge
                        return True
            return False

        for src in range(count):
            assert augment(src, set())
        chosen = list(owner.values())
        for edge in chosen:
            left.remove(edge)
        sent = np.zeros(count, np.int32)
        slot = np.zeros(count, np.int32)
        for edge in chosen:
            sent[edge[0]] = edge[1]
            slot[edge[2]] = edge[3]
        rounds.append(([(edge[0], edge[2]) for edge in chosen], sent, slot))
    return rounds


def transform_tables(e_n, land_shape, port_shape):
    parts = 2 * e_n
    shapes = (land_shape, port_shape)
    most = max(rows * (cols // 2 + 1) for rows, cols in shapes)
    per_part = -(-most // (16 * parts)) * 16
    forward, inverse, weight, counts = [], [], [], []
    for rows, cols in shapes:
        half = cols // 2 + 1
        point = np.arange(per_part * parts)
        valid = point < rows * half
        kr, f = point // half, point % half
        tiles = []
        for part in range(parts):
            c, e = part // e_n, part % e_n
            h = np.arange(rows // e_n) + e * (rows // e_n)
            w = np.arange(cols // 2) + c * (cols // 2)
            tiles.append((np.repeat(h, len(w)), np.tile(w, len(h))))
        cell_h = np.concatenate([tile[0] for tile in tiles])
        cell_w = np.concatenate([tile[1] for tile in tiles])
        size = rows * cols
        phase = (kr[:, None] * cell_h[None, :] * cols + f[:, None] * cell_w[None, :] * rows) % size
        angle = phase * (2.0 * math.pi / size)
        table = np.stack([np.cos(angle), -np.sin(angle)]) * valid[None, :, None]
        table = table.astype(np.float32).astype(jnp.bfloat16)
        cells = size // parts
        factor = np.where((f == 0) | (2 * f == cols), 1.0, 2.0) * valid
        counts.append([int(valid[p * per_part : (p + 1) * per_part].sum()) for p in range(parts)])
        for part in range(parts):
            order = [(part + step) % parts for step in range(parts)]
            own_points = slice(part * per_part, (part + 1) * per_part)
            own_cells = slice(part * cells, (part + 1) * cells)
            forward.append(
                np.concatenate([table[:, own_points, q * cells : (q + 1) * cells] for q in order], axis=2)
            )
            back = np.concatenate([table[:, q * per_part : (q + 1) * per_part, own_cells] for q in order], axis=1)
            inverse.append(np.ascontiguousarray(back.transpose(0, 2, 1)))
            weight.append(factor[own_points].astype(np.float32))
    forward, inverse = (np.stack(item).reshape(len(item), -1, item[0].shape[2]) for item in (forward, inverse))
    wide = max(-(-forward.shape[2] // 128), -(-inverse.shape[2] // 128)) * 128
    forward, inverse = (np.pad(item, ((0, 0), (0, 0), (0, wide - item.shape[2]))) for item in (forward, inverse))
    return np.concatenate([forward, inverse], axis=1), np.stack(weight), np.asarray(counts, np.int32)


SWAP = [(0, 1), (1, 0)]


def pick(table, index):
    return lax.dynamic_index_in_dim(jnp.asarray(table), index, 0, keepdims=False)


def partners(pieces, axes, step):
    count = lax.axis_size(axes)
    return lax.ppermute(pieces, axes, [(i, i ^ step) for i in range(count)])


def split_halves(land, port, place):
    channels = land.shape[3]
    shapes = [maps.shape[1:3] for maps in (land, port)]
    cells = shapes[0][0] * shapes[0][1] // 2

    def body(land_ref, port_ref, place_ref, mine_ref, theirs_ref):
        c = place_ref[1]
        for kind, ref in enumerate((land_ref, port_ref)):
            half = shapes[kind][1] // 2
            for out_ref, core in ((mine_ref, c), (theirs_ref, 1 - c)):
                at = pl.ds(pl.multiple_of(core * half, half), half)
                out_ref[kind] = ref[0, :, at, :].reshape(cells, channels)

    outs = [shape((2, cells, channels), land.dtype)] * 2
    return run(body, outs, (land, port, place), "split_halves", scalars=1)


def join_halves(mine, theirs, like, place):
    def body(mine_ref, theirs_ref, place_ref, *out_refs):
        c = place_ref[1]
        for kind, out_ref in enumerate(out_refs):
            _, rows, cols, channels = out_ref.shape
            half = cols // 2
            for ref, core in ((mine_ref, c), (theirs_ref, 1 - c)):
                at = pl.ds(pl.multiple_of(core * half, half), half)
                out_ref[0, :, at, :] = ref[kind].reshape(rows, half, channels)

    return run(body, [shape(maps.shape, maps.dtype) for maps in like], (mine, theirs, place), "join_halves", scalars=1)


def to_slots(mine, theirs, place):
    def body(mine_ref, theirs_ref, place_ref, *out_refs):
        here, c = place_ref[2], place_ref[1]
        for step, out_ref in enumerate(out_refs):
            there = here ^ step
            kind, core = there // 2, there % 2

            @pl.when(core == c)
            def _():
                out_ref[...] = mine_ref[kind]

            @pl.when(core != c)
            def _():
                out_ref[...] = theirs_ref[kind]

    outs = [shape(mine.shape[1:], mine.dtype)] * 4
    return run(body, outs, (mine, theirs, place), "to_slots", scalars=1)


def from_slots(pieces, place):
    def body(*refs):
        place_ref, mine_ref, theirs_ref = refs[-3:]
        here, c = place_ref[2], place_ref[1]
        for step in range(4):
            there = here ^ step
            kind, core = there // 2, there % 2

            @pl.when(core == c)
            def _():
                mine_ref[kind] = refs[step][...]

            @pl.when(core != c)
            def _():
                theirs_ref[kind] = refs[step][...]

    outs = [shape((2,) + pieces[0].shape, pieces[0].dtype)] * 2
    return run(body, outs, (*pieces, place), "from_slots", scalars=1)


def in_order(pieces, here):
    rows = pieces[0].shape[0]

    def body(*refs):
        here_ref, out_ref = refs[-2:]
        for step in range(len(pieces)):
            out_ref[here_ref[0] ^ step] = refs[step][...]

    outs = [shape((len(pieces),) + pieces[0].shape, pieces[0].dtype)]
    out = run(body, outs, (*pieces, here), "in_order", scalars=1)[0]
    return out.reshape((len(pieces) * rows,) + pieces[0].shape[1:])


def for_partners(blocks, here):
    count = blocks.shape[0]

    def body(blocks_ref, here_ref, *out_refs):
        for step in range(count):
            out_refs[step][...] = blocks_ref[here_ref[0] ^ step]

    outs = [shape(blocks.shape[1:], blocks.dtype)] * count
    return run(body, outs, (blocks, here), "for_partners", scalars=1)


def advance(steps):
    return next(steps)


def finish(steps):
    while True:
        try:
            next(steps)
        except StopIteration as stop:
            return stop.value


def over_line(pieces):
    axes = ("k", "z", "e")
    return [pieces[0]] + [partners(pieces[step], axes, step) for step in range(1, lax.axis_size(axes))]


def over_plane(pieces):
    return [pieces[0]] + [partners(pieces[step], "g", step) for step in range(1, lax.axis_size("g"))]


def to_tile(land, port, rounds, place, here):
    channels = land.shape[3]
    if lax.axis_size("e") == 1:
        mine, theirs = split_halves(land, port, place)
        theirs = lax.ppermute(theirs, "c", SWAP)
        yield
        pieces = over_line(to_slots(mine, theirs, place))
        yield
        return in_order(pieces, here[0])
    me = lax.axis_index(LINE)
    units = []
    for maps in (land, port):
        cols = maps.shape[2] // 2
        units += [maps[0, :, :cols].reshape(-1, channels), maps[0, :, cols:].reshape(-1, channels)]
    units = jnp.stack(units)
    got = [lax.ppermute(pick(units, pick(sent, me)), LINE, pairs) for pairs, sent, _ in rounds]
    yield
    slots = np.stack([slot for _, _, slot in rounds], axis=1)
    order = pick(np.argsort(slots, axis=1).astype(np.int32), me)
    yield
    return jnp.concatenate([pick(jnp.stack(got), order[i]) for i in range(4)], axis=0)


def from_tile(tile, rounds, place, here):
    units = tile.reshape(4, -1, tile.shape[1])
    if lax.axis_size("e") == 1:
        pieces = over_line(for_partners(units, here[0]))
        yield
        mine, theirs = from_slots(pieces, place)
        return mine, lax.ppermute(theirs, "c", SWAP)
    me = lax.axis_index(LINE)
    got = [lax.ppermute(pick(units, pick(slot, me)), LINE, [(b, a) for a, b in pairs]) for pairs, _, slot in rounds]
    yield
    sents = np.stack([sent for _, sent, _ in rounds], axis=1)
    order = pick(np.argsort(sents, axis=1).astype(np.int32), me)
    both = jnp.stack([pick(jnp.stack(got), order[i]) for i in range(4)]).reshape((2, 2) + units.shape[1:])
    c = lax.axis_index("c")
    return (
        lax.dynamic_index_in_dim(both, c, 1, keepdims=False),
        lax.dynamic_index_in_dim(both, 1 - c, 1, keepdims=False),
    )


def shared(block):
    parts = lax.axis_size(PART)
    pieces = [
        lax.ppermute(block, PART, [((p + step) % parts, p) for p in range(parts)]) for step in range(1, parts)
    ]
    return pieces[0] if parts == 2 else jnp.concatenate(pieces, axis=0)


def gelu_parts(v):
    k = math.sqrt(2.0 / math.pi)
    square = v * v
    t = jnp.tanh(k * v * (1.0 + 0.044715 * square))
    half = 0.5 * (1.0 + t)
    return v * half, half + 0.5 * v * (1.0 - t * t) * (k * (1.0 + 3.0 * 0.044715 * square))


def gelu(v):
    return 0.5 * v * (1.0 + jnp.tanh(math.sqrt(2.0 / math.pi) * v * (1.0 + 0.044715 * (v * v))))


def dot(a, b):
    return lax.dot_general(a, b, (((1,), (0,)), ((), ())), preferred_element_type=f32)


def dot_t(a, b):
    return lax.dot_general(a, b, (((1,), (1,)), ((), ())), preferred_element_type=f32)


def outer(a, b):
    return lax.dot_general(a, b, (((0,), (0,)), ((), ())), preferred_element_type=f32)


def device_counts(counts, kind, width, e_n, z_n):
    row = lax.broadcasted_iota(jnp.int32, (width, 1), 0)
    part = row // (e_n * z_n) % 2 * e_n + row % e_n
    out = jnp.zeros((width, 1), f32)
    for p in range(len(counts[0])):
        out = jnp.where(part == p, jnp.where(kind == 0, float(counts[0][p]), float(counts[1][p])), out)
    return out


def moments(every, counts, total):
    sums, squares = every[:, 0, :], every[:, 1, :]
    mean = jnp.sum(sums, axis=0, keepdims=True) / total
    apart = sums / counts - mean
    square = jnp.sum(squares + counts * apart * apart, axis=0, keepdims=True)
    return mean, lax.rsqrt(square / total + EPS)


def emit(out_ref, first, second):
    both = jnp.concatenate([first, second], axis=0)
    out_ref[...] = jnp.broadcast_to(both[None], out_ref.shape)


def row_step(rows):
    return next(step for step in (64, 32, 16, 8) if rows % step == 0)


def sweep(rows, body, carry=0, step=None):
    step = step or row_step(rows)
    if rows == step:
        return body(slice(0, rows), carry)
    return lax.fori_loop(0, rows // step, lambda i, carry: body(pl.ds(pl.multiple_of(i * step, step), step), carry), carry)


def folded(values):
    return jnp.sum(values.reshape(values.shape[0] // 8, 8, values.shape[1]), axis=0)


def column(values):
    return jnp.sum(values, axis=0, keepdims=True)


def emit_moments(out_ref, ref, count, factor_ref=None):
    rows, columns = ref.shape
    zero = jnp.zeros((8, columns), f32)
    local_sum = column(sweep(rows, lambda at, acc: acc + folded(ref[at, :]), zero))
    mean = local_sum / count

    def squares(at, acc):
        centered = ref[at, :] - mean
        if factor_ref is not None:
            centered = jnp.where(factor_ref[at, :] > 0.0, centered, 0.0)
        return acc + folded(centered * centered)

    emit(out_ref, local_sum, column(sweep(rows, squares, zero)))


def pair(columns):
    return jnp.zeros((8, columns), f32), jnp.zeros((8, columns), f32)


def add_sums(sums, q, normed):
    return sums[0] + folded(q), sums[1] + folded(q * normed)


def emit_sums(out_ref, sums):
    emit(out_ref, column(sums[0]), column(sums[1]))


def back_terms(every_ref, total):
    sums = jnp.sum(every_ref[...], axis=0)
    return sums, sums[0:1] / total, sums[1:2] / total


VMEM = pl.BlockSpec(memory_space=pltpu.VMEM)
SMEM = pl.BlockSpec(memory_space=pltpu.SMEM)
ANY = pl.BlockSpec(memory_space=pl.ANY)
HBM = pl.BlockSpec(memory_space=pltpu.HBM)


class Order:
    last = ()


def run(body, outs, ins, name, scratch=(), limit=8, scalars=0):
    vectors = len(ins) - scalars
    waits = len(Order.last)

    def ordered(*refs):
        body(*refs[:vectors], *refs[vectors + waits :])

    result = pl.pallas_call(
        ordered,
        out_shape=outs,
        in_specs=[HBM if item is None else VMEM for item in _spaces(ins[:vectors])] + [ANY] * waits + [SMEM] * scalars,
        out_specs=[VMEM] * len(outs),
        scratch_shapes=list(scratch),
        cost_estimate=pl.CostEstimate(flops=1, bytes_accessed=1, transcendentals=0),
        compiler_params=pltpu.CompilerParams(vmem_limit_bytes=limit * 1024 * 1024),
        name=name,
    )(*[item.array if isinstance(item, InPlace) else item for item in ins[:vectors]], *Order.last, *ins[vectors:])
    Order.last = (result[0],)
    return result


def hold(*arrays):
    Order.last = (*Order.last, *arrays)


def gate(every):
    def body(in_ref, out_ref):
        out_ref[...] = in_ref[0]

    run(body, [shape(every.shape[1:])], (every,), "gate")


class InPlace:
    def __init__(self, array):
        self.array = array


def _spaces(items):
    return [None if isinstance(item, InPlace) else item for item in items]


def shape(dims, kind=f32):
    return jax.ShapeDtypeStruct(tuple(dims), kind)


def reduce_first(x, reduce_kernel, width, narrow):
    cells = x.shape[0]
    half = reduce_kernel.shape[1]

    def body(x_ref, r_ref, reduced_ref, stats_ref):
        reduced_ref[...] = dot(x_ref[:, narrow:], r_ref[...])
        emit_moments(stats_ref, reduced_ref, float(cells))

    return run(body, [shape((cells, half)), shape((width, 2, half))], (x, reduce_kernel), "reduce_first")


def reduce_next(both, every, gain, bias, s, reduce_kernel, narrow):
    cells, channels = both.shape
    half = reduce_kernel.shape[1]
    width = every.shape[0]

    def body(both_ref, every_ref, g_ref, b_ref, r_ref, low_ref, reduced_ref, stats_ref, mi_ref):
        mean, inv = moments(every_ref[...], float(cells), float(cells * width))
        mi_ref[...] = jnp.concatenate([mean, inv], axis=0)
        gain_row, bias_row = g_ref[s : s + 1], b_ref[s : s + 1]

        def apply(at, carry):
            low_ref[at, :] = gelu((both_ref[at, :] - mean) * inv * gain_row + bias_row).astype(bf16)
            return carry

        sweep(cells, apply, step=32)
        reduced_ref[...] = dot(low_ref[:, narrow:], r_ref[...])
        emit_moments(stats_ref, reduced_ref, float(cells))

    outs = [shape((cells, channels), bf16), shape((cells, half)), shape((width, 2, half)), shape((2, channels))]
    return run(body, outs, (both, every, gain, bias, reduce_kernel), "reduce_next")


def hidden_act(reduced, every, gain, bias, s):
    cells, channels = reduced.shape
    width = every.shape[0]

    def body(v_ref, every_ref, g_ref, b_ref, low_ref, hidden_ref, mi_ref):
        mean, inv = moments(every_ref[...], float(cells), float(cells * width))
        mi_ref[...] = jnp.concatenate([mean, inv], axis=0)
        gain_row, bias_row = g_ref[s : s + 1], b_ref[s : s + 1]

        def apply(at, carry):
            act = gelu((v_ref[at, :] - mean) * inv * gain_row + bias_row)
            hidden_ref[at, :] = act
            low_ref[at, :] = act.astype(bf16)
            return carry

        sweep(cells, apply)

    outs = [shape((cells, channels), bf16), shape((cells, channels)), shape((2, channels))]
    return run(body, outs, (reduced, every, gain, bias), "hidden_act")


def freq_act(mixed, every, gain, bias, s, factor, place, counts, e_n, z_n):
    points, channels = mixed.shape
    width = every.shape[0]

    def body(v_ref, every_ref, g_ref, b_ref, factor_ref, place_ref, low_ref, mi_ref):
        by_device = device_counts(counts, place_ref[0], width, e_n, z_n)
        mean, inv = moments(every_ref[...], by_device, jnp.sum(by_device))
        mi_ref[...] = jnp.concatenate([mean, inv], axis=0)
        gain_row, bias_row = g_ref[s : s + 1], b_ref[s : s + 1]

        def apply(at, carry):
            act = gelu((v_ref[at, :] - mean) * inv * gain_row + bias_row)
            low_ref[at, :] = (act * factor_ref[at, :]).astype(bf16)
            return carry

        sweep(points, apply)

    outs = [shape((points, channels), bf16), shape((2, channels))]
    return run(body, outs, (mixed, every, gain, bias, factor, place), "freq_act", scalars=1)


def blocks_of(rows, most):
    count = -(-rows // most)
    while rows % (16 * count):
        count += 1
    return [slice(i * rows // count, (i + 1) * rows // count) for i in range(count)]


def spectrum_forward(table, own, others, freq_kernel, factor, scale, width):
    points = table.shape[1]
    cells, half = own.shape
    wide = freq_kernel.shape[1]

    def body(t_ref, own_ref, others_ref, w_ref, factor_ref, real_ref, imag_ref, mixed_ref, stats_ref):
        for side, out_ref in enumerate((real_ref, imag_ref)):
            for at in blocks_of(points, 272):
                z = dot(t_ref[side, at, :cells], own_ref[...]) + dot(t_ref[side, at, cells:], others_ref[...])
                out_ref[at, :] = (z * scale).astype(bf16)
        mixed_ref[...] = dot(real_ref[...], w_ref[:half]) + dot(imag_ref[...], w_ref[half:])
        count = jnp.sum(jnp.where(factor_ref[...] > 0.0, 1.0, 0.0))
        emit_moments(stats_ref, mixed_ref, count, factor_ref)

    outs = [shape((points, half), bf16), shape((points, half), bf16), shape((points, wide)), shape((width, 2, wide))]
    return run(body, outs, (table, own, others, freq_kernel, factor), "spectrum_forward")


def inverse_forward(table, own, others, hidden, pre, expand_t, scale, width):
    cells = table.shape[1]
    half = hidden.shape[1]
    channels = pre.shape[1]
    narrow = channels - expand_t.shape[0]

    def body(t_ref, own_ref, others_ref, hidden_ref, pre_ref, e_ref, summed_ref, both_ref, stats_ref):
        freq = jnp.concatenate([own_ref[...], others_ref[...]], axis=0)
        real, imag = freq[:, :half], freq[:, half:]
        total = freq.shape[0]
        for at in blocks_of(cells, 256):
            returned = dot(t_ref[0, at, :total], real) + dot(t_ref[1, at, :total], imag)
            summed_ref[at, :] = (hidden_ref[at, :] + returned * scale).astype(bf16)
        both_ref[:, :narrow] = pre_ref[:, :narrow]
        for at in blocks_of(cells, 256):
            both_ref[at, narrow:] = pre_ref[at, narrow:] + dot_t(summed_ref[at, :], e_ref[...])
        emit_moments(stats_ref, both_ref, float(cells))

    outs = [shape((cells, half), bf16), shape((cells, channels)), shape((width, 2, channels))]
    return run(body, outs, (table, own, others, hidden, pre, expand_t), "inverse_forward")


def turn(both, every, gain, bias, s, x, cot):
    cells, channels = both.shape

    width = every.shape[0]

    def body(both_ref, every_ref, g_ref, b_ref, x_ref, cot_ref, out_ref, q_ref, sums_ref, mi_ref):
        mean, inv = moments(every_ref[...], float(cells), float(cells * width))
        mi_ref[...] = jnp.concatenate([mean, inv], axis=0)
        gain_row, bias_row = g_ref[s : s + 1], b_ref[s : s + 1]

        def apply(at, sums):
            normed = (both_ref[at, :] - mean) * inv
            state, slope = gelu_parts(normed * gain_row + bias_row)
            out_ref[at, :] = (x_ref[at, :].astype(f32) + state).astype(bf16)
            q = slope * cot_ref[at, :].astype(f32)
            q_ref[at, :] = q
            return add_sums(sums, q, normed)

        emit_sums(sums_ref, sweep(cells, apply, pair(channels), step=32))

    outs = [shape((cells, channels), bf16), shape((cells, channels)), shape((width, 2, channels)), shape((2, channels))]
    return run(body, outs, (both, every, gain, bias, x, cot), "turn")


def grad_pre(q, both, mi, every, gain, s, expand_t, total):
    cells, channels = both.shape
    broad, half = expand_t.shape
    narrow = channels - broad

    def body(q_ref, both_ref, mi_ref, every_ref, g_ref, e_ref, *refs):
        low_ref, summed_ref, summed_low_ref, sums_ref = refs
        sums, bias_term, gain_term = back_terms(every_ref, total)
        sums_ref[...] = sums
        mean, inv = mi_ref[0:1], mi_ref[1:2]
        gain_row = g_ref[s : s + 1] * inv

        def apply(at, carry):
            normed = (both_ref[at, :] - mean) * inv
            low_ref[at, :] = (gain_row * (q_ref[at, :] - bias_term - normed * gain_term)).astype(bf16)
            return carry

        sweep(cells, apply, step=32)
        summed_ref[...] = dot(low_ref[:, narrow:], e_ref[...])
        summed_low_ref[...] = summed_ref[...].astype(bf16)

    outs = [shape((cells, channels), bf16), shape((cells, half)), shape((cells, half), bf16), shape((2, channels))]
    return run(body, outs, (q, both, mi, every, gain, expand_t), "grad_pre")


def spectrum_backward(table, own, others, mixed, mi, gain, bias, s, factor, scale, width):
    points, wide = mixed.shape
    cells, half = own.shape

    def body(t_ref, own_ref, others_ref, mixed_ref, mi_ref, g_ref, b_ref, factor_ref, *refs):
        q_ref, sums_ref, n_ref = refs
        mean, inv = mi_ref[0:1], mi_ref[1:2]
        gain_row, bias_row = g_ref[s : s + 1], b_ref[s : s + 1]
        for side in range(2):
            for at in blocks_of(points, 272):
                z = dot(t_ref[side, at, :cells], own_ref[...]) + dot(t_ref[side, at, cells:], others_ref[...])
                q_ref[at, side * half : (side + 1) * half] = z * (factor_ref[at, :] * scale)

        def apply(at, sums):
            normed = (mixed_ref[at, :] - mean) * inv
            q = gelu_parts(normed * gain_row + bias_row)[1] * q_ref[at, :]
            q_ref[at, :] = q
            n_ref[at, :] = normed
            return add_sums(sums, q, normed)

        emit_sums(sums_ref, sweep(points, apply, pair(wide)))

    outs = [shape((points, wide)), shape((width, 2, wide)), shape((points, wide))]
    return run(body, outs, (table, own, others, mixed, mi, gain, bias, factor), "spectrum_backward")


def norm_low(low_ref, q_ref, n_ref, mi_ref, gain_row, bias_term, gain_term):
    gain_row = gain_row * mi_ref[1:2]

    def apply(at, carry):
        low_ref[at, :] = (gain_row * (q_ref[at, :] - bias_term - n_ref[at, :] * gain_term)).astype(bf16)
        return carry

    sweep(q_ref.shape[0], apply)


def grad_mixed(q, normed, mi, every, gain, s, freq_kernel, place, totals):
    points, wide = q.shape

    def body(q_ref, n_ref, mi_ref, every_ref, g_ref, w_ref, place_ref, low_ref, back_ref, sums_ref):
        total = jnp.where(place_ref[0] == 0, float(totals[0]), float(totals[1]))
        sums, bias_term, gain_term = back_terms(every_ref, total)
        sums_ref[...] = sums
        norm_low(low_ref, q_ref, n_ref, mi_ref, g_ref[s : s + 1], bias_term, gain_term)
        back_ref[...] = dot_t(low_ref[...], w_ref[...]).astype(bf16)

    outs = [shape((points, wide), bf16), shape((points, wide), bf16), shape((2, wide))]
    return run(body, outs, (q, normed, mi, every, gain, freq_kernel, place), "grad_mixed", scalars=1)


def inverse_backward(table, own, others, summed, reduced, mi, gain, bias, s, scale, width):
    cells = table.shape[1]
    half = summed.shape[1]

    def body(t_ref, own_ref, others_ref, summed_ref, reduced_ref, mi_ref, g_ref, b_ref, *refs):
        q_ref, sums_ref, n_ref = refs
        mean, inv = mi_ref[0:1], mi_ref[1:2]
        gain_row, bias_row = g_ref[s : s + 1], b_ref[s : s + 1]
        freq = jnp.concatenate([own_ref[...], others_ref[...]], axis=0)
        real, imag = freq[:, :half], freq[:, half:]
        total = freq.shape[0]
        for at in blocks_of(cells, 256):
            back = dot(t_ref[0, at, :total], real) + dot(t_ref[1, at, :total], imag)
            q_ref[at, :] = summed_ref[at, :] + back * scale

        def apply(at, sums):
            normed = (reduced_ref[at, :] - mean) * inv
            q = gelu_parts(normed * gain_row + bias_row)[1] * q_ref[at, :]
            q_ref[at, :] = q
            n_ref[at, :] = normed
            return add_sums(sums, q, normed)

        emit_sums(sums_ref, sweep(cells, apply, pair(half)))

    outs = [shape((cells, half)), shape((width, 2, half)), shape((cells, half))]
    return run(body, outs, (table, own, others, summed, reduced, mi, gain, bias), "inverse_backward")


def grad_reduced(q, normed, mi, every, gain, s, reduce_kernel, total, conv_back, both, mi_3, gain_3, bias_3, width):
    cells, half = q.shape
    channels = both.shape[1]
    narrow = channels - reduce_kernel.shape[0]

    def body(q_ref, n_ref, mi_ref, every_ref, g_ref, r_ref, conv_ref, both_ref, mi3_ref, g3_ref, b3_ref, *refs):
        low_ref, out_ref, sums3_ref, sums_ref = refs
        sums, bias_term, gain_term = back_terms(every_ref, total)
        sums_ref[...] = sums
        norm_low(low_ref, q_ref, n_ref, mi_ref, g_ref[s : s + 1], bias_term, gain_term)
        out_ref[:, :narrow] = conv_ref[:, :narrow]
        for at in blocks_of(cells, 256):
            out_ref[at, narrow:] = conv_ref[at, narrow:] + dot_t(low_ref[at, :], r_ref[...])
        mean, inv = mi3_ref[0:1], mi3_ref[1:2]
        gain_row, bias_row = g3_ref[s - 1 : s], b3_ref[s - 1 : s]

        def apply(at, sums):
            normed_3 = (both_ref[at, :] - mean) * inv
            grad = gelu_parts(normed_3 * gain_row + bias_row)[1] * out_ref[at, :]
            out_ref[at, :] = grad
            return add_sums(sums, grad, normed_3)

        emit_sums(sums3_ref, sweep(cells, apply, pair(channels), step=32))

    outs = [shape((cells, half), bf16), shape((cells, channels)), shape((width, 2, channels)), shape((2, half))]
    ins = (q, normed, mi, every, gain, reduce_kernel, conv_back, both, mi_3, gain_3, bias_3)
    return run(body, outs, ins, "grad_reduced")


def grad_last(q, normed, mi, every, gain, s, total):
    cells, half = q.shape

    def body(q_ref, n_ref, mi_ref, every_ref, g_ref, *refs):
        low_ref, sums_ref = refs
        sums, bias_term, gain_term = back_terms(every_ref, total)
        sums_ref[...] = sums
        norm_low(low_ref, q_ref, n_ref, mi_ref, g_ref[s : s + 1], bias_term, gain_term)

    outs = [shape((cells, half), bf16), shape((2, half))]
    return run(body, outs, (q, normed, mi, every, gain), "grad_last")


def input_grad(cots, conv, late, reduce_kernel, place):
    channels = cots[0].shape[3]
    narrow = channels - reduce_kernel.shape[0]

    def body(cot0_ref, cot1_ref, *refs):
        conv_refs, late_refs, (r_ref, place_ref), out_refs = refs[:2], refs[2:4], refs[4:6], refs[6:]
        c = place_ref[1]
        for kind, (cot_ref, out_ref) in enumerate(zip((cot0_ref, cot1_ref), out_refs)):
            _, rows, cols, _ = cot_ref.shape
            half = cols // 2
            for side, core in enumerate((c, 1 - c)):
                at = pl.ds(pl.multiple_of(core * half, half), half)
                into = dot_t(late_refs[side][kind], r_ref[...]).reshape(rows, half, channels - narrow)
                base = conv_refs[side][kind].astype(f32).reshape(rows, half, channels) + cot_ref[0, :, at, :].astype(f32)
                out_ref[0, :, at, :narrow] = base[..., :narrow].astype(bf16)
                out_ref[0, :, at, narrow:] = (base[..., narrow:] + into).astype(bf16)

    outs = [shape(cot.shape, bf16) for cot in cots]
    ins = (*cots, *conv, *late, reduce_kernel, place)
    return run(body, outs, ins, "input_grad", limit=12, scalars=1)


def edge_cells(low, above, place, unit):
    cells, channels = low.shape
    blocks = cells // unit + 4

    def body(*refs):
        x_ref, place_ref, out_ref = refs[0], refs[-2], refs[-1]
        if above is None:
            zeros = jnp.zeros((2, channels), f32)
            ends = x_ref[...].astype(f32).reshape(blocks - 4, unit, channels)
            first = jnp.concatenate([zeros, ends[:, 0], zeros], axis=0)
            last = jnp.concatenate([zeros, ends[:, unit - 1], zeros], axis=0)
        else:
            wide = jnp.concatenate([refs[1][...], x_ref[...], refs[2][...]], axis=0)
            ends = wide.astype(f32).reshape(blocks, unit, channels)
            first, last = ends[:, 0], ends[:, unit - 1]
        land, left = place_ref[0] == 0, place_ref[1] == 0
        last = jnp.where(land, jnp.concatenate([last[1:], last[:1]], axis=0), last)
        first = jnp.where(land, jnp.concatenate([first[-1:], first[:-1]], axis=0), first)
        out_ref[...] = jnp.where(left, last, first).astype(bf16)

    ins = (low, place) if above is None else (low, *above, place)
    return run(body, [shape((blocks, channels), bf16)], ins, "edge_cells", scalars=1)[0]


def surroundings(low, place, unit):
    e_n = lax.axis_size("e")
    above = None
    if e_n > 1:
        ahead = [(e, e + 1) for e in range(e_n - 1)]
        above = (
            lax.ppermute(low[-2 * unit :], "e", ahead),
            lax.ppermute(low[: 2 * unit], "e", [(b, a) for a, b in ahead]),
        )
    beside = lax.ppermute(edge_cells(low, above, place, unit), "c", SWAP)
    return above, beside


def shifted_columns(x_ref, above_refs, beside_ref, land, left, out_ref, unit):
    cells, channels = x_ref.shape
    blocks = cells // unit + 4
    block = lax.broadcasted_iota(jnp.int32, (blocks, unit, 1), 0)
    cell = lax.broadcasted_iota(jnp.int32, (blocks, unit, 1), 1)
    for lane in range(0, channels, 128):
        at = slice(lane, lane + 128)
        if above_refs:
            top, bottom = above_refs[0][:, at], above_refs[1][:, at]
        else:
            top = bottom = jnp.zeros((2 * unit, 128), bf16)
        wide = jnp.concatenate([top, x_ref[:, at], bottom], axis=0)
        out_ref[1, :, at] = wide
        wide = wide.astype(f32)
        beside = beside_ref[:, at].astype(f32)[:, None, :]
        for j, edge, odd in ((0, 0, 0), (2, unit - 1, 1)):
            moved = pltpu.roll(wide, 1 if j == 0 else blocks * unit - 1, 0).reshape(blocks, unit, 128)
            outer_side = (cell == edge) & (jnp.logical_not(land) | (block % 2 == odd))
            fill = jnp.where(left if j == 2 else jnp.logical_not(left), beside, 0.0)
            out_ref[j, :, at] = jnp.where(outer_side, fill, moved).reshape(blocks * unit, 128).astype(bf16)


def rows_at(i, first, count, land, unit):
    if i == 1:
        return slice(2 * unit + first, 2 * unit + first + count)
    step = jnp.where(land, 2 * unit, unit)
    return pl.ds(pl.multiple_of(2 * unit + first + (i - 1) * step, unit), count)


def conv_forward(low, above, beside, place, unit, local_kernel, global_t):
    cells, channels = low.shape
    narrow = local_kernel.shape[1] // 9
    padded = cells + 4 * unit
    extra = () if above is None else above
    start = 4 + len(extra)

    def body(*refs):
        x_ref, beside_ref, l_ref, g_ref = refs[0], *refs[1 + len(extra) : 4 + len(extra)]
        place_ref, pre_ref, cols_ref, wide_ref = refs[start:]
        land, left = place_ref[0] == 0, place_ref[1] == 0
        shifted_columns(x_ref, refs[1 : 1 + len(extra)], beside_ref, land, left, wide_ref, unit)
        cols_ref[...] = wide_ref[:, :, :narrow]
        for at in blocks_of(cells, 512):
            count = at.stop - at.start
            local = jnp.zeros((count, narrow), f32)
            patches = []
            for t in range(9):
                block = wide_ref[t % 3, rows_at(t // 3, at.start, count, land, unit), :]
                local = local + dot(block, l_ref[:, t * narrow : (t + 1) * narrow])
                patches.append(block[:, :narrow])
            pre_ref[at, :narrow] = local
            pre_ref[at, narrow:] = dot_t(jnp.concatenate(patches, axis=1), g_ref[...])

    outs = [shape((cells, channels)), shape((3, padded, narrow), bf16)]
    ins = (low, *extra, beside, local_kernel, global_t, place)
    return run(body, outs, ins, "conv_forward", [pltpu.VMEM((3, padded, channels), bf16)], 12, 1)


def conv_backward(low, above, beside, place, unit, local_kernel, global_t, kind):
    cells, channels = low.shape
    narrow = local_kernel.shape[1] // 9
    padded = cells + 4 * unit
    extra = () if above is None else above
    start = 4 + len(extra)

    def body(*refs):
        x_ref, beside_ref, l_ref, g_ref = refs[0], *refs[1 + len(extra) : 4 + len(extra)]
        place_ref, grad_ref, patches_ref, wide_ref = refs[start:]
        land, left = place_ref[0] == 0, place_ref[1] == 0
        shifted_columns(x_ref, refs[1 : 1 + len(extra)], beside_ref, land, left, wide_ref, unit)
        for at in blocks_of(cells, 512):
            count = at.stop - at.start
            into = jnp.zeros((count, narrow), f32)
            for t in range(9):
                block = wide_ref[2 - t % 3, rows_at(2 - t // 3, at.start, count, land, unit), :]
                patches_ref[at, t * narrow : (t + 1) * narrow] = block[:, :narrow]
                into = into + dot(block[:, narrow:], g_ref[:, t * narrow : (t + 1) * narrow])
            grad = dot_t(patches_ref[at, :], l_ref[...])
            grad_ref[at, :narrow] = (grad[:, :narrow] + into).astype(kind)
            grad_ref[at, narrow:] = grad[:, narrow:].astype(kind)

    outs = [shape((cells, channels), kind), shape((cells, 9 * narrow), bf16)]
    ins = (low, *extra, beside, local_kernel, global_t, place)
    return run(body, outs, ins, "conv_backward", [pltpu.VMEM((3, padded, channels), bf16)], 12, 1)


def spaced(rows, own, pad):
    row = lax.broadcasted_iota(jnp.int32, (rows, rows // own * pad), 0)
    place = lax.broadcasted_iota(jnp.int32, (rows, rows // own * pad), 1)
    return jnp.where(place == row // own * pad + row % own, 1.0, 0.0).astype(bf16)


def copies(values, count):
    def body(in_ref, out_ref):
        for i in range(count):
            out_ref[i] = in_ref[...]

    return run(body, [shape((count,) + values.shape, values.dtype)], (values,), "copies")[0]


def unpack_small(blocks, own, half):
    pad, columns = blocks.shape[-2:]
    devices = math.prod(blocks.shape[:-2])
    wide = columns - 2 * half

    def body(full_ref, *out_refs):
        split_small(full_ref[...].reshape(devices * pad, columns), spaced(devices * own, own, pad), wide, half, out_refs)

    outs = [shape((devices * own, width), bf16) for width in (wide, half, half)]
    return run(body, outs, (blocks,), "unpack_small", limit=12)


def split_small(full, place, wide, half, out_refs):
    full = dot(place, full).astype(bf16)
    out_refs[0][...] = full[:, :wide]
    out_refs[1][...] = full[:, wide : wide + half]
    out_refs[2][...] = full[:, wide + half : wide + 2 * half]


def unpack_kernels(full, sections, own_in, pad_in, own_out, half):
    devices, rows, columns = full.shape
    pad = (rows - sections * pad_in) // (2 * sections - 1)
    plain = own_in == pad_in
    wide = devices * own_out
    each = pad_in + pad

    def body(full_ref, *refs):
        out_refs, small_refs = refs[: 2 * sections], refs[2 * sections : 5 * sections - 3]
        local_ref, global_ref, small_ref, sems = refs[5 * sections - 3 :]
        copies = []
        for s in range(sections):
            target = out_refs[2 * s] if plain else local_ref.at[s]
            sources = [(s * each, pad_in, target), (s * each + pad_in, pad, global_ref.at[s])]
            if s:
                sources.append((sections * each + (s - 1) * pad, pad, small_ref.at[s - 1]))
            for k, (first, count, target) in enumerate(sources):
                source = full_ref.at[:, pl.ds(first, count), :]
                copies.append(pltpu.make_async_copy(source, target, sems.at[s, k]))
        for copy in copies:
            copy.start()
        for copy in copies:
            copy.wait()
        place = spaced(devices * own_out, own_out, pad)
        for s in range(sections):
            if not plain:
                block = local_ref[s].reshape(devices * pad_in, columns)
                out_refs[2 * s][...] = dot(spaced(devices * own_in, own_in, pad_in), block).astype(bf16)
            out_refs[2 * s + 1][...] = dot(place, global_ref[s].reshape(devices * pad, columns)).astype(bf16)
            if s:
                block = small_ref[s - 1].reshape(devices * pad, columns)
                split_small(block, place, wide, half, small_refs[3 * s - 3 : 3 * s])

    local = (devices, pad_in, columns) if plain else (devices * own_in, columns)
    outs = [shape(dims, bf16) for dims in (local, (devices * own_out, columns))] * sections
    outs += [shape((devices * own_out, width), bf16) for width in (wide, half, half)] * (sections - 1)
    scratch = [
        pltpu.VMEM((8,) * 4 if plain else (sections, devices, pad_in, columns), bf16),
        pltpu.VMEM((sections, devices, pad, columns), bf16),
        pltpu.VMEM((max(sections - 1, 1), devices, pad, columns), bf16),
        pltpu.SemaphoreType.DMA((sections, 3)),
    ]
    limit = 14 if plain else 52
    out = run(body, outs, (InPlace(full),), "unpack_kernels", scratch, limit)
    kernels = [(out[2 * s].reshape(devices * own_in, columns), out[2 * s + 1]) for s in range(sections)]
    return kernels, out[2 * sections :]


def early_grads(x_low, patches, grad_low, shifted, summed, place, unit, own, pad, alike):
    cells, channels = x_low.shape
    narrow = shifted.shape[2]
    broad = channels - narrow
    half = summed.shape[1]
    wide = 9 * narrow

    def body(x_ref, p_ref, g_ref, s_ref, m_ref, place_ref, *out_refs):
        land = place_ref[0] == 0
        local_ref, other_ref, first = (out_refs[0], out_refs[0], wide) if alike else (*out_refs, 0)
        for i in range(3):
            at = slice(3 * i * narrow, 3 * (i + 1) * narrow)
            local_ref[:, at] = outer(x_ref[...], p_ref[:, at]).astype(bf16)
        grad = dot(g_ref[:, narrow:], spaced(broad, own, pad)).astype(bf16)
        for i in range(3):
            taps = [s_ref[j, rows_at(i, 0, cells, land, unit), :] for j in range(3)]
            at = slice(first + 3 * i * narrow, first + 3 * (i + 1) * narrow)
            other_ref[:, at] = outer(grad, jnp.concatenate(taps, axis=1)).astype(bf16)
        other_ref[:, first + wide :] = outer(grad, m_ref[...]).astype(bf16)

    padded = broad // own * pad
    if alike:
        outs = [shape((channels, 2 * wide + half), bf16)]
    else:
        outs = [shape((channels, wide), bf16), shape((padded, wide + half), bf16)]
    ins = (x_low, patches, grad_low, shifted, summed, place)
    return run(body, outs, ins, "early_grads", limit=12, scalars=1)


def late_grads(x_low, reduced_low, real, imag, mixed_low, own, pad):
    channels = x_low.shape[1]
    wide = mixed_low.shape[1]
    half = reduced_low.shape[1]
    narrow = channels - wide

    def body(x_ref, r_ref, real_ref, imag_ref, m_ref, out_ref):
        freq = jnp.concatenate([outer(real_ref[...], m_ref[...]), outer(imag_ref[...], m_ref[...])], axis=0)
        reduce = outer(x_ref[:, narrow:], r_ref[...])
        place = spaced(wide, own, pad)
        out_ref[:, :wide] = outer(place, freq.astype(bf16)).astype(bf16)
        out_ref[:, wide:] = outer(place, reduce.astype(bf16)).astype(bf16)

    outs = [shape((wide // own * pad, wide + half), bf16)]
    return run(body, outs, (x_low, reduced_low, real, imag, mixed_low), "late_grads")[0]


def core_parts(shares, here, g_n):
    parts = [part.reshape((g_n, 2, -1) + part.shape[1:]) for part in shares]
    rows, widths = parts[0].shape[2], [part.shape[3] for part in parts]
    starts = [sum(widths[:i]) for i in range(len(widths) + 1)]

    def body(*refs):
        c = refs[len(parts)][0]
        theirs_ref, mine_ref = refs[len(parts) + 1 :]
        for i, ref in enumerate(refs[: len(parts)]):
            at = slice(starts[i], starts[i + 1])
            for g in range(g_n):
                theirs_ref[g, :, at] = ref[g, 1 - c]
                mine_ref[g, :, at] = ref[g, c]

    outs = [shape((g_n, rows, starts[-1]), bf16)] * 2
    return run(body, outs, (*parts, here[2]), "core_parts", scalars=1)


def add_parts(mine, theirs, here):
    g_n = mine.shape[0]

    def body(mine_ref, theirs_ref, *refs):
        for step in range(g_n):
            g = refs[0][0] ^ step
            total = mine_ref[g].astype(f32) + theirs_ref[g].astype(f32)
            refs[1 + step][...] = total if step == 0 else total.astype(bf16)

    outs = [shape(mine.shape[1:], f32 if step == 0 else bf16) for step in range(g_n)]
    return run(body, outs, (mine, theirs, here[1]), "add_parts", scalars=1)


def add_plane(pieces, here, line_n):
    rows, columns = pieces[0].shape
    block = rows // line_n

    def body(*refs):
        for i in range(line_n):
            at = slice(i * block, (i + 1) * block)
            total = refs[0][at, :].astype(f32)
            for ref in refs[1:-1]:
                total = total + ref[at, :].astype(f32)
            refs[-1][i] = total.astype(bf16)

    return run(body, [shape((line_n, block, columns), bf16)], pieces, "add_plane")[0]


def halved(keep, got, index, count, last):
    entries, rows, columns = keep.shape
    if count:
        entries, rows = count, entries * rows // count
        keep, got = (item.reshape(count, rows, columns) for item in (keep, got))

    def body(keep_ref, got_ref, index_ref, *out_refs):
        for step in range(entries):
            at = index_ref[0] ^ step if count else step
            total = keep_ref[at].astype(f32) + got_ref[at].astype(f32)
            if last:
                out_refs[0][...] = total
            elif step < entries // 2:
                out_refs[0][step] = total
            else:
                out_refs[1][step - entries // 2] = total.astype(bf16)

    if last:
        outs = [shape((rows, columns))]
    else:
        outs = [shape((entries // 2, rows, columns)), shape((entries // 2, rows, columns), bf16)]
    return run(body, outs, (keep, got, index), "halved", scalars=1)


def owned_by_halves(shares, here):
    g_n = lax.axis_size("g")
    line = ("k", "z", "e")
    line_n = lax.axis_size(line)
    theirs, keep = core_parts(shares, here, g_n)
    got = lax.ppermute(theirs, "c", SWAP)
    yield
    for axes, index, count in (("g", here[1], g_n), (line, here[0], line_n)):
        first, bit = True, count // 2
        while bit:
            keep, send = halved(keep, got, index, count if first else 0, False)
            got = partners(send, axes, bit)
            yield
            first, bit = False, bit // 2
    return halved(keep, got, here[0], 0, True)[0]


def owned(shares, here):
    g_n = lax.axis_size("g")
    line = ("k", "z", "e")
    line_n = lax.axis_size(line)
    theirs, mine = core_parts(shares, here, g_n)
    theirs = lax.ppermute(theirs, "c", SWAP)
    yield
    pieces = over_plane(add_parts(mine, theirs, here))
    yield
    sums = lax.all_to_all(add_plane(pieces, here, line_n), line, 0, 0, tiled=True)
    yield
    return total_of(sums)


def owned_apart(shares):
    for axes in (("g", "c"), ("k", "z", "e")):
        count = lax.axis_size(axes)
        shares = lax.psum_scatter(shares.reshape(count, -1, shares.shape[-1]), axes, scatter_dimension=0, tiled=True)
    return shares.reshape(-1, shares.shape[-1])


def total_of(blocks):
    def body(in_ref, out_ref):
        total = in_ref[0].astype(f32)
        for i in range(1, blocks.shape[0]):
            total = total + in_ref[i].astype(f32)
        out_ref[...] = total

    return run(body, [shape(blocks.shape[1:])], (blocks,), "total_of")[0]


def pack_sums(sums):
    widths = [item.shape[1] for item in sums]

    def body(*refs):
        refs[-1][...] = jnp.concatenate([ref[...] for ref in refs[:-1]], axis=1)

    return run(body, [shape((2, sum(widths)))], sums, "pack_sums")[0]


def results(totals, sums, other_sums, own_in, own_out, narrow, half, channels, alike):
    sections = len(totals)
    wides = (9 * narrow, 9 * narrow + half, 3 * half)
    flat, where = [], {}
    for s in range(sections):
        parts = [[(0, s), (1, s)]] if alike else [[(0, s)], [(1, s)]]
        if s == 0 and sections > 1:
            parts = [parts[0] + [(2, 1)]] if alike else parts + [[(2, 1)]]
        if s != 1:
            parts = parts + [[(2, s)]]
        assert len(parts) == len(totals[s])
        for group, item in zip(parts, totals[s]):
            start = 0
            for part in group:
                where[part] = (len(flat), start)
                start += wides[part[0]]
            flat.append(item)

    def body(*refs):
        sums_ref, other_ref, local_ref, global_ref, reduce_ref, freq_ref, expand_ref, *norm_refs = refs[len(flat) :]
        for s in range(sections):

            def columns(part, start, count, rows):
                index, first = where[part, s]
                return refs[index][:rows, first + start : first + start + count].astype(f32)

            for t in range(9):
                local_ref[s, t] = columns(0, t * narrow, narrow, own_in)
                global_ref[t, :, s, :] = columns(1, t * narrow, narrow, own_out)
            expand_ref[:, s, :] = columns(1, 9 * narrow, half, own_out)
            freq_ref[:, s, :] = columns(2, 0, 2 * half, own_out)
            reduce_ref[:, s, :] = columns(2, 2 * half, half, own_out)
        both = sums_ref[...] + other_ref[...]
        at = 0
        for s in range(sections):
            for index, wide in enumerate((half, 2 * half, channels)):
                norm_refs[2 * index][s : s + 1, :] = both[1:2, at : at + wide]
                norm_refs[2 * index + 1][s : s + 1, :] = both[0:1, at : at + wide]
                at += wide

    outs = [
        shape((sections, 9, own_in, narrow)),
        shape((9, own_out, sections, narrow)),
        shape((own_out, sections, half)),
        shape((own_out, sections, 2 * half)),
        shape((own_out, sections, half)),
    ]
    outs += [shape((sections, wide)) for wide in (half, half, 2 * half, 2 * half, channels, channels)]
    out = run(body, outs, (*flat, sums, other_sums), "results")
    return (
        out[0],
        jnp.transpose(out[1], (2, 0, 3, 1)),
        jnp.transpose(out[2], (1, 0, 2)),
        jnp.transpose(out[3], (1, 0, 2)),
        jnp.transpose(out[4], (1, 2, 0)),
        *out[5:],
    )


def pick_tables(table, factors, variant, size):
    points, cells = factors.shape[1], size // lax.axis_size(PART)
    columns = -(-points * lax.axis_size(PART) // 128) * 128

    def body(table_ref, factor_ref, v_ref, forward_ref, inverse_ref, out_ref, sems):
        v = v_ref[0]
        copies = []
        for side in range(2):
            source = table_ref.at[v, pl.ds(side * points, points), pl.ds(0, size)]
            copies.append(pltpu.make_async_copy(source, forward_ref.at[side], sems.at[0, side]))
            source = table_ref.at[v, pl.ds(2 * points + side * cells, cells), pl.ds(0, columns)]
            copies.append(pltpu.make_async_copy(source, inverse_ref.at[side], sems.at[1, side]))
        for copy in copies:
            copy.start()
        out_ref[...] = factor_ref[v]
        for copy in copies:
            copy.wait()

    outs = [shape((2, points, size), bf16), shape((2, cells, columns), bf16), shape(factors.shape[1:])]
    ins = (InPlace(table), factors, variant)
    return run(body, outs, ins, "pick_tables", [pltpu.SemaphoreType.DMA((2, 2))], 12, 1)


def per_device(plan, *args):
    (
        land,
        port,
        to_local,
        to_global,
        reduce_weight,
        freq_weight,
        expand_weight,
        spec_gain,
        spec_bias,
        freq_gain,
        freq_bias,
        out_gain,
        out_bias,
        cot_land,
        cot_port,
    ) = args
    rounds, table, weight_table, point_counts = plan
    sections = to_local.shape[0]
    devices = lax.axis_size(ALL)
    own_in = to_local.shape[2]
    own_out = to_global.shape[3]
    pad = -(-own_out // 16) * 16
    narrow = to_local.shape[3]
    channels = own_in * devices
    half = reduce_weight.shape[2]
    unit = port.shape[2] // 2
    k, c, part = lax.axis_index("k"), lax.axis_index("c"), lax.axis_index(PART)
    line_here = lax.axis_index(("k", "z", "e"))
    place = jnp.stack([k, c, line_here]).astype(jnp.int32)
    here = tuple(index.astype(jnp.int32).reshape(1) for index in (line_here, lax.axis_index("g"), c))
    variant = k * lax.axis_size(PART) + part
    g_n, z_n, e_n = lax.axis_size("g"), lax.axis_size("z"), lax.axis_size("e")
    width = lax.axis_size(KIND)

    pad_in = -(-own_in // 16) * 16
    Order.last = ()

    grow = ((0, 0), (0, pad - own_out), (0, 0))
    taps_local = jnp.transpose(to_local, (0, 2, 1, 3)).reshape(sections, own_in, 9 * narrow)
    taps_local = jnp.pad(taps_local, ((0, 0), (0, pad_in - own_in), (0, 0)))
    taps_global = jnp.pad(jnp.transpose(to_global, (0, 3, 1, 2)).reshape(sections, own_out, 9 * narrow), grow)
    packed = jnp.concatenate([freq_weight, reduce_weight, jnp.transpose(expand_weight, (0, 2, 1))], axis=2)
    packed = jnp.pad(packed, grow)
    small = copies(packed[0], lax.axis_size(("k", "z", "e")))
    small = lax.all_to_all(small, ("k", "z", "e"), 0, 0, tiled=True)
    later = jnp.pad(packed[1:], ((0, 0), (0, 0), (0, 9 * narrow - packed.shape[2])))
    taps = jnp.concatenate([taps_local, taps_global], axis=1)
    taps = jnp.concatenate([item.reshape(-1, 9 * narrow) for item in (taps, later)], axis=0)
    taps = lax.all_gather(taps, ALL)
    x_steps = to_tile(land, port, rounds, place, here)
    advance(x_steps)
    advance(x_steps)
    small = copies(small, lax.axis_size(("g", "c")))
    small = lax.all_to_all(small, ("g", "c"), 0, 0, tiled=True)
    variant = variant.reshape(1)
    size = land.shape[1] * land.shape[2] * lax.axis_size(("k", "z", "e"))
    forward, inverse, factor = pick_tables(jnp.asarray(table), jnp.asarray(weight_table)[..., None], variant, size)
    small = unpack_small(small, own_out, half)
    x = finish(x_steps)

    cells = x.shape[0]
    scale = 1.0 / math.sqrt(size)
    cell_total = float(g_n * z_n * size)
    point_totals = [int(item.sum()) * g_n * z_n for item in point_counts]

    def exchange(stats):
        every = lax.all_to_all(stats, KIND, 0, 0, tiled=True)
        Order.last = (every,)
        return every

    kept = []
    for s in range(sections):
        freq_kernel, reduce_kernel, expand_t = small[3 * s : 3 * s + 3]
        if s == 0:
            low = x
            reduced, stats = reduce_first(x, reduce_kernel, width, narrow)
        else:
            low, reduced, stats, kept[-1]["mi_3"] = reduce_next(both, every, out_gain, out_bias, s - 1, reduce_kernel, narrow)
        every = exchange(stats)
        if s == 1:
            gate(every)
            cot = finish(cot_steps)
        if s == 0:
            cot_steps = to_tile(cot_land, cot_port, rounds, place, here)
            advance(cot_steps)
        else:
            above, beside = surroundings(low, place, unit)
        hidden_low, hidden, mi_1 = hidden_act(reduced, every, spec_gain, spec_bias, s)
        others = shared(hidden_low)
        if s > 0:
            pre, shifted = conv_forward(low, above, beside, place, unit, *kernels[s])
        real, imag, mixed, stats = spectrum_forward(forward, hidden_low, others, freq_kernel, factor, scale, width)
        every = exchange(stats)
        if s == 0:
            above, beside = surroundings(low, place, unit)
            kernels, more = unpack_kernels(taps, sections, own_in, pad_in, own_out, half)
            small = [*small, *more]
            hold(beside)
        freq_low, mi_2 = freq_act(mixed, every, freq_gain, freq_bias, s, factor, place, point_counts, e_n, z_n)
        others = shared(freq_low)
        if s == 0:
            pre, shifted = conv_forward(low, above, beside, place, unit, *kernels[s])
            advance(cot_steps)
        summed, both, stats = inverse_forward(inverse, freq_low, others, hidden, pre, expand_t, scale, width)
        every = exchange(stats)
        kept.append(
            dict(low=low, shifted=shifted, reduced=reduced, mi_1=mi_1, real=real, imag=imag, mixed=mixed, mi_2=mi_2, summed=summed, both=both)
        )
    if sections == 1:
        cot = finish(cot_steps)
    out, q_3, sums, kept[-1]["mi_3"] = turn(both, every, out_gain, out_bias, sections - 1, x, cot)

    alike = own_in == pad
    norm_sums = [None] * sections
    totals = [None] * sections
    last_steps = None
    for s in reversed(range(sections)):
        freq_kernel, reduce_kernel, expand_t = small[3 * s : 3 * s + 3]
        item = kept[s]
        every = exchange(sums)
        if s == sections - 2:
            gate(every)
            out_parts = finish(out_steps)
        low, summed, summed_low, sums_3 = grad_pre(
            q_3, item["both"], item["mi_3"], every, out_gain, s, expand_t, cell_total
        )
        others = shared(summed_low)
        above, beside = surroundings(low, place, unit)

        def kernel_grads():
            return early_grads(
                item["low"], patches, low, item["shifted"], item["summed"], place, unit, own_out, pad, alike
            )

        if s == 0:
            if sections > 1:
                hold(out_parts[1])
            conv_back, patches = conv_backward(low, above, beside, place, unit, *kernels[s], f32 if s > 0 else bf16)
            conv_steps = from_tile(conv_back, rounds, place, here)
            advance(conv_steps)
            grads = kernel_grads()
            if sections > 1:
                grads = (*grads, late_grads(kept[1]["low"], reduced_low, kept[1]["real"], kept[1]["imag"], mixed_low, own_out, pad))
        else:
            hold(beside)
        q, sums, normed = spectrum_backward(
            forward, summed_low, others, item["mixed"], item["mi_2"], freq_gain, freq_bias, s, factor, scale, width
        )
        every = exchange(sums)
        if s == 0:
            gate(every)
            conv_parts = finish(conv_steps)
            if alike:
                last_steps = [owned(grads, here)]
            else:
                last_steps = [owned((grad,), here) for grad in grads]
            for steps in last_steps:
                advance(steps)
        mixed_low, back, sums_2 = grad_mixed(
            q, normed, item["mi_2"], every, freq_gain, s, freq_kernel, place, point_totals
        )
        others = shared(back)
        if s > 0:
            conv_back, patches = conv_backward(low, above, beside, place, unit, *kernels[s], f32 if s > 0 else bf16)
            grads = kernel_grads()
            totals[s] = [owned_apart(grad) for grad in grads]
        else:
            hold(conv_parts[1])
            for steps in last_steps:
                advance(steps)
        if s == sections - 1:
            out_steps = from_tile(out, rounds, place, here)
            advance(out_steps)
        q, sums, normed = inverse_backward(
            inverse, back, others, summed, item["reduced"], item["mi_1"], spec_gain, spec_bias, s, scale, width
        )
        every = exchange(sums)
        if s > 0:
            below = kept[s - 1]
            reduced_low, q_3, sums, sums_1 = grad_reduced(
                q, normed, item["mi_1"], every, spec_gain, s, reduce_kernel, cell_total,
                conv_back, below["both"], below["mi_3"], out_gain, out_bias, width,
            )
            if s > 1:
                totals[s].append(owned_apart(late_grads(item["low"], reduced_low, item["real"], item["imag"], mixed_low, own_out, pad)))
        else:
            if sections > 1:
                hold(*totals[1])
            reduced_low, sums_1 = grad_last(q, normed, item["mi_1"], every, spec_gain, s, cell_total)
        norm_sums[s] = (sums_1, sums_2, sums_3)

    if sections == 1:
        out_parts = finish(out_steps)
    end_steps = from_tile(reduced_low, rounds, place, here)
    advance(end_steps)
    late_grad = late_grads(kept[0]["low"], reduced_low, kept[0]["real"], kept[0]["imag"], mixed_low, own_out, pad)
    late_steps = owned_by_halves((late_grad,), here)
    advance(late_steps)
    for steps in last_steps:
        advance(steps)
    advance(late_steps)
    packed_sums = pack_sums([item for s in range(sections) for item in norm_sums[s]])
    other_sums = lax.ppermute(packed_sums, "k", SWAP)
    land_out, port_out = join_halves(*out_parts, (land, port), place)
    advance(late_steps)
    end_parts = finish(end_steps)
    advance(late_steps)
    last_totals = [finish(steps) for steps in last_steps]
    advance(late_steps)
    land_grad, port_grad = input_grad((cot_land, cot_port), conv_parts, end_parts, small[1], place)
    totals[0] = last_totals + [finish(late_steps)]
    rest = results(totals, packed_sums, other_sums, own_in, own_out, narrow, half, channels, alike)
    return (land_out, port_out, land_grad, port_grad, *rest)


def solution(mesh):
    f_n, s_n = mesh.shape["fsdp"], mesh.shape["sp"]
    e_n = s_n // 4
    fine = Mesh(np.asarray(mesh.devices).reshape(f_n // 2, 2, 2, 2, e_n), ALL)
    maps = P(("g", "c"), ("k", "z", "e"), None, None)
    split = ALL

    def whole(*args):
        land, port = args[0], args[1]
        plan = (
            routes(e_n),
            *transform_tables(e_n, land.shape[1:3], port.shape[1:3]),
        )
        weights = (
            P(None, None, split, None),
            P(None, None, None, split),
            P(None, split, None),
            P(None, split, None),
            P(None, None, split),
        )
        return jax.shard_map(
            lambda *local: per_device(plan, *local),
            mesh=fine,
            in_specs=(maps, maps, *weights, P(), P(), P(), P(), P(), P(), maps, maps),
            out_specs=(maps, maps, maps, maps, *weights, P(), P(), P(), P(), P(), P()),
            check_vma=False,
        )(*args)

    return whole
```

```python
import math

import jax
import jax.numpy as jnp
import numpy as np
from jax import lax
from jax.experimental import pallas as pl
from jax.experimental.pallas import tpu as pltpu
from jax.sharding import Mesh, PartitionSpec as P

EPS = 1e-05
LINE = ("c", "k", "z", "e")
KIND = ("g", "c", "z", "e")
PART = ("c", "e")
ALL = ("g", "c", "k", "z", "e")
f32 = jnp.float32
bf16 = jnp.bfloat16


def routes(e_n):
    s_n = 4 * e_n
    count = 2 * s_n
    left = []
    for c in range(2):
        for s in range(s_n):
            for unit in range(4):
                kind, half = unit // 2, unit % 2
                left.append((c * s_n + s, unit, half * s_n + (kind * 2 + c) * e_n + s // 4, s % 4))
    rounds = []
    for _ in range(4):
        owner = {}

        def augment(src, seen):
            for edge in left:
                if edge[0] == src and edge[2] not in seen:
                    seen.add(edge[2])
                    if edge[2] not in owner or augment(owner[edge[2]][0], seen):
                        owner[edge[2]] = edge
                        return True
            return False

        for src in range(count):
            assert augment(src, set())
        chosen = list(owner.values())
        for edge in chosen:
            left.remove(edge)
        sent = np.zeros(count, np.int32)
        slot = np.zeros(count, np.int32)
        for edge in chosen:
            sent[edge[0]] = edge[1]
            slot[edge[2]] = edge[3]
        rounds.append(([(edge[0], edge[2]) for edge in chosen], sent, slot))
    return rounds


def transform_tables(e_n, land_shape, port_shape):
    parts = 2 * e_n
    shapes = (land_shape, port_shape)
    most = max(rows * (cols // 2 + 1) for rows, cols in shapes)
    per_part = -(-most // (16 * parts)) * 16
    forward, inverse, weight, counts = [], [], [], []
    for rows, cols in shapes:
        half = cols // 2 + 1
        point = np.arange(per_part * parts)
        valid = point < rows * half
        kr, f = point // half, point % half
        tiles = []
        for part in range(parts):
            c, e = part // e_n, part % e_n
            h = np.arange(rows // e_n) + e * (rows // e_n)
            w = np.arange(cols // 2) + c * (cols // 2)
            tiles.append((np.repeat(h, len(w)), np.tile(w, len(h))))
        cell_h = np.concatenate([tile[0] for tile in tiles])
        cell_w = np.concatenate([tile[1] for tile in tiles])
        size = rows * cols
        phase = (kr[:, None] * cell_h[None, :] * cols + f[:, None] * cell_w[None, :] * rows) % size
        angle = phase * (2.0 * math.pi / size)
        table = np.stack([np.cos(angle), -np.sin(angle)]) * valid[None, :, None]
        table = table.astype(np.float32).astype(jnp.bfloat16)
        cells = size // parts
        factor = np.where((f == 0) | (2 * f == cols), 1.0, 2.0) * valid
        counts.append([int(valid[p * per_part : (p + 1) * per_part].sum()) for p in range(parts)])
        for part in range(parts):
            order = [(part + step) % parts for step in range(parts)]
            own_points = slice(part * per_part, (part + 1) * per_part)
            own_cells = slice(part * cells, (part + 1) * cells)
            forward.append(
                np.concatenate([table[:, own_points, q * cells : (q + 1) * cells] for q in order], axis=2)
            )
            back = np.concatenate([table[:, q * per_part : (q + 1) * per_part, own_cells] for q in order], axis=1)
            inverse.append(np.ascontiguousarray(back.transpose(0, 2, 1)))
            weight.append(factor[own_points].astype(np.float32))
    forward, inverse = (np.stack(item).reshape(len(item), -1, item[0].shape[2]) for item in (forward, inverse))
    wide = max(-(-forward.shape[2] // 128), -(-inverse.shape[2] // 128)) * 128
    forward, inverse = (np.pad(item, ((0, 0), (0, 0), (0, wide - item.shape[2]))) for item in (forward, inverse))
    return np.concatenate([forward, inverse], axis=1), np.stack(weight), np.asarray(counts, np.int32)


SWAP = [(0, 1), (1, 0)]


def pick(table, index):
    return lax.dynamic_index_in_dim(jnp.asarray(table), index, 0, keepdims=False)


def partners(pieces, axes, step):
    count = lax.axis_size(axes)
    return lax.ppermute(pieces, axes, [(i, i ^ step) for i in range(count)])


def split_halves(land, port, place):
    channels = land.shape[3]
    shapes = [maps.shape[1:3] for maps in (land, port)]
    cells = shapes[0][0] * shapes[0][1] // 2

    def body(land_ref, port_ref, place_ref, mine_ref, theirs_ref):
        c = place_ref[1]
        for kind, ref in enumerate((land_ref, port_ref)):
            half = shapes[kind][1] // 2
            for out_ref, core in ((mine_ref, c), (theirs_ref, 1 - c)):
                at = pl.ds(pl.multiple_of(core * half, half), half)
                out_ref[kind] = ref[0, :, at, :].reshape(cells, channels)

    outs = [shape((2, cells, channels), land.dtype)] * 2
    return run(body, outs, (land, port, place), "split_halves", scalars=1)


def join_halves(mine, theirs, like, place):
    def body(mine_ref, theirs_ref, place_ref, *out_refs):
        c = place_ref[1]
        for kind, out_ref in enumerate(out_refs):
            _, rows, cols, channels = out_ref.shape
            half = cols // 2
            for ref, core in ((mine_ref, c), (theirs_ref, 1 - c)):
                at = pl.ds(pl.multiple_of(core * half, half), half)
                out_ref[0, :, at, :] = ref[kind].reshape(rows, half, channels)

    return run(body, [shape(maps.shape, maps.dtype) for maps in like], (mine, theirs, place), "join_halves", scalars=1)


def to_slots(mine, theirs, place):
    def body(mine_ref, theirs_ref, place_ref, *out_refs):
        here, c = place_ref[2], place_ref[1]
        for step, out_ref in enumerate(out_refs):
            there = here ^ step
            kind, core = there // 2, there % 2

            @pl.when(core == c)
            def _():
                out_ref[...] = mine_ref[kind]

            @pl.when(core != c)
            def _():
                out_ref[...] = theirs_ref[kind]

    outs = [shape(mine.shape[1:], mine.dtype)] * 4
    return run(body, outs, (mine, theirs, place), "to_slots", scalars=1)


def from_slots(pieces, place):
    def body(*refs):
        place_ref, mine_ref, theirs_ref = refs[-3:]
        here, c = place_ref[2], place_ref[1]
        for step in range(4):
            there = here ^ step
            kind, core = there // 2, there % 2

            @pl.when(core == c)
            def _():
                mine_ref[kind] = refs[step][...]

            @pl.when(core != c)
            def _():
                theirs_ref[kind] = refs[step][...]

    outs = [shape((2,) + pieces[0].shape, pieces[0].dtype)] * 2
    return run(body, outs, (*pieces, place), "from_slots", scalars=1)


def from_line(blocks, place):
    def body(blocks_ref, place_ref, mine_ref, theirs_ref):
        c = place_ref[1]
        for kind in range(2):
            mine_ref[kind] = blocks_ref[2 * kind + c]
            theirs_ref[kind] = blocks_ref[2 * kind + 1 - c]

    outs = [shape((2,) + blocks.shape[1:], blocks.dtype)] * 2
    return run(body, outs, (blocks, place), "from_line", scalars=1)


def in_order(pieces, here):
    rows = pieces[0].shape[0]

    def body(*refs):
        here_ref, out_ref = refs[-2:]
        for step in range(len(pieces)):
            out_ref[here_ref[0] ^ step] = refs[step][...]

    outs = [shape((len(pieces),) + pieces[0].shape, pieces[0].dtype)]
    out = run(body, outs, (*pieces, here), "in_order", scalars=1)[0]
    return out.reshape((len(pieces) * rows,) + pieces[0].shape[1:])


def for_partners(blocks, here):
    count = blocks.shape[0]

    def body(blocks_ref, here_ref, *out_refs):
        for step in range(count):
            out_refs[step][...] = blocks_ref[here_ref[0] ^ step]

    outs = [shape(blocks.shape[1:], blocks.dtype)] * count
    return run(body, outs, (blocks, here), "for_partners", scalars=1)


def advance(steps):
    return next(steps)


def finish(steps):
    while True:
        try:
            next(steps)
        except StopIteration as stop:
            return stop.value


def over_line(pieces):
    axes = ("k", "z", "e")
    return [pieces[0]] + [partners(pieces[step], axes, step) for step in range(1, lax.axis_size(axes))]


def over_plane(pieces):
    return [pieces[0]] + [partners(pieces[step], "g", step) for step in range(1, lax.axis_size("g"))]


def to_tile(land, port, rounds, place, here):
    channels = land.shape[3]
    if lax.axis_size("e") == 1:
        mine, theirs = split_halves(land, port, place)
        theirs = lax.ppermute(theirs, "c", SWAP)
        yield
        pieces = over_line(to_slots(mine, theirs, place))
        yield
        return in_order(pieces, here[0])
    me = lax.axis_index(LINE)
    units = []
    for maps in (land, port):
        cols = maps.shape[2] // 2
        units += [maps[0, :, :cols].reshape(-1, channels), maps[0, :, cols:].reshape(-1, channels)]
    units = jnp.stack(units)
    got = [lax.ppermute(pick(units, pick(sent, me)), LINE, pairs) for pairs, sent, _ in rounds]
    yield
    slots = np.stack([slot for _, _, slot in rounds], axis=1)
    order = pick(np.argsort(slots, axis=1).astype(np.int32), me)
    yield
    return jnp.concatenate([pick(jnp.stack(got), order[i]) for i in range(4)], axis=0)


def from_tile(tile, rounds, place, here):
    units = tile.reshape(4, -1, tile.shape[1])
    if lax.axis_size("e") == 1:
        pieces = over_line(for_partners(units, here[0]))
        yield
        mine, theirs = from_slots(pieces, place)
        return mine, lax.ppermute(theirs, "c", SWAP)
    me = lax.axis_index(LINE)
    got = [lax.ppermute(pick(units, pick(slot, me)), LINE, [(b, a) for a, b in pairs]) for pairs, _, slot in rounds]
    yield
    sents = np.stack([sent for _, sent, _ in rounds], axis=1)
    order = pick(np.argsort(sents, axis=1).astype(np.int32), me)
    both = jnp.stack([pick(jnp.stack(got), order[i]) for i in range(4)]).reshape((2, 2) + units.shape[1:])
    c = lax.axis_index("c")
    return (
        lax.dynamic_index_in_dim(both, c, 1, keepdims=False),
        lax.dynamic_index_in_dim(both, 1 - c, 1, keepdims=False),
    )


def shared(block):
    parts = lax.axis_size(PART)
    pieces = [
        lax.ppermute(block, PART, [((p + step) % parts, p) for p in range(parts)]) for step in range(1, parts)
    ]
    return pieces[0] if parts == 2 else jnp.concatenate(pieces, axis=0)


def gelu_parts(v):
    k = math.sqrt(2.0 / math.pi)
    square = v * v
    t = jnp.tanh(k * v * (1.0 + 0.044715 * square))
    half = 0.5 * (1.0 + t)
    return v * half, half + 0.5 * v * (1.0 - t * t) * (k * (1.0 + 3.0 * 0.044715 * square))


def gelu(v):
    return 0.5 * v * (1.0 + jnp.tanh(math.sqrt(2.0 / math.pi) * v * (1.0 + 0.044715 * (v * v))))


def dot(a, b):
    return lax.dot_general(a, b, (((1,), (0,)), ((), ())), preferred_element_type=f32)


def dot_t(a, b):
    return lax.dot_general(a, b, (((1,), (1,)), ((), ())), preferred_element_type=f32)


def outer(a, b):
    return lax.dot_general(a, b, (((0,), (0,)), ((), ())), preferred_element_type=f32)


def device_counts(counts, kind, width, e_n, z_n):
    row = lax.broadcasted_iota(jnp.int32, (width, 1), 0)
    part = row // (e_n * z_n) % 2 * e_n + row % e_n
    out = jnp.zeros((width, 1), f32)
    for p in range(len(counts[0])):
        out = jnp.where(part == p, jnp.where(kind == 0, float(counts[0][p]), float(counts[1][p])), out)
    return out


def moments(every, counts, total):
    sums, squares = every[:, 0, :], every[:, 1, :]
    mean = jnp.sum(sums, axis=0, keepdims=True) / total
    apart = sums / counts - mean
    square = jnp.sum(squares + counts * apart * apart, axis=0, keepdims=True)
    return mean, lax.rsqrt(square / total + EPS)


def emit(out_ref, first, second):
    both = jnp.concatenate([first, second], axis=0)
    out_ref[...] = jnp.broadcast_to(both[None], out_ref.shape)


def row_step(rows):
    return next(step for step in (64, 32, 16, 8) if rows % step == 0)


def sweep(rows, body, carry=0, step=None):
    step = step or row_step(rows)
    if rows == step:
        return body(slice(0, rows), carry)
    return lax.fori_loop(0, rows // step, lambda i, carry: body(pl.ds(pl.multiple_of(i * step, step), step), carry), carry)


def folded(values):
    return jnp.sum(values.reshape(values.shape[0] // 8, 8, values.shape[1]), axis=0)


def column(values):
    return jnp.sum(values, axis=0, keepdims=True)


def lanes_of(values, columns):
    return jnp.concatenate([values] * (columns // 128), axis=1)


def emit_moments(out_ref, ref, count, factor_ref=None):
    rows, columns = ref.shape
    zero = jnp.zeros((8, columns), f32)
    local_sum = column(sweep(rows, lambda at, acc: acc + folded(ref[at, :]), zero))
    mean = local_sum / count

    def squares(at, acc):
        centered = ref[at, :] - mean
        if factor_ref is not None:
            centered = jnp.where(lanes_of(factor_ref[at, :], columns) > 0.0, centered, 0.0)
        return acc + folded(centered * centered)

    emit(out_ref, local_sum, column(sweep(rows, squares, zero)))


def pair(columns):
    return jnp.zeros((8, columns), f32), jnp.zeros((8, columns), f32)


def add_sums(sums, q, normed):
    return sums[0] + folded(q), sums[1] + folded(q * normed)


def emit_sums(out_ref, sums):
    emit(out_ref, column(sums[0]), column(sums[1]))


def back_terms(every_ref, total):
    sums = jnp.sum(every_ref[...], axis=0)
    return sums, sums[0:1] / total, sums[1:2] / total


VMEM = pl.BlockSpec(memory_space=pltpu.VMEM)
SMEM = pl.BlockSpec(memory_space=pltpu.SMEM)
ANY = pl.BlockSpec(memory_space=pl.ANY)
HBM = pl.BlockSpec(memory_space=pltpu.HBM)


class Order:
    last = ()


def run(body, outs, ins, name, scratch=(), limit=8, scalars=0):
    vectors = len(ins) - scalars
    waits = len(Order.last)

    def ordered(*refs):
        body(*refs[:vectors], *refs[vectors + waits :])

    result = pl.pallas_call(
        ordered,
        out_shape=outs,
        in_specs=[HBM if item is None else VMEM for item in _spaces(ins[:vectors])] + [ANY] * waits + [SMEM] * scalars,
        out_specs=[VMEM] * len(outs),
        scratch_shapes=list(scratch),
        compiler_params=pltpu.CompilerParams(vmem_limit_bytes=limit * 1024 * 1024),
        name=name,
    )(*[item.array if isinstance(item, InPlace) else item for item in ins[:vectors]], *Order.last, *ins[vectors:])
    Order.last = (min(result, key=lambda item: math.prod(item.shape)),)
    return result


def hold(*arrays):
    Order.last = (*Order.last, *arrays)


def gate(every):
    def body(in_ref, out_ref):
        out_ref[...] = in_ref[0]

    run(body, [shape(every.shape[1:])], (every,), "gate")


class InPlace:
    def __init__(self, array):
        self.array = array


def _spaces(items):
    return [None if isinstance(item, InPlace) else item for item in items]


def shape(dims, kind=f32):
    return jax.ShapeDtypeStruct(tuple(dims), kind)


def reduce_first(x, reduce_kernel, width, narrow):
    cells = x.shape[0]
    half = reduce_kernel.shape[1]

    def body(x_ref, r_ref, reduced_ref, stats_ref):
        reduced_ref[...] = dot(x_ref[:, narrow:], r_ref[...])
        emit_moments(stats_ref, reduced_ref, float(cells))

    return run(body, [shape((cells, half)), shape((width, 2, half))], (x, reduce_kernel), "reduce_first")


def reduce_next(both, every, gain, bias, s, reduce_kernel, narrow):
    cells, channels = both.shape
    half = reduce_kernel.shape[1]
    width = every.shape[0]

    def body(both_ref, every_ref, g_ref, b_ref, r_ref, low_ref, reduced_ref, stats_ref, mi_ref):
        mean, inv = moments(every_ref[...], float(cells), float(cells * width))
        mi_ref[...] = jnp.concatenate([mean, inv], axis=0)
        gain_row, bias_row = g_ref[s : s + 1], b_ref[s : s + 1]

        def apply(at, carry):
            low_ref[at, :] = gelu((both_ref[at, :] - mean) * inv * gain_row + bias_row).astype(bf16)
            return carry

        sweep(cells, apply, step=32)
        reduced_ref[...] = dot(low_ref[:, narrow:], r_ref[...])
        emit_moments(stats_ref, reduced_ref, float(cells))

    outs = [shape((cells, channels), bf16), shape((cells, half)), shape((width, 2, half)), shape((2, channels))]
    return run(body, outs, (both, every, gain, bias, reduce_kernel), "reduce_next")


def hidden_act(reduced, every, gain, bias, s):
    cells, channels = reduced.shape
    width = every.shape[0]

    def body(v_ref, every_ref, g_ref, b_ref, low_ref, hidden_ref, mi_ref):
        mean, inv = moments(every_ref[...], float(cells), float(cells * width))
        mi_ref[...] = jnp.concatenate([mean, inv], axis=0)
        gain_row, bias_row = g_ref[s : s + 1], b_ref[s : s + 1]

        def apply(at, carry):
            act = gelu((v_ref[at, :] - mean) * inv * gain_row + bias_row)
            hidden_ref[at, :] = act
            low_ref[at, :] = act.astype(bf16)
            return carry

        sweep(cells, apply)

    outs = [shape((cells, channels), bf16), shape((cells, channels)), shape((2, channels))]
    return run(body, outs, (reduced, every, gain, bias), "hidden_act")


def freq_act(mixed, every, gain, bias, s, factor, place, counts, e_n, z_n):
    points, channels = mixed.shape
    width = every.shape[0]

    def body(v_ref, every_ref, g_ref, b_ref, factor_ref, place_ref, low_ref, mi_ref):
        by_device = device_counts(counts, place_ref[0], width, e_n, z_n)
        mean, inv = moments(every_ref[...], by_device, jnp.sum(by_device))
        mi_ref[...] = jnp.concatenate([mean, inv], axis=0)
        gain_row, bias_row = g_ref[s : s + 1], b_ref[s : s + 1]

        def apply(at, carry):
            act = gelu((v_ref[at, :] - mean) * inv * gain_row + bias_row)
            low_ref[at, :] = (act * lanes_of(factor_ref[at, :], channels)).astype(bf16)
            return carry

        sweep(points, apply)

    outs = [shape((points, channels), bf16), shape((2, channels))]
    return run(body, outs, (mixed, every, gain, bias, factor, place), "freq_act", scalars=1)


def blocks_of(rows, most):
    count = -(-rows // most)
    while rows % (16 * count):
        count += 1
    return [slice(i * rows // count, (i + 1) * rows // count) for i in range(count)]


def spectrum_forward(table, own, others, freq_kernel, factor, scale, width):
    points = table.shape[1]
    cells, half = own.shape
    wide = freq_kernel.shape[1]

    def body(t_ref, own_ref, others_ref, w_ref, factor_ref, real_ref, imag_ref, mixed_ref, stats_ref):
        for side, out_ref in enumerate((real_ref, imag_ref)):
            for at in blocks_of(points, 272):
                z = dot(t_ref[side, at, :cells], own_ref[...]) + dot(t_ref[side, at, cells:], others_ref[...])
                out_ref[at, :] = (z * scale).astype(bf16)
        mixed_ref[...] = dot(real_ref[...], w_ref[:half]) + dot(imag_ref[...], w_ref[half:])
        count = jnp.sum(jnp.where(factor_ref[:, :1] > 0.0, 1.0, 0.0))
        emit_moments(stats_ref, mixed_ref, count, factor_ref)

    outs = [shape((points, half), bf16), shape((points, half), bf16), shape((points, wide)), shape((width, 2, wide))]
    return run(body, outs, (table, own, others, freq_kernel, factor), "spectrum_forward")


def inverse_forward(table, own, others, hidden, pre, expand_t, scale, width):
    cells = table.shape[1]
    half = hidden.shape[1]
    channels = pre.shape[1]
    narrow = channels - expand_t.shape[0]

    def body(t_ref, own_ref, others_ref, hidden_ref, pre_ref, e_ref, summed_ref, both_ref, stats_ref):
        freq = jnp.concatenate([own_ref[...], others_ref[...]], axis=0)
        real, imag = freq[:, :half], freq[:, half:]
        total = freq.shape[0]
        for at in blocks_of(cells, 256):
            returned = dot(t_ref[0, at, :total], real) + dot(t_ref[1, at, :total], imag)
            summed_ref[at, :] = (hidden_ref[at, :] + returned * scale).astype(bf16)
        both_ref[:, :narrow] = pre_ref[:, :narrow]
        for at in blocks_of(cells, 256):
            both_ref[at, narrow:] = pre_ref[at, narrow:] + dot_t(summed_ref[at, :], e_ref[...])
        emit_moments(stats_ref, both_ref, float(cells))

    outs = [shape((cells, half), bf16), shape((cells, channels)), shape((width, 2, channels))]
    return run(body, outs, (table, own, others, hidden, pre, expand_t), "inverse_forward")


def turn(both, every, gain, bias, s, x, cot):
    cells, channels = both.shape

    width = every.shape[0]

    def body(both_ref, every_ref, g_ref, b_ref, x_ref, cot_ref, out_ref, q_ref, sums_ref, mi_ref):
        mean, inv = moments(every_ref[...], float(cells), float(cells * width))
        mi_ref[...] = jnp.concatenate([mean, inv], axis=0)
        gain_row, bias_row = g_ref[s : s + 1], b_ref[s : s + 1]

        def apply(at, sums):
            normed = (both_ref[at, :] - mean) * inv
            state, slope = gelu_parts(normed * gain_row + bias_row)
            out_ref[at, :] = (x_ref[at, :].astype(f32) + state).astype(bf16)
            q = slope * cot_ref[at, :].astype(f32)
            q_ref[at, :] = q
            return add_sums(sums, q, normed)

        emit_sums(sums_ref, sweep(cells, apply, pair(channels), step=32))

    outs = [shape((cells, channels), bf16), shape((cells, channels)), shape((width, 2, channels)), shape((2, channels))]
    return run(body, outs, (both, every, gain, bias, x, cot), "turn")


def grad_pre(q, both, mi, every, gain, s, expand_t, total):
    cells, channels = both.shape
    broad, half = expand_t.shape
    narrow = channels - broad

    def body(q_ref, both_ref, mi_ref, every_ref, g_ref, e_ref, *refs):
        low_ref, summed_ref, summed_low_ref, sums_ref = refs
        sums, bias_term, gain_term = back_terms(every_ref, total)
        sums_ref[...] = sums
        mean, inv = mi_ref[0:1], mi_ref[1:2]
        gain_row = g_ref[s : s + 1] * inv

        def apply(at, carry):
            normed = (both_ref[at, :] - mean) * inv
            low_ref[at, :] = (gain_row * (q_ref[at, :] - bias_term - normed * gain_term)).astype(bf16)
            return carry

        sweep(cells, apply, step=32)
        summed_ref[...] = dot(low_ref[:, narrow:], e_ref[...])
        summed_low_ref[...] = summed_ref[...].astype(bf16)

    outs = [shape((cells, channels), bf16), shape((cells, half)), shape((cells, half), bf16), shape((2, channels))]
    return run(body, outs, (q, both, mi, every, gain, expand_t), "grad_pre")


def spectrum_backward(table, own, others, mixed, mi, gain, bias, s, factor, scale, width):
    points, wide = mixed.shape
    cells, half = own.shape

    def body(t_ref, own_ref, others_ref, mixed_ref, mi_ref, g_ref, b_ref, factor_ref, *refs):
        q_ref, sums_ref, n_ref = refs
        mean, inv = mi_ref[0:1], mi_ref[1:2]
        gain_row, bias_row = g_ref[s : s + 1], b_ref[s : s + 1]
        for side in range(2):
            for at in blocks_of(points, 272):
                z = dot(t_ref[side, at, :cells], own_ref[...]) + dot(t_ref[side, at, cells:], others_ref[...])
                q_ref[at, side * half : (side + 1) * half] = z * scale

        def apply(at, sums):
            normed = (mixed_ref[at, :] - mean) * inv
            q = gelu_parts(normed * gain_row + bias_row)[1] * (q_ref[at, :] * lanes_of(factor_ref[at, :], wide))
            q_ref[at, :] = q
            n_ref[at, :] = normed
            return add_sums(sums, q, normed)

        emit_sums(sums_ref, sweep(points, apply, pair(wide)))

    outs = [shape((points, wide)), shape((width, 2, wide)), shape((points, wide))]
    return run(body, outs, (table, own, others, mixed, mi, gain, bias, factor), "spectrum_backward")


def norm_low(low_ref, q_ref, n_ref, mi_ref, gain_row, bias_term, gain_term):
    gain_row = gain_row * mi_ref[1:2]

    def apply(at, carry):
        low_ref[at, :] = (gain_row * (q_ref[at, :] - bias_term - n_ref[at, :] * gain_term)).astype(bf16)
        return carry

    sweep(q_ref.shape[0], apply)


def grad_mixed(q, normed, mi, every, gain, s, freq_kernel, place, totals):
    points, wide = q.shape

    def body(q_ref, n_ref, mi_ref, every_ref, g_ref, w_ref, place_ref, low_ref, back_ref, sums_ref):
        total = jnp.where(place_ref[0] == 0, float(totals[0]), float(totals[1]))
        sums, bias_term, gain_term = back_terms(every_ref, total)
        sums_ref[...] = sums
        norm_low(low_ref, q_ref, n_ref, mi_ref, g_ref[s : s + 1], bias_term, gain_term)
        back_ref[...] = dot_t(low_ref[...], w_ref[...]).astype(bf16)

    outs = [shape((points, wide), bf16), shape((points, wide), bf16), shape((2, wide))]
    return run(body, outs, (q, normed, mi, every, gain, freq_kernel, place), "grad_mixed", scalars=1)


def inverse_backward(table, own, others, summed, reduced, mi, gain, bias, s, scale, width):
    cells = table.shape[1]
    half = summed.shape[1]

    def body(t_ref, own_ref, others_ref, summed_ref, reduced_ref, mi_ref, g_ref, b_ref, *refs):
        q_ref, sums_ref, n_ref = refs
        mean, inv = mi_ref[0:1], mi_ref[1:2]
        gain_row, bias_row = g_ref[s : s + 1], b_ref[s : s + 1]
        freq = jnp.concatenate([own_ref[...], others_ref[...]], axis=0)
        real, imag = freq[:, :half], freq[:, half:]
        total = freq.shape[0]
        for at in blocks_of(cells, 256):
            back = dot(t_ref[0, at, :total], real) + dot(t_ref[1, at, :total], imag)
            q_ref[at, :] = summed_ref[at, :] + back * scale

        def apply(at, sums):
            normed = (reduced_ref[at, :] - mean) * inv
            q = gelu_parts(normed * gain_row + bias_row)[1] * q_ref[at, :]
            q_ref[at, :] = q
            n_ref[at, :] = normed
            return add_sums(sums, q, normed)

        emit_sums(sums_ref, sweep(cells, apply, pair(half)))

    outs = [shape((cells, half)), shape((width, 2, half)), shape((cells, half))]
    return run(body, outs, (table, own, others, summed, reduced, mi, gain, bias), "inverse_backward")


def grad_reduced(q, normed, mi, every, gain, s, reduce_kernel, total, conv_back, both, mi_3, gain_3, bias_3, width):
    cells, half = q.shape
    channels = both.shape[1]
    narrow = channels - reduce_kernel.shape[0]

    def body(q_ref, n_ref, mi_ref, every_ref, g_ref, r_ref, conv_ref, both_ref, mi3_ref, g3_ref, b3_ref, *refs):
        low_ref, out_ref, sums3_ref, sums_ref = refs
        sums, bias_term, gain_term = back_terms(every_ref, total)
        sums_ref[...] = sums
        norm_low(low_ref, q_ref, n_ref, mi_ref, g_ref[s : s + 1], bias_term, gain_term)
        out_ref[:, :narrow] = conv_ref[:, :narrow]
        for at in blocks_of(cells, 256):
            out_ref[at, narrow:] = conv_ref[at, narrow:] + dot_t(low_ref[at, :], r_ref[...])
        mean, inv = mi3_ref[0:1], mi3_ref[1:2]
        gain_row, bias_row = g3_ref[s - 1 : s], b3_ref[s - 1 : s]

        def apply(at, sums):
            normed_3 = (both_ref[at, :] - mean) * inv
            grad = gelu_parts(normed_3 * gain_row + bias_row)[1] * out_ref[at, :]
            out_ref[at, :] = grad
            return add_sums(sums, grad, normed_3)

        emit_sums(sums3_ref, sweep(cells, apply, pair(channels), step=32))

    outs = [shape((cells, half), bf16), shape((cells, channels)), shape((width, 2, channels)), shape((2, half))]
    ins = (q, normed, mi, every, gain, reduce_kernel, conv_back, both, mi_3, gain_3, bias_3)
    return run(body, outs, ins, "grad_reduced")


def grad_last(q, normed, mi, every, gain, s, total):
    cells, half = q.shape

    def body(q_ref, n_ref, mi_ref, every_ref, g_ref, *refs):
        low_ref, sums_ref = refs
        sums, bias_term, gain_term = back_terms(every_ref, total)
        sums_ref[...] = sums
        norm_low(low_ref, q_ref, n_ref, mi_ref, g_ref[s : s + 1], bias_term, gain_term)

    outs = [shape((cells, half), bf16), shape((2, half))]
    return run(body, outs, (q, normed, mi, every, gain), "grad_last")


def input_grad(cots, conv, late, reduce_kernel, place):
    channels = cots[0].shape[3]
    narrow = channels - reduce_kernel.shape[0]

    def body(cot0_ref, cot1_ref, *refs):
        conv_refs, late_refs, (r_ref, place_ref), out_refs = refs[:2], refs[2:4], refs[4:6], refs[6:]
        c = place_ref[1]
        for kind, (cot_ref, out_ref) in enumerate(zip((cot0_ref, cot1_ref), out_refs)):
            _, rows, cols, _ = cot_ref.shape
            half = cols // 2
            for side, core in enumerate((c, 1 - c)):
                at = pl.ds(pl.multiple_of(core * half, half), half)
                into = dot_t(late_refs[side][kind], r_ref[...]).reshape(rows, half, channels - narrow)
                base = conv_refs[side][kind].astype(f32).reshape(rows, half, channels) + cot_ref[0, :, at, :].astype(f32)
                out_ref[0, :, at, :narrow] = base[..., :narrow].astype(bf16)
                out_ref[0, :, at, narrow:] = (base[..., narrow:] + into).astype(bf16)

    outs = [shape(cot.shape, bf16) for cot in cots]
    ins = (*cots, *conv, *late, reduce_kernel, place)
    return run(body, outs, ins, "input_grad", limit=12, scalars=1)


def edge_cells(low, above, place, unit):
    cells, channels = low.shape
    blocks = cells // unit + 4

    def body(*refs):
        x_ref, place_ref, out_ref = refs[0], refs[-2], refs[-1]
        if above is None:
            zeros = jnp.zeros((2, channels), f32)
            ends = x_ref[...].astype(f32).reshape(blocks - 4, unit, channels)
            first = jnp.concatenate([zeros, ends[:, 0], zeros], axis=0)
            last = jnp.concatenate([zeros, ends[:, unit - 1], zeros], axis=0)
        else:
            wide = jnp.concatenate([refs[1][...], x_ref[...], refs[2][...]], axis=0)
            ends = wide.astype(f32).reshape(blocks, unit, channels)
            first, last = ends[:, 0], ends[:, unit - 1]
        land, left = place_ref[0] == 0, place_ref[1] == 0
        last = jnp.where(land, jnp.concatenate([last[1:], last[:1]], axis=0), last)
        first = jnp.where(land, jnp.concatenate([first[-1:], first[:-1]], axis=0), first)
        out_ref[...] = jnp.where(left, last, first).astype(bf16)

    ins = (low, place) if above is None else (low, *above, place)
    return run(body, [shape((blocks, channels), bf16)], ins, "edge_cells", scalars=1)[0]


def surroundings(low, place, unit):
    e_n = lax.axis_size("e")
    above = None
    if e_n > 1:
        ahead = [(e, e + 1) for e in range(e_n - 1)]
        above = (
            lax.ppermute(low[-2 * unit :], "e", ahead),
            lax.ppermute(low[: 2 * unit], "e", [(b, a) for a, b in ahead]),
        )
    beside = lax.ppermute(edge_cells(low, above, place, unit), "c", SWAP)
    return above, beside


def shifted_columns(x_ref, above_refs, beside_ref, land, left, out_ref, unit):
    cells, channels = x_ref.shape
    blocks = cells // unit + 4
    block = lax.broadcasted_iota(jnp.int32, (blocks, unit, 1), 0)
    cell = lax.broadcasted_iota(jnp.int32, (blocks, unit, 1), 1)
    for lane in range(0, channels, 128):
        at = slice(lane, lane + 128)
        if above_refs:
            top, bottom = above_refs[0][:, at], above_refs[1][:, at]
        else:
            top = bottom = jnp.zeros((2 * unit, 128), bf16)
        wide = jnp.concatenate([top, x_ref[:, at], bottom], axis=0)
        out_ref[1, :, at] = wide
        wide = wide.astype(f32)
        beside = beside_ref[:, at].astype(f32)[:, None, :]
        for j, edge, odd in ((0, 0, 0), (2, unit - 1, 1)):
            moved = pltpu.roll(wide, 1 if j == 0 else blocks * unit - 1, 0).reshape(blocks, unit, 128)
            outer_side = (cell == edge) & (jnp.logical_not(land) | (block % 2 == odd))
            fill = jnp.where(left if j == 2 else jnp.logical_not(left), beside, 0.0)
            out_ref[j, :, at] = jnp.where(outer_side, fill, moved).reshape(blocks * unit, 128).astype(bf16)


def rows_at(i, first, count, land, unit):
    if i == 1:
        return slice(2 * unit + first, 2 * unit + first + count)
    step = jnp.where(land, 2 * unit, unit)
    return pl.ds(pl.multiple_of(2 * unit + first + (i - 1) * step, unit), count)


def conv_forward(low, above, beside, place, unit, local_kernel, global_t):
    cells, channels = low.shape
    narrow = local_kernel.shape[1] // 9
    padded = cells + 4 * unit
    extra = () if above is None else above
    start = 4 + len(extra)

    def body(*refs):
        x_ref, beside_ref, l_ref, g_ref = refs[0], *refs[1 + len(extra) : 4 + len(extra)]
        place_ref, pre_ref, cols_ref, wide_ref = refs[start:]
        land, left = place_ref[0] == 0, place_ref[1] == 0
        shifted_columns(x_ref, refs[1 : 1 + len(extra)], beside_ref, land, left, wide_ref, unit)
        cols_ref[...] = wide_ref[:, :, :narrow]
        for at in blocks_of(cells, 512):
            count = at.stop - at.start
            local = jnp.zeros((count, narrow), f32)
            patches = []
            for t in range(9):
                block = wide_ref[t % 3, rows_at(t // 3, at.start, count, land, unit), :]
                local = local + dot(block, l_ref[:, t * narrow : (t + 1) * narrow])
                patches.append(block[:, :narrow])
            pre_ref[at, :narrow] = local
            pre_ref[at, narrow:] = dot_t(jnp.concatenate(patches, axis=1), g_ref[...])

    outs = [shape((cells, channels)), shape((3, padded, narrow), bf16)]
    ins = (low, *extra, beside, local_kernel, global_t, place)
    return run(body, outs, ins, "conv_forward", [pltpu.VMEM((3, padded, channels), bf16)], 12, 1)


def conv_backward(low, above, beside, place, unit, local_kernel, global_t, kind):
    cells, channels = low.shape
    narrow = local_kernel.shape[1] // 9
    padded = cells + 4 * unit
    extra = () if above is None else above
    start = 4 + len(extra)

    def body(*refs):
        x_ref, beside_ref, l_ref, g_ref = refs[0], *refs[1 + len(extra) : 4 + len(extra)]
        place_ref, grad_ref, patches_ref, wide_ref = refs[start:]
        land, left = place_ref[0] == 0, place_ref[1] == 0
        shifted_columns(x_ref, refs[1 : 1 + len(extra)], beside_ref, land, left, wide_ref, unit)
        for at in blocks_of(cells, 512):
            count = at.stop - at.start
            into = jnp.zeros((count, narrow), f32)
            for t in range(9):
                block = wide_ref[2 - t % 3, rows_at(2 - t // 3, at.start, count, land, unit), :]
                patches_ref[at, t * narrow : (t + 1) * narrow] = block[:, :narrow]
                into = into + dot(block[:, narrow:], g_ref[:, t * narrow : (t + 1) * narrow])
            grad = dot_t(patches_ref[at, :], l_ref[...])
            grad_ref[at, :narrow] = (grad[:, :narrow] + into).astype(kind)
            grad_ref[at, narrow:] = grad[:, narrow:].astype(kind)

    outs = [shape((cells, channels), kind), shape((cells, 9 * narrow), bf16)]
    ins = (low, *extra, beside, local_kernel, global_t, place)
    return run(body, outs, ins, "conv_backward", [pltpu.VMEM((3, padded, channels), bf16)], 12, 1)


def spaced(rows, own, pad):
    row = lax.broadcasted_iota(jnp.int32, (rows, rows // own * pad), 0)
    place = lax.broadcasted_iota(jnp.int32, (rows, rows // own * pad), 1)
    return jnp.where(place == row // own * pad + row % own, 1.0, 0.0).astype(bf16)


def copies(values, count):
    def body(in_ref, out_ref):
        for i in range(count):
            out_ref[i] = in_ref[...]

    return run(body, [shape((count,) + values.shape, values.dtype)], (values,), "copies")[0]


def unpack_small(blocks, own, half):
    pad, columns = blocks.shape[-2:]
    devices = math.prod(blocks.shape[:-2])
    wide = columns - 2 * half

    def body(full_ref, *out_refs):
        split_small(full_ref[...].reshape(devices * pad, columns), spaced(devices * own, own, pad), wide, half, out_refs)

    outs = [shape((devices * own, width), bf16) for width in (wide, half, half)]
    return run(body, outs, (blocks,), "unpack_small", limit=12)


def split_small(full, place, wide, half, out_refs):
    full = dot(place, full).astype(bf16)
    out_refs[0][...] = full[:, :wide]
    out_refs[1][...] = full[:, wide : wide + half]
    out_refs[2][...] = full[:, wide + half : wide + 2 * half]


def unpack_kernels(full, sections, own_in, pad_in, own_out, half):
    devices, rows, columns = full.shape
    pad = (rows - sections * pad_in) // (2 * sections - 1)
    plain = own_in == pad_in
    wide = devices * own_out
    each = pad_in + pad

    def body(full_ref, *refs):
        out_refs, small_refs = refs[: 2 * sections], refs[2 * sections : 5 * sections - 3]
        local_ref, global_ref, small_ref, sems = refs[5 * sections - 3 :]
        copies = []
        for s in range(sections):
            target = out_refs[2 * s] if plain else local_ref.at[s]
            sources = [(s * each, pad_in, target), (s * each + pad_in, pad, global_ref.at[s])]
            if s:
                sources.append((sections * each + (s - 1) * pad, pad, small_ref.at[s - 1]))
            for k, (first, count, target) in enumerate(sources):
                source = full_ref.at[:, pl.ds(first, count), :]
                copies.append(pltpu.make_async_copy(source, target, sems.at[s, k]))
        for copy in copies:
            copy.start()
        for copy in copies:
            copy.wait()
        place = spaced(devices * own_out, own_out, pad)
        for s in range(sections):
            if not plain:
                block = local_ref[s].reshape(devices * pad_in, columns)
                out_refs[2 * s][...] = dot(spaced(devices * own_in, own_in, pad_in), block).astype(bf16)
            out_refs[2 * s + 1][...] = dot(place, global_ref[s].reshape(devices * pad, columns)).astype(bf16)
            if s:
                block = small_ref[s - 1].reshape(devices * pad, columns)
                split_small(block, place, wide, half, small_refs[3 * s - 3 : 3 * s])

    local = (devices, pad_in, columns) if plain else (devices * own_in, columns)
    outs = [shape(dims, bf16) for dims in (local, (devices * own_out, columns))] * sections
    outs += [shape((devices * own_out, width), bf16) for width in (wide, half, half)] * (sections - 1)
    scratch = [
        pltpu.VMEM((8,) * 4 if plain else (sections, devices, pad_in, columns), bf16),
        pltpu.VMEM((sections, devices, pad, columns), bf16),
        pltpu.VMEM((max(sections - 1, 1), devices, pad, columns), bf16),
        pltpu.SemaphoreType.DMA((sections, 3)),
    ]
    limit = 44 if plain else 52
    out = run(body, outs, (InPlace(full),), "unpack_kernels", scratch, limit)
    kernels = [(out[2 * s].reshape(devices * own_in, columns), out[2 * s + 1]) for s in range(sections)]
    return kernels, out[2 * sections :]


def early_grads(x_low, patches, grad_low, shifted, summed, place, unit, own, pad, alike):
    cells, channels = x_low.shape
    narrow = shifted.shape[2]
    broad = channels - narrow
    half = summed.shape[1]
    wide = 9 * narrow

    def body(x_ref, p_ref, g_ref, s_ref, m_ref, place_ref, *out_refs):
        land = place_ref[0] == 0
        out_refs[-1][...] = jnp.zeros((8, 128), f32)
        local_ref, other_ref, first = (out_refs[0], out_refs[0], wide) if alike else (*out_refs[:2], 0)
        for i in range(3):
            at = slice(3 * i * narrow, 3 * (i + 1) * narrow)
            local_ref[:, at] = outer(x_ref[...], p_ref[:, at]).astype(bf16)
        grad = dot(g_ref[:, narrow:], spaced(broad, own, pad)).astype(bf16)
        for i in range(3):
            taps = [s_ref[j, rows_at(i, 0, cells, land, unit), :] for j in range(3)]
            at = slice(first + 3 * i * narrow, first + 3 * (i + 1) * narrow)
            other_ref[:, at] = outer(grad, jnp.concatenate(taps, axis=1)).astype(bf16)
        other_ref[:, first + wide :] = outer(grad, m_ref[...]).astype(bf16)

    padded = broad // own * pad
    if alike:
        outs = [shape((channels, 2 * wide + half), bf16)]
    else:
        outs = [shape((channels, wide), bf16), shape((padded, wide + half), bf16)]
    outs.append(shape((8, 128)))
    ins = (x_low, patches, grad_low, shifted, summed, place)
    return run(body, outs, ins, "early_grads", limit=12, scalars=1)[:-1]


def freq_grads(real, imag, mixed_low, own, pad):
    wide = mixed_low.shape[1]

    def body(real_ref, imag_ref, m_ref, out_ref):
        freq = jnp.concatenate([outer(real_ref[...], m_ref[...]), outer(imag_ref[...], m_ref[...])], axis=0)
        out_ref[...] = outer(spaced(wide, own, pad), freq.astype(bf16)).astype(bf16)

    return run(body, [shape((wide // own * pad, wide), bf16)], (real, imag, mixed_low), "freq_grads")[0]


def reduce_grads(x_low, reduced_low, narrow, own, pad):
    broad = x_low.shape[1] - narrow

    def body(x_ref, r_ref, out_ref):
        reduce = outer(x_ref[:, narrow:], r_ref[...])
        out_ref[...] = outer(spaced(broad, own, pad), reduce.astype(bf16)).astype(bf16)

    outs = [shape((broad // own * pad, reduced_low.shape[1]), bf16)]
    return run(body, outs, (x_low, reduced_low), "reduce_grads")[0]


def core_parts(shares, here, g_n):
    parts = [part.reshape((g_n, 2, -1) + part.shape[1:]) for part in shares]
    rows, widths = parts[0].shape[2], [part.shape[3] for part in parts]
    starts = [sum(widths[:i]) for i in range(len(widths) + 1)]

    def body(*refs):
        c = refs[len(parts)][0]
        theirs_ref, mine_ref = refs[len(parts) + 1 :]
        for i, ref in enumerate(refs[: len(parts)]):
            at = slice(starts[i], starts[i + 1])
            for g in range(g_n):
                theirs_ref[g, :, at] = ref[g, 1 - c]
                mine_ref[g, :, at] = ref[g, c]

    outs = [shape((g_n, rows, starts[-1]), bf16)] * 2
    return run(body, outs, (*parts, here[2]), "core_parts", scalars=1)


def add_parts(mine, theirs, here):
    g_n = mine.shape[0]

    def body(mine_ref, theirs_ref, *refs):
        for step in range(g_n):
            g = refs[0][0] ^ step
            total = mine_ref[g].astype(f32) + theirs_ref[g].astype(f32)
            refs[1 + step][...] = total if step == 0 else total.astype(bf16)

    outs = [shape(mine.shape[1:], f32 if step == 0 else bf16) for step in range(g_n)]
    return run(body, outs, (mine, theirs, here[1]), "add_parts", scalars=1)


def add_plane(pieces, here, line_n):
    rows, columns = pieces[0].shape
    block = rows // line_n

    def body(*refs):
        for i in range(line_n):
            at = slice(i * block, (i + 1) * block)
            total = refs[0][at, :].astype(f32)
            for ref in refs[1:-1]:
                total = total + ref[at, :].astype(f32)
            refs[-1][i] = total.astype(bf16)

    return run(body, [shape((line_n, block, columns), bf16)], pieces, "add_plane")[0]


def owned(shares, here):
    g_n = lax.axis_size("g")
    line = ("k", "z", "e")
    line_n = lax.axis_size(line)
    theirs, mine = core_parts(shares, here, g_n)
    theirs = lax.ppermute(theirs, "c", SWAP)
    yield
    pieces = over_plane(add_parts(mine, theirs, here))
    yield
    sums = add_plane(pieces, here, line_n)
    yield
    if line_n > 4:
        pieces = [lax.all_to_all(sums, line, 0, 0, tiled=True)]
    else:
        pieces = over_line(for_partners(sums, here[0]))
    yield
    return total_of(pieces)


def owned_apart(shares):
    for axes in (("g", "c"), ("k", "z", "e")):
        shares = shares.reshape(lax.axis_size(axes), -1, shares.shape[-1])
        shares = lax.psum_scatter(shares, axes, scatter_dimension=0, tiled=True).reshape(-1, shares.shape[-1])
        if "g" in axes:
            yield
            shares = copies(shares, 1)[0]
    return shares


def total_of(blocks):
    dims = blocks[0].shape[-2:]

    def body(*refs):
        total = jnp.zeros(dims, f32)
        for ref in refs[:-1]:
            for part in [ref[i] for i in range(ref.shape[0])] if len(ref.shape) == 3 else [ref[...]]:
                total = total + part.astype(f32)
        refs[-1][...] = total

    return run(body, [shape(dims)], blocks, "total_of")[0]


def pack_sums(sums):
    widths = [item.shape[1] for item in sums]

    def body(*refs):
        refs[-1][...] = jnp.concatenate([ref[...] for ref in refs[:-1]], axis=1)

    return run(body, [shape((2, sum(widths)))], sums, "pack_sums")[0]


def results(totals, sums, other_sums, own_in, own_out, narrow, half, channels, alike):
    sections = len(totals)
    wides = (9 * narrow, 9 * narrow + half, 2 * half, half)
    flat, where = [], {}
    for s in range(sections):
        if s == 0:
            rest = [(1, 0)] + ([(2, 1), (3, 1)] if sections > 1 else []) + [(2, 0)]
        else:
            rest = [(1, s)]
        parts = [[(0, s), *rest]] if alike else [[(0, s)], rest]
        if s != 1:
            parts.append([(3, s)] if s == 0 else [(2, s), (3, s)])
        assert len(parts) == len(totals[s])
        for group, item in zip(parts, totals[s]):
            start = 0
            for part in group:
                where[part] = (len(flat), start)
                start += wides[part[0]]
            flat.append(item)

    def body(*refs):
        sums_ref, other_ref, local_ref, global_ref, reduce_ref, freq_ref, expand_ref, *norm_refs = refs[len(flat) :]
        for s in range(sections):

            def columns(part, start, count, rows):
                index, first = where[part, s]
                return refs[index][:rows, first + start : first + start + count].astype(f32)

            for t in range(9):
                local_ref[s, t] = columns(0, t * narrow, narrow, own_in)
                global_ref[t, :, s, :] = columns(1, t * narrow, narrow, own_out)
            expand_ref[:, s, :] = columns(1, 9 * narrow, half, own_out)
            freq_ref[:, s, :] = columns(2, 0, 2 * half, own_out)
            reduce_ref[:, s, :] = columns(3, 0, half, own_out)
        both = sums_ref[...] + other_ref[...]
        at = 0
        for s in range(sections):
            for index, wide in enumerate((half, 2 * half, channels)):
                norm_refs[2 * index][s : s + 1, :] = both[1:2, at : at + wide]
                norm_refs[2 * index + 1][s : s + 1, :] = both[0:1, at : at + wide]
                at += wide

    outs = [
        shape((sections, 9, own_in, narrow)),
        shape((9, own_out, sections, narrow)),
        shape((own_out, sections, half)),
        shape((own_out, sections, 2 * half)),
        shape((own_out, sections, half)),
    ]
    outs += [shape((sections, wide)) for wide in (half, half, 2 * half, 2 * half, channels, channels)]
    out = run(body, outs, (*flat, sums, other_sums), "results")
    return (
        out[0],
        jnp.transpose(out[1], (2, 0, 3, 1)),
        jnp.transpose(out[2], (1, 0, 2)),
        jnp.transpose(out[3], (1, 0, 2)),
        jnp.transpose(out[4], (1, 2, 0)),
        *out[5:],
    )


def pick_tables(table, factors, variant, size):
    points, cells = factors.shape[1], size // lax.axis_size(PART)
    columns = -(-points * lax.axis_size(PART) // 128) * 128

    def body(table_ref, factor_ref, v_ref, forward_ref, inverse_ref, out_ref, sems):
        v = v_ref[0]
        copies = []
        for side in range(2):
            source = table_ref.at[v, pl.ds(side * points, points), pl.ds(0, size)]
            copies.append(pltpu.make_async_copy(source, forward_ref.at[side], sems.at[0, side]))
            source = table_ref.at[v, pl.ds(2 * points + side * cells, cells), pl.ds(0, columns)]
            copies.append(pltpu.make_async_copy(source, inverse_ref.at[side], sems.at[1, side]))
        for copy in copies:
            copy.start()
        out_ref[...] = factor_ref[v]
        for copy in copies:
            copy.wait()

    outs = [shape((2, points, size), bf16), shape((2, cells, columns), bf16), shape(factors.shape[1:])]
    ins = (InPlace(table), factors, variant)
    return run(body, outs, ins, "pick_tables", [pltpu.SemaphoreType.DMA((2, 2))], 12, 1)


def per_device(plan, *args):
    (
        land,
        port,
        to_local,
        to_global,
        reduce_weight,
        freq_weight,
        expand_weight,
        spec_gain,
        spec_bias,
        freq_gain,
        freq_bias,
        out_gain,
        out_bias,
        cot_land,
        cot_port,
    ) = args
    rounds, table, weight_table, point_counts = plan
    sections = to_local.shape[0]
    devices = lax.axis_size(ALL)
    own_in = to_local.shape[2]
    own_out = to_global.shape[3]
    pad = -(-own_out // 16) * 16
    narrow = to_local.shape[3]
    channels = own_in * devices
    half = reduce_weight.shape[2]
    unit = port.shape[2] // 2
    k, c, part = lax.axis_index("k"), lax.axis_index("c"), lax.axis_index(PART)
    line_here = lax.axis_index(("k", "z", "e"))
    place = jnp.stack([k, c, line_here]).astype(jnp.int32)
    here = tuple(index.astype(jnp.int32).reshape(1) for index in (line_here, lax.axis_index("g"), c))
    variant = k * lax.axis_size(PART) + part
    g_n, z_n, e_n = lax.axis_size("g"), lax.axis_size("z"), lax.axis_size("e")
    width = lax.axis_size(KIND)

    pad_in = -(-own_in // 16) * 16
    Order.last = ()

    grow = ((0, 0), (0, pad - own_out), (0, 0))
    taps_local = jnp.transpose(to_local, (0, 2, 1, 3)).reshape(sections, own_in, 9 * narrow)
    taps_local = jnp.pad(taps_local, ((0, 0), (0, pad_in - own_in), (0, 0)))
    taps_global = jnp.pad(jnp.transpose(to_global, (0, 3, 1, 2)).reshape(sections, own_out, 9 * narrow), grow)
    packed = jnp.concatenate([freq_weight, reduce_weight, jnp.transpose(expand_weight, (0, 2, 1))], axis=2)
    packed = jnp.pad(packed, grow)
    small = copies(packed[0], lax.axis_size(("k", "z", "e")))
    small = lax.all_to_all(small, ("k", "z", "e"), 0, 0, tiled=True)
    later = jnp.pad(packed[1:], ((0, 0), (0, 0), (0, 9 * narrow - packed.shape[2])))
    taps = jnp.concatenate([taps_local, taps_global], axis=1)
    taps = jnp.concatenate([item.reshape(-1, 9 * narrow) for item in (taps, later)], axis=0)
    taps = lax.all_gather(taps, ALL)
    x_steps = to_tile(land, port, rounds, place, here)
    advance(x_steps)
    advance(x_steps)
    small = copies(small, lax.axis_size(("g", "c")))
    small = lax.all_to_all(small, ("g", "c"), 0, 0, tiled=True)
    variant = variant.reshape(1)
    size = land.shape[1] * land.shape[2] * lax.axis_size(("k", "z", "e"))
    forward, inverse, factor = pick_tables(jnp.asarray(table), jnp.asarray(np.repeat(weight_table[..., None], 128, axis=2)), variant, size)
    small = unpack_small(small, own_out, half)
    x = finish(x_steps)

    cells = x.shape[0]
    scale = 1.0 / math.sqrt(size)
    cell_total = float(g_n * z_n * size)
    point_totals = [int(item.sum()) * g_n * z_n for item in point_counts]

    def exchange(stats):
        every = lax.all_to_all(stats, KIND, 0, 0, tiled=True)
        Order.last = (every,)
        return every

    kept = []
    for s in range(sections):
        freq_kernel, reduce_kernel, expand_t = small[3 * s : 3 * s + 3]
        if s == 0:
            low = x
            reduced, stats = reduce_first(x, reduce_kernel, width, narrow)
        else:
            low, reduced, stats, kept[-1]["mi_3"] = reduce_next(both, every, out_gain, out_bias, s - 1, reduce_kernel, narrow)
        every = exchange(stats)
        if s == 1:
            gate(every)
            cot = finish(cot_steps)
        if s == 0:
            cot_steps = to_tile(cot_land, cot_port, rounds, place, here)
            advance(cot_steps)
        else:
            above, beside = surroundings(low, place, unit)
        hidden_low, hidden, mi_1 = hidden_act(reduced, every, spec_gain, spec_bias, s)
        others = shared(hidden_low)
        if s > 0:
            pre, shifted = conv_forward(low, above, beside, place, unit, *kernels[s])
        real, imag, mixed, stats = spectrum_forward(forward, hidden_low, others, freq_kernel, factor, scale, width)
        every = exchange(stats)
        if s == 0:
            above, beside = surroundings(low, place, unit)
            kernels, more = unpack_kernels(taps, sections, own_in, pad_in, own_out, half)
            small = [*small, *more]
            hold(beside)
        freq_low, mi_2 = freq_act(mixed, every, freq_gain, freq_bias, s, factor, place, point_counts, e_n, z_n)
        others = shared(freq_low)
        if s == 0:
            pre, shifted = conv_forward(low, above, beside, place, unit, *kernels[s])
            advance(cot_steps)
        summed, both, stats = inverse_forward(inverse, freq_low, others, hidden, pre, expand_t, scale, width)
        every = exchange(stats)
        kept.append(
            dict(low=low, shifted=shifted, reduced=reduced, mi_1=mi_1, real=real, imag=imag, mixed=mixed, mi_2=mi_2, summed=summed, both=both)
        )
    if sections == 1:
        cot = finish(cot_steps)
    out, q_3, sums, kept[-1]["mi_3"] = turn(both, every, out_gain, out_bias, sections - 1, x, cot)

    alike = own_in == pad

    def late_grads(item):
        return (
            freq_grads(item["real"], item["imag"], mixed_low, own_out, pad),
            reduce_grads(item["low"], reduced_low, narrow, own_out, pad),
        )

    norm_sums = [None] * sections
    totals = [None] * sections
    last_steps = None
    for s in reversed(range(sections)):
        freq_kernel, reduce_kernel, expand_t = small[3 * s : 3 * s + 3]
        item = kept[s]
        every = exchange(sums)
        if s == sections - 2:
            gate(every)
            out_parts = finish(out_steps)
        low, summed, summed_low, sums_3 = grad_pre(
            q_3, item["both"], item["mi_3"], every, out_gain, s, expand_t, cell_total
        )
        others = shared(summed_low)
        above, beside = surroundings(low, place, unit)

        def kernel_grads():
            return early_grads(
                item["low"], patches, low, item["shifted"], item["summed"], place, unit, own_out, pad, alike
            )

        if s == 0:
            for k in range(1, sections):
                totals[k] = [finish(steps) for steps in totals[k]]
            conv_back, patches = conv_backward(low, above, beside, place, unit, *kernels[s], f32 if s > 0 else bf16)
            conv_steps = from_tile(conv_back, rounds, place, here)
            advance(conv_steps)
            grads = kernel_grads()
            if sections > 1:
                grads = (*grads, *late_grads(kept[1]))
        else:
            hold(beside)
        q, sums, normed = spectrum_backward(
            forward, summed_low, others, item["mixed"], item["mi_2"], freq_gain, freq_bias, s, factor, scale, width
        )
        every = exchange(sums)
        if s == 0:
            gate(every)
            conv_parts = finish(conv_steps)
        mixed_low, back, sums_2 = grad_mixed(
            q, normed, item["mi_2"], every, freq_gain, s, freq_kernel, place, point_totals
        )
        others = shared(back)
        if s > 0:
            conv_back, patches = conv_backward(low, above, beside, place, unit, *kernels[s], f32 if s > 0 else bf16)
            grads = kernel_grads()
            totals[s] = [owned_apart(grad) for grad in grads]
            for steps in totals[s]:
                advance(steps)
        else:
            grads = (*grads, freq_grads(item["real"], item["imag"], mixed_low, own_out, pad))
            if alike:
                last_steps = [owned(grads, here)]
            else:
                last_steps = [owned(grads[:1], here), owned(grads[1:], here)]
            for steps in last_steps:
                advance(steps)
        if s == sections - 1:
            out_steps = from_tile(out, rounds, place, here)
            advance(out_steps)
        q, sums, normed = inverse_backward(
            inverse, back, others, summed, item["reduced"], item["mi_1"], spec_gain, spec_bias, s, scale, width
        )
        every = exchange(sums)
        if s > 0:
            below = kept[s - 1]
            reduced_low, q_3, sums, sums_1 = grad_reduced(
                q, normed, item["mi_1"], every, spec_gain, s, reduce_kernel, cell_total,
                conv_back, below["both"], below["mi_3"], out_gain, out_bias, width,
            )
            if s > 1:
                totals[s].append(owned_apart(jnp.concatenate(late_grads(item), axis=1)))
                advance(totals[s][-1])
        else:
            for steps in last_steps:
                advance(steps)
            reduced_low, sums_1 = grad_last(q, normed, item["mi_1"], every, spec_gain, s, cell_total)
        norm_sums[s] = (sums_1, sums_2, sums_3)

    if sections == 1:
        out_parts = finish(out_steps)
    end = lax.all_to_all(reduced_low.reshape(4, -1, half), ("k", "z"), 0, 0, tiled=True) if e_n == 1 else None
    land_out, port_out = join_halves(*out_parts, (land, port), place)
    if e_n == 1:
        mine, theirs = from_line(end, place)
        end_parts = mine, lax.ppermute(theirs, "c", SWAP)
    else:
        end_parts = finish(from_tile(reduced_low, rounds, place, here))
    reduce_grad = reduce_grads(kept[0]["low"], reduced_low, narrow, own_out, pad)
    reduce_grad = lax.all_to_all(reduce_grad.reshape(devices, pad, half), ALL, 0, 0, tiled=True)
    for steps in last_steps:
        advance(steps)
    for steps in last_steps:
        advance(steps)
    packed_sums = pack_sums([item for s in range(sections) for item in norm_sums[s]])
    other_sums = lax.ppermute(packed_sums, "k", SWAP)
    land_grad, port_grad = input_grad((cot_land, cot_port), conv_parts, end_parts, small[1], place)
    totals[0] = [finish(steps) for steps in last_steps] + [total_of([reduce_grad])]
    rest = results(totals, packed_sums, other_sums, own_in, own_out, narrow, half, channels, alike)
    return (land_out, port_out, land_grad, port_grad, *rest)


def solution(mesh):
    f_n, s_n = mesh.shape["fsdp"], mesh.shape["sp"]
    e_n = s_n // 4
    fine = Mesh(np.asarray(mesh.devices).reshape(f_n // 2, 2, 2, 2, e_n), ALL)
    maps = P(("g", "c"), ("k", "z", "e"), None, None)
    split = ALL

    def whole(*args):
        land, port = args[0], args[1]
        plan = (
            routes(e_n),
            *transform_tables(e_n, land.shape[1:3], port.shape[1:3]),
        )
        weights = (
            P(None, None, split, None),
            P(None, None, None, split),
            P(None, split, None),
            P(None, split, None),
            P(None, None, split),
        )
        return jax.shard_map(
            lambda *local: per_device(plan, *local),
            mesh=fine,
            in_specs=(maps, maps, *weights, P(), P(), P(), P(), P(), P(), maps, maps),
            out_specs=(maps, maps, maps, maps, *weights, P(), P(), P(), P(), P(), P()),
            check_vma=False,
        )(*args)

    return whole
```

```python
import math

import jax
import jax.numpy as jnp
import numpy as np
from jax import lax
from jax.experimental import pallas as pl
from jax.experimental.pallas import tpu as pltpu
from jax.sharding import Mesh, PartitionSpec as P

EPS = 1e-05
LINE = ("c", "k", "z", "e")
KIND = ("g", "c", "z", "e")
PART = ("c", "e")
ALL = ("g", "c", "k", "z", "e")
f32 = jnp.float32
bf16 = jnp.bfloat16


def routes(e_n):
    s_n = 4 * e_n
    count = 2 * s_n
    left = []
    for c in range(2):
        for s in range(s_n):
            for unit in range(4):
                kind, half = unit // 2, unit % 2
                left.append((c * s_n + s, unit, half * s_n + (kind * 2 + c) * e_n + s // 4, s % 4))
    rounds = []
    for _ in range(4):
        owner = {}

        def augment(src, seen):
            for edge in left:
                if edge[0] == src and edge[2] not in seen:
                    seen.add(edge[2])
                    if edge[2] not in owner or augment(owner[edge[2]][0], seen):
                        owner[edge[2]] = edge
                        return True
            return False

        for src in range(count):
            assert augment(src, set())
        chosen = list(owner.values())
        for edge in chosen:
            left.remove(edge)
        sent = np.zeros(count, np.int32)
        slot = np.zeros(count, np.int32)
        for edge in chosen:
            sent[edge[0]] = edge[1]
            slot[edge[2]] = edge[3]
        rounds.append(([(edge[0], edge[2]) for edge in chosen], sent, slot))
    return rounds


def transform_tables(e_n, land_shape, port_shape):
    parts = 2 * e_n
    shapes = (land_shape, port_shape)
    most = max(rows * (cols // 2 + 1) for rows, cols in shapes)
    per_part = -(-most // (16 * parts)) * 16
    forward, inverse, weight, counts = [], [], [], []
    for rows, cols in shapes:
        half = cols // 2 + 1
        point = np.arange(per_part * parts)
        valid = point < rows * half
        kr, f = point // half, point % half
        tiles = []
        for part in range(parts):
            c, e = part // e_n, part % e_n
            h = np.arange(rows // e_n) + e * (rows // e_n)
            w = np.arange(cols // 2) + c * (cols // 2)
            tiles.append((np.repeat(h, len(w)), np.tile(w, len(h))))
        cell_h = np.concatenate([tile[0] for tile in tiles])
        cell_w = np.concatenate([tile[1] for tile in tiles])
        size = rows * cols
        phase = (kr[:, None] * cell_h[None, :] * cols + f[:, None] * cell_w[None, :] * rows) % size
        angle = phase * (2.0 * math.pi / size)
        table = np.stack([np.cos(angle), -np.sin(angle)]) * valid[None, :, None]
        table = table.astype(np.float32).astype(jnp.bfloat16)
        cells = size // parts
        factor = np.where((f == 0) | (2 * f == cols), 1.0, 2.0) * valid
        counts.append([int(valid[p * per_part : (p + 1) * per_part].sum()) for p in range(parts)])
        for part in range(parts):
            order = [(part + step) % parts for step in range(parts)]
            own_points = slice(part * per_part, (part + 1) * per_part)
            own_cells = slice(part * cells, (part + 1) * cells)
            forward.append(
                np.concatenate([table[:, own_points, q * cells : (q + 1) * cells] for q in order], axis=2)
            )
            back = np.concatenate([table[:, q * per_part : (q + 1) * per_part, own_cells] for q in order], axis=1)
            inverse.append(np.ascontiguousarray(back.transpose(0, 2, 1)))
            weight.append(factor[own_points].astype(np.float32))
    forward, inverse = (np.stack(item).reshape(len(item), -1, item[0].shape[2]) for item in (forward, inverse))
    wide = max(-(-forward.shape[2] // 128), -(-inverse.shape[2] // 128)) * 128
    forward, inverse = (np.pad(item, ((0, 0), (0, 0), (0, wide - item.shape[2]))) for item in (forward, inverse))
    return np.concatenate([forward, inverse], axis=1), np.stack(weight), np.asarray(counts, np.int32)


SWAP = [(0, 1), (1, 0)]


def pick(table, index):
    return lax.dynamic_index_in_dim(jnp.asarray(table), index, 0, keepdims=False)


def partners(pieces, axes, step):
    count = lax.axis_size(axes)
    return lax.ppermute(pieces, axes, [(i, i ^ step) for i in range(count)])


def split_halves(land, port, place):
    channels = land.shape[3]
    shapes = [maps.shape[1:3] for maps in (land, port)]
    cells = shapes[0][0] * shapes[0][1] // 2

    def body(land_ref, port_ref, place_ref, mine_ref, theirs_ref):
        c = place_ref[1]
        for kind, ref in enumerate((land_ref, port_ref)):
            half = shapes[kind][1] // 2
            for out_ref, core in ((mine_ref, c), (theirs_ref, 1 - c)):
                at = pl.ds(pl.multiple_of(core * half, half), half)
                out_ref[kind] = ref[0, :, at, :].reshape(cells, channels)

    outs = [shape((2, cells, channels), land.dtype)] * 2
    return run(body, outs, (land, port, place), "split_halves", scalars=1)


def join_halves(mine, theirs, like, place):
    def body(mine_ref, theirs_ref, place_ref, *out_refs):
        c = place_ref[1]
        for kind, out_ref in enumerate(out_refs):
            _, rows, cols, channels = out_ref.shape
            half = cols // 2
            for ref, core in ((mine_ref, c), (theirs_ref, 1 - c)):
                at = pl.ds(pl.multiple_of(core * half, half), half)
                out_ref[0, :, at, :] = ref[kind].reshape(rows, half, channels)

    return run(body, [shape(maps.shape, maps.dtype) for maps in like], (mine, theirs, place), "join_halves", scalars=1)


def to_slots(mine, theirs, place):
    def body(mine_ref, theirs_ref, place_ref, *out_refs):
        here, c = place_ref[2], place_ref[1]
        for step, out_ref in enumerate(out_refs):
            there = here ^ step
            kind, core = there // 2, there % 2

            @pl.when(core == c)
            def _():
                out_ref[...] = mine_ref[kind]

            @pl.when(core != c)
            def _():
                out_ref[...] = theirs_ref[kind]

    outs = [shape(mine.shape[1:], mine.dtype)] * 4
    return run(body, outs, (mine, theirs, place), "to_slots", scalars=1)


def from_slots(pieces, place):
    def body(*refs):
        place_ref, mine_ref, theirs_ref = refs[-3:]
        here, c = place_ref[2], place_ref[1]
        for step in range(4):
            there = here ^ step
            kind, core = there // 2, there % 2

            @pl.when(core == c)
            def _():
                mine_ref[kind] = refs[step][...]

            @pl.when(core != c)
            def _():
                theirs_ref[kind] = refs[step][...]

    outs = [shape((2,) + pieces[0].shape, pieces[0].dtype)] * 2
    return run(body, outs, (*pieces, place), "from_slots", scalars=1)


def from_line(blocks, place):
    def body(blocks_ref, place_ref, mine_ref, theirs_ref):
        c = place_ref[1]
        for kind in range(2):
            mine_ref[kind] = blocks_ref[2 * kind + c]
            theirs_ref[kind] = blocks_ref[2 * kind + 1 - c]

    outs = [shape((2,) + blocks.shape[1:], blocks.dtype)] * 2
    return run(body, outs, (blocks, place), "from_line", scalars=1)


def in_order(pieces, here):
    rows = pieces[0].shape[0]

    def body(*refs):
        here_ref, out_ref = refs[-2:]
        for step in range(len(pieces)):
            out_ref[here_ref[0] ^ step] = refs[step][...]

    outs = [shape((len(pieces),) + pieces[0].shape, pieces[0].dtype)]
    out = run(body, outs, (*pieces, here), "in_order", scalars=1)[0]
    return out.reshape((len(pieces) * rows,) + pieces[0].shape[1:])


def for_partners(blocks, here):
    count = blocks.shape[0]

    def body(blocks_ref, here_ref, *out_refs):
        for step in range(count):
            out_refs[step][...] = blocks_ref[here_ref[0] ^ step]

    outs = [shape(blocks.shape[1:], blocks.dtype)] * count
    return run(body, outs, (blocks, here), "for_partners", scalars=1)


def advance(steps):
    return next(steps)


def finish(steps):
    while True:
        try:
            next(steps)
        except StopIteration as stop:
            return stop.value


def over_line(pieces):
    axes = ("k", "z", "e")
    return [pieces[0]] + [partners(pieces[step], axes, step) for step in range(1, lax.axis_size(axes))]


def over_plane(pieces):
    return [pieces[0]] + [partners(pieces[step], "g", step) for step in range(1, lax.axis_size("g"))]


def to_tile(land, port, rounds, place, here):
    channels = land.shape[3]
    if lax.axis_size("e") == 1:
        mine, theirs = split_halves(land, port, place)
        theirs = lax.ppermute(theirs, "c", SWAP)
        yield
        pieces = over_line(to_slots(mine, theirs, place))
        yield
        return in_order(pieces, here[0])
    me = lax.axis_index(LINE)
    units = []
    for maps in (land, port):
        cols = maps.shape[2] // 2
        units += [maps[0, :, :cols].reshape(-1, channels), maps[0, :, cols:].reshape(-1, channels)]
    units = jnp.stack(units)
    got = [lax.ppermute(pick(units, pick(sent, me)), LINE, pairs) for pairs, sent, _ in rounds]
    yield
    slots = np.stack([slot for _, _, slot in rounds], axis=1)
    order = pick(np.argsort(slots, axis=1).astype(np.int32), me)
    yield
    return jnp.concatenate([pick(jnp.stack(got), order[i]) for i in range(4)], axis=0)


def from_tile(tile, rounds, place, here):
    units = tile.reshape(4, -1, tile.shape[1])
    if lax.axis_size("e") == 1:
        pieces = over_line(for_partners(units, here[0]))
        yield
        mine, theirs = from_slots(pieces, place)
        return mine, lax.ppermute(theirs, "c", SWAP)
    me = lax.axis_index(LINE)
    got = [lax.ppermute(pick(units, pick(slot, me)), LINE, [(b, a) for a, b in pairs]) for pairs, _, slot in rounds]
    yield
    sents = np.stack([sent for _, sent, _ in rounds], axis=1)
    order = pick(np.argsort(sents, axis=1).astype(np.int32), me)
    both = jnp.stack([pick(jnp.stack(got), order[i]) for i in range(4)]).reshape((2, 2) + units.shape[1:])
    c = lax.axis_index("c")
    return (
        lax.dynamic_index_in_dim(both, c, 1, keepdims=False),
        lax.dynamic_index_in_dim(both, 1 - c, 1, keepdims=False),
    )


def shared(block):
    parts = lax.axis_size(PART)
    pieces = [
        lax.ppermute(block, PART, [((p + step) % parts, p) for p in range(parts)]) for step in range(1, parts)
    ]
    return pieces[0] if parts == 2 else jnp.concatenate(pieces, axis=0)


def gelu_parts(v):
    k = math.sqrt(2.0 / math.pi)
    square = v * v
    t = jnp.tanh(k * v * (1.0 + 0.044715 * square))
    half = 0.5 * (1.0 + t)
    return v * half, half + 0.5 * v * (1.0 - t * t) * (k * (1.0 + 3.0 * 0.044715 * square))


def gelu(v):
    return 0.5 * v * (1.0 + jnp.tanh(math.sqrt(2.0 / math.pi) * v * (1.0 + 0.044715 * (v * v))))


def dot(a, b):
    return lax.dot_general(a, b, (((1,), (0,)), ((), ())), preferred_element_type=f32)


def dot_t(a, b):
    return lax.dot_general(a, b, (((1,), (1,)), ((), ())), preferred_element_type=f32)


def outer(a, b):
    return lax.dot_general(a, b, (((0,), (0,)), ((), ())), preferred_element_type=f32)


def device_counts(counts, kind, width, e_n, z_n):
    row = lax.broadcasted_iota(jnp.int32, (width, 1), 0)
    part = row // (e_n * z_n) % 2 * e_n + row % e_n
    out = jnp.zeros((width, 1), f32)
    for p in range(len(counts[0])):
        out = jnp.where(part == p, jnp.where(kind == 0, float(counts[0][p]), float(counts[1][p])), out)
    return out


def moments(every, counts, total):
    sums, squares = every[:, 0, :], every[:, 1, :]
    mean = jnp.sum(sums, axis=0, keepdims=True) / total
    apart = sums / counts - mean
    square = jnp.sum(squares + counts * apart * apart, axis=0, keepdims=True)
    return mean, lax.rsqrt(square / total + EPS)


def emit(out_ref, first, second):
    both = jnp.concatenate([first, second], axis=0)
    out_ref[...] = jnp.broadcast_to(both[None], out_ref.shape)


def row_step(rows):
    return next(step for step in (64, 32, 16, 8) if rows % step == 0)


def sweep(rows, body, carry=0, step=None):
    step = step or row_step(rows)
    if rows == step:
        return body(slice(0, rows), carry)
    return lax.fori_loop(0, rows // step, lambda i, carry: body(pl.ds(pl.multiple_of(i * step, step), step), carry), carry)


def folded(values):
    return jnp.sum(values.reshape(values.shape[0] // 8, 8, values.shape[1]), axis=0)


def column(values):
    return jnp.sum(values, axis=0, keepdims=True)


def lanes_of(values, columns):
    return jnp.concatenate([values] * (columns // 128), axis=1)


def emit_moments(out_ref, ref, count, factor_ref=None):
    rows, columns = ref.shape
    zero = jnp.zeros((8, columns), f32)
    local_sum = column(sweep(rows, lambda at, acc: acc + folded(ref[at, :]), zero))
    mean = local_sum / count

    def squares(at, acc):
        centered = ref[at, :] - mean
        if factor_ref is not None:
            centered = jnp.where(lanes_of(factor_ref[at, :], columns) > 0.0, centered, 0.0)
        return acc + folded(centered * centered)

    emit(out_ref, local_sum, column(sweep(rows, squares, zero)))


def pair(columns):
    return jnp.zeros((8, columns), f32), jnp.zeros((8, columns), f32)


def add_sums(sums, q, normed):
    return sums[0] + folded(q), sums[1] + folded(q * normed)


def emit_sums(out_ref, sums):
    emit(out_ref, column(sums[0]), column(sums[1]))


def back_terms(every_ref, total):
    sums = jnp.sum(every_ref[...], axis=0)
    return sums, sums[0:1] / total, sums[1:2] / total


VMEM = pl.BlockSpec(memory_space=pltpu.VMEM)
SMEM = pl.BlockSpec(memory_space=pltpu.SMEM)
ANY = pl.BlockSpec(memory_space=pl.ANY)
HBM = pl.BlockSpec(memory_space=pltpu.HBM)


class Order:
    last = ()


def run(body, outs, ins, name, scratch=(), limit=8, scalars=0):
    vectors = len(ins) - scalars
    waits = len(Order.last)

    def ordered(*refs):
        body(*refs[:vectors], *refs[vectors + waits :])

    result = pl.pallas_call(
        ordered,
        out_shape=outs,
        in_specs=[HBM if item is None else VMEM for item in _spaces(ins[:vectors])] + [ANY] * waits + [SMEM] * scalars,
        out_specs=[VMEM] * len(outs),
        scratch_shapes=list(scratch),
        compiler_params=pltpu.CompilerParams(vmem_limit_bytes=limit * 1024 * 1024),
        name=name,
    )(*[item.array if isinstance(item, InPlace) else item for item in ins[:vectors]], *Order.last, *ins[vectors:])
    Order.last = (min(result, key=lambda item: math.prod(item.shape)),)
    return result


def hold(*arrays):
    Order.last = (*Order.last, *arrays)


def gate(every):
    def body(in_ref, out_ref):
        out_ref[...] = in_ref[0]

    run(body, [shape(every.shape[1:])], (every,), "gate")


class InPlace:
    def __init__(self, array):
        self.array = array


def _spaces(items):
    return [None if isinstance(item, InPlace) else item for item in items]


def shape(dims, kind=f32):
    return jax.ShapeDtypeStruct(tuple(dims), kind)


def reduce_first(x, reduce_kernel, width, narrow):
    cells = x.shape[0]
    half = reduce_kernel.shape[1]

    def body(x_ref, r_ref, reduced_ref, stats_ref):
        reduced_ref[...] = dot(x_ref[:, narrow:], r_ref[...])
        emit_moments(stats_ref, reduced_ref, float(cells))

    return run(body, [shape((cells, half)), shape((width, 2, half))], (x, reduce_kernel), "reduce_first")


def reduce_next(both, every, gain, bias, s, reduce_kernel, narrow, place, unit):
    cells, channels = both.shape
    half = reduce_kernel.shape[1]
    width = every.shape[0]

    def body(both_ref, every_ref, g_ref, b_ref, r_ref, place_ref, low_ref, reduced_ref, stats_ref, mi_ref, edge_ref):
        mean, inv = moments(every_ref[...], float(cells), float(cells * width))
        mi_ref[...] = jnp.concatenate([mean, inv], axis=0)
        gain_row, bias_row = g_ref[s : s + 1], b_ref[s : s + 1]

        def apply(at, carry):
            low_ref[at, :] = gelu((both_ref[at, :] - mean) * inv * gain_row + bias_row).astype(bf16)
            return carry

        sweep(cells, apply, step=32)
        reduced_ref[...] = dot(low_ref[:, narrow:], r_ref[...])
        emit_moments(stats_ref, reduced_ref, float(cells))
        edge_ref[...] = edge_rows(low_ref[...].astype(f32).reshape(-1, unit, channels), (), place_ref, unit)

    outs = [shape((cells, channels), bf16), shape((cells, half)), shape((width, 2, half)), shape((2, channels))]
    outs.append(shape((cells // unit + 4, channels), bf16))
    return run(body, outs, (both, every, gain, bias, reduce_kernel, place), "reduce_next", scalars=1)


def hidden_act(reduced, every, gain, bias, s):
    cells, channels = reduced.shape
    width = every.shape[0]

    def body(v_ref, every_ref, g_ref, b_ref, low_ref, hidden_ref, mi_ref):
        mean, inv = moments(every_ref[...], float(cells), float(cells * width))
        mi_ref[...] = jnp.concatenate([mean, inv], axis=0)
        gain_row, bias_row = g_ref[s : s + 1], b_ref[s : s + 1]

        def apply(at, carry):
            act = gelu((v_ref[at, :] - mean) * inv * gain_row + bias_row)
            hidden_ref[at, :] = act
            low_ref[at, :] = act.astype(bf16)
            return carry

        sweep(cells, apply)

    outs = [shape((cells, channels), bf16), shape((cells, channels)), shape((2, channels))]
    return run(body, outs, (reduced, every, gain, bias), "hidden_act")


def freq_act(mixed, every, gain, bias, s, factor, place, counts, e_n, z_n):
    points, channels = mixed.shape
    width = every.shape[0]

    def body(v_ref, every_ref, g_ref, b_ref, factor_ref, place_ref, low_ref, mi_ref):
        by_device = device_counts(counts, place_ref[0], width, e_n, z_n)
        mean, inv = moments(every_ref[...], by_device, jnp.sum(by_device))
        mi_ref[...] = jnp.concatenate([mean, inv], axis=0)
        gain_row, bias_row = g_ref[s : s + 1], b_ref[s : s + 1]

        def apply(at, carry):
            act = gelu((v_ref[at, :] - mean) * inv * gain_row + bias_row)
            low_ref[at, :] = (act * lanes_of(factor_ref[at, :], channels)).astype(bf16)
            return carry

        sweep(points, apply)

    outs = [shape((points, channels), bf16), shape((2, channels))]
    return run(body, outs, (mixed, every, gain, bias, factor, place), "freq_act", scalars=1)


def blocks_of(rows, most):
    count = -(-rows // most)
    while rows % (16 * count):
        count += 1
    return [slice(i * rows // count, (i + 1) * rows // count) for i in range(count)]


def spectrum_forward(table, own, others, freq_kernel, factor, scale, width):
    points = table.shape[1]
    cells, half = own.shape
    wide = freq_kernel.shape[1]

    def body(t_ref, own_ref, others_ref, w_ref, factor_ref, real_ref, imag_ref, mixed_ref, stats_ref):
        for side, out_ref in enumerate((real_ref, imag_ref)):
            for at in blocks_of(points, 272):
                z = dot(t_ref[side, at, :cells], own_ref[...]) + dot(t_ref[side, at, cells:], others_ref[...])
                out_ref[at, :] = (z * scale).astype(bf16)
        mixed_ref[...] = dot(real_ref[...], w_ref[:half]) + dot(imag_ref[...], w_ref[half:])
        count = jnp.sum(jnp.where(factor_ref[:, :1] > 0.0, 1.0, 0.0))
        emit_moments(stats_ref, mixed_ref, count, factor_ref)

    outs = [shape((points, half), bf16), shape((points, half), bf16), shape((points, wide)), shape((width, 2, wide))]
    return run(body, outs, (table, own, others, freq_kernel, factor), "spectrum_forward")


def inverse_forward(table, own, others, hidden, pre, expand_t, scale, width):
    cells = table.shape[1]
    half = hidden.shape[1]
    channels = pre.shape[1]
    narrow = channels - expand_t.shape[0]

    def body(t_ref, own_ref, others_ref, hidden_ref, pre_ref, e_ref, summed_ref, both_ref, stats_ref):
        freq = jnp.concatenate([own_ref[...], others_ref[...]], axis=0)
        real, imag = freq[:, :half], freq[:, half:]
        total = freq.shape[0]
        for at in blocks_of(cells, 256):
            returned = dot(t_ref[0, at, :total], real) + dot(t_ref[1, at, :total], imag)
            summed_ref[at, :] = (hidden_ref[at, :] + returned * scale).astype(bf16)
        both_ref[:, :narrow] = pre_ref[:, :narrow]
        for at in blocks_of(cells, 256):
            both_ref[at, narrow:] = pre_ref[at, narrow:] + dot_t(summed_ref[at, :], e_ref[...])
        emit_moments(stats_ref, both_ref, float(cells))

    outs = [shape((cells, half), bf16), shape((cells, channels)), shape((width, 2, channels))]
    return run(body, outs, (table, own, others, hidden, pre, expand_t), "inverse_forward")


def turn(both, every, gain, bias, s, x, cot):
    cells, channels = both.shape

    width = every.shape[0]

    def body(both_ref, every_ref, g_ref, b_ref, x_ref, cot_ref, out_ref, q_ref, sums_ref, mi_ref):
        mean, inv = moments(every_ref[...], float(cells), float(cells * width))
        mi_ref[...] = jnp.concatenate([mean, inv], axis=0)
        gain_row, bias_row = g_ref[s : s + 1], b_ref[s : s + 1]

        def apply(at, sums):
            normed = (both_ref[at, :] - mean) * inv
            state, slope = gelu_parts(normed * gain_row + bias_row)
            out_ref[at, :] = (x_ref[at, :].astype(f32) + state).astype(bf16)
            q = slope * cot_ref[at, :].astype(f32)
            q_ref[at, :] = q
            return add_sums(sums, q, normed)

        emit_sums(sums_ref, sweep(cells, apply, pair(channels), step=32))

    outs = [shape((cells, channels), bf16), shape((cells, channels)), shape((width, 2, channels)), shape((2, channels))]
    return run(body, outs, (both, every, gain, bias, x, cot), "turn")


def grad_pre(q, both, mi, every, gain, s, expand_t, total, place, unit):
    cells, channels = both.shape
    broad, half = expand_t.shape
    narrow = channels - broad

    def body(q_ref, both_ref, mi_ref, every_ref, g_ref, e_ref, place_ref, *refs):
        low_ref, summed_ref, summed_low_ref, sums_ref, edge_ref = refs
        sums, bias_term, gain_term = back_terms(every_ref, total)
        sums_ref[...] = sums
        mean, inv = mi_ref[0:1], mi_ref[1:2]
        gain_row = g_ref[s : s + 1] * inv

        def apply(at, carry):
            normed = (both_ref[at, :] - mean) * inv
            low_ref[at, :] = (gain_row * (q_ref[at, :] - bias_term - normed * gain_term)).astype(bf16)
            return carry

        sweep(cells, apply, step=32)
        summed_ref[...] = dot(low_ref[:, narrow:], e_ref[...])
        summed_low_ref[...] = summed_ref[...].astype(bf16)
        edge_ref[...] = edge_rows(low_ref[...].astype(f32).reshape(-1, unit, channels), (), place_ref, unit)

    outs = [shape((cells, channels), bf16), shape((cells, half)), shape((cells, half), bf16), shape((2, channels))]
    outs.append(shape((cells // unit + 4, channels), bf16))
    return run(body, outs, (q, both, mi, every, gain, expand_t, place), "grad_pre", scalars=1)


def spectrum_backward(table, own, others, mixed, mi, gain, bias, s, factor, scale, width):
    points, wide = mixed.shape
    cells, half = own.shape

    def body(t_ref, own_ref, others_ref, mixed_ref, mi_ref, g_ref, b_ref, factor_ref, *refs):
        q_ref, sums_ref, n_ref = refs
        mean, inv = mi_ref[0:1], mi_ref[1:2]
        gain_row, bias_row = g_ref[s : s + 1], b_ref[s : s + 1]
        for side in range(2):
            for at in blocks_of(points, 272):
                z = dot(t_ref[side, at, :cells], own_ref[...]) + dot(t_ref[side, at, cells:], others_ref[...])
                q_ref[at, side * half : (side + 1) * half] = z * scale

        def apply(at, sums):
            normed = (mixed_ref[at, :] - mean) * inv
            q = gelu_parts(normed * gain_row + bias_row)[1] * (q_ref[at, :] * lanes_of(factor_ref[at, :], wide))
            q_ref[at, :] = q
            n_ref[at, :] = normed
            return add_sums(sums, q, normed)

        emit_sums(sums_ref, sweep(points, apply, pair(wide)))

    outs = [shape((points, wide)), shape((width, 2, wide)), shape((points, wide))]
    return run(body, outs, (table, own, others, mixed, mi, gain, bias, factor), "spectrum_backward")


def norm_low(low_ref, q_ref, n_ref, mi_ref, gain_row, bias_term, gain_term):
    gain_row = gain_row * mi_ref[1:2]

    def apply(at, carry):
        low_ref[at, :] = (gain_row * (q_ref[at, :] - bias_term - n_ref[at, :] * gain_term)).astype(bf16)
        return carry

    sweep(q_ref.shape[0], apply)


def grad_mixed(q, normed, mi, every, gain, s, freq_kernel, place, totals):
    points, wide = q.shape

    def body(q_ref, n_ref, mi_ref, every_ref, g_ref, w_ref, place_ref, low_ref, back_ref, sums_ref):
        total = jnp.where(place_ref[0] == 0, float(totals[0]), float(totals[1]))
        sums, bias_term, gain_term = back_terms(every_ref, total)
        sums_ref[...] = sums
        norm_low(low_ref, q_ref, n_ref, mi_ref, g_ref[s : s + 1], bias_term, gain_term)
        back_ref[...] = dot_t(low_ref[...], w_ref[...]).astype(bf16)

    outs = [shape((points, wide), bf16), shape((points, wide), bf16), shape((2, wide))]
    return run(body, outs, (q, normed, mi, every, gain, freq_kernel, place), "grad_mixed", scalars=1)


def inverse_backward(table, own, others, summed, reduced, mi, gain, bias, s, scale, width):
    cells = table.shape[1]
    half = summed.shape[1]

    def body(t_ref, own_ref, others_ref, summed_ref, reduced_ref, mi_ref, g_ref, b_ref, *refs):
        q_ref, sums_ref, n_ref = refs
        mean, inv = mi_ref[0:1], mi_ref[1:2]
        gain_row, bias_row = g_ref[s : s + 1], b_ref[s : s + 1]
        freq = jnp.concatenate([own_ref[...], others_ref[...]], axis=0)
        real, imag = freq[:, :half], freq[:, half:]
        total = freq.shape[0]
        for at in blocks_of(cells, 256):
            back = dot(t_ref[0, at, :total], real) + dot(t_ref[1, at, :total], imag)
            q_ref[at, :] = summed_ref[at, :] + back * scale

        def apply(at, sums):
            normed = (reduced_ref[at, :] - mean) * inv
            q = gelu_parts(normed * gain_row + bias_row)[1] * q_ref[at, :]
            q_ref[at, :] = q
            n_ref[at, :] = normed
            return add_sums(sums, q, normed)

        emit_sums(sums_ref, sweep(cells, apply, pair(half)))

    outs = [shape((cells, half)), shape((width, 2, half)), shape((cells, half))]
    return run(body, outs, (table, own, others, summed, reduced, mi, gain, bias), "inverse_backward")


def grad_reduced(q, normed, mi, every, gain, s, reduce_kernel, total, conv_back, both, mi_3, gain_3, bias_3, width):
    cells, half = q.shape
    channels = both.shape[1]
    narrow = channels - reduce_kernel.shape[0]

    def body(q_ref, n_ref, mi_ref, every_ref, g_ref, r_ref, conv_ref, both_ref, mi3_ref, g3_ref, b3_ref, *refs):
        low_ref, out_ref, sums3_ref, sums_ref = refs
        sums, bias_term, gain_term = back_terms(every_ref, total)
        sums_ref[...] = sums
        norm_low(low_ref, q_ref, n_ref, mi_ref, g_ref[s : s + 1], bias_term, gain_term)
        out_ref[:, :narrow] = conv_ref[:, :narrow]
        for at in blocks_of(cells, 256):
            out_ref[at, narrow:] = conv_ref[at, narrow:] + dot_t(low_ref[at, :], r_ref[...])
        mean, inv = mi3_ref[0:1], mi3_ref[1:2]
        gain_row, bias_row = g3_ref[s - 1 : s], b3_ref[s - 1 : s]

        def apply(at, sums):
            normed_3 = (both_ref[at, :] - mean) * inv
            grad = gelu_parts(normed_3 * gain_row + bias_row)[1] * out_ref[at, :]
            out_ref[at, :] = grad
            return add_sums(sums, grad, normed_3)

        emit_sums(sums3_ref, sweep(cells, apply, pair(channels), step=32))

    outs = [shape((cells, half), bf16), shape((cells, channels)), shape((width, 2, channels)), shape((2, half))]
    ins = (q, normed, mi, every, gain, reduce_kernel, conv_back, both, mi_3, gain_3, bias_3)
    return run(body, outs, ins, "grad_reduced")


def grad_last(q, normed, mi, every, gain, s, total):
    cells, half = q.shape

    def body(q_ref, n_ref, mi_ref, every_ref, g_ref, *refs):
        low_ref, sums_ref = refs
        sums, bias_term, gain_term = back_terms(every_ref, total)
        sums_ref[...] = sums
        norm_low(low_ref, q_ref, n_ref, mi_ref, g_ref[s : s + 1], bias_term, gain_term)

    outs = [shape((cells, half), bf16), shape((2, half))]
    return run(body, outs, (q, normed, mi, every, gain), "grad_last")


def input_grad(cots, conv, late, reduce_kernel, place):
    channels = cots[0].shape[3]
    narrow = channels - reduce_kernel.shape[0]

    def body(cot0_ref, cot1_ref, *refs):
        conv_refs, late_refs, (r_ref, place_ref), out_refs = refs[:2], refs[2:4], refs[4:6], refs[6:]
        c = place_ref[1]
        for kind, (cot_ref, out_ref) in enumerate(zip((cot0_ref, cot1_ref), out_refs)):
            _, rows, cols, _ = cot_ref.shape
            half = cols // 2
            for side, core in enumerate((c, 1 - c)):
                at = pl.ds(pl.multiple_of(core * half, half), half)
                into = dot_t(late_refs[side][kind], r_ref[...]).reshape(rows, half, channels - narrow)
                base = conv_refs[side][kind].astype(f32).reshape(rows, half, channels) + cot_ref[0, :, at, :].astype(f32)
                out_ref[0, :, at, :narrow] = base[..., :narrow].astype(bf16)
                out_ref[0, :, at, narrow:] = (base[..., narrow:] + into).astype(bf16)

    outs = [shape(cot.shape, bf16) for cot in cots]
    ins = (*cots, *conv, *late, reduce_kernel, place)
    return run(body, outs, ins, "input_grad", limit=12, scalars=1)


def edge_rows(ends, above, place_ref, unit):
    first, last = ends[:, 0], ends[:, unit - 1]
    if not above:
        zeros = jnp.zeros((2, ends.shape[2]), f32)
        first, last = (jnp.concatenate([zeros, item, zeros], axis=0) for item in (first, last))
    land, left = place_ref[0] == 0, place_ref[1] == 0
    last = jnp.where(land, jnp.concatenate([last[1:], last[:1]], axis=0), last)
    first = jnp.where(land, jnp.concatenate([first[-1:], first[:-1]], axis=0), first)
    return jnp.where(left, last, first).astype(bf16)


def edge_cells(low, above, place, unit):
    channels = low.shape[1]
    blocks = low.shape[0] // unit + 4
    above = above or ()

    def body(*refs):
        *tile_refs, place_ref, out_ref = refs
        if above:
            wide = jnp.concatenate([tile_refs[1][...], tile_refs[0][...], tile_refs[2][...]], axis=0)
        else:
            wide = tile_refs[0][...]
        out_ref[...] = edge_rows(wide.astype(f32).reshape(-1, unit, channels), above, place_ref, unit)

    return run(body, [shape((blocks, channels), bf16)], (low, *above, place), "edge_cells", scalars=1)[0]


def surroundings(low, place, unit, edge=None):
    e_n = lax.axis_size("e")
    above = None
    if e_n > 1:
        ahead = [(e, e + 1) for e in range(e_n - 1)]
        above = (
            lax.ppermute(low[-2 * unit :], "e", ahead),
            lax.ppermute(low[: 2 * unit], "e", [(b, a) for a, b in ahead]),
        )
    if edge is None or above:
        edge = edge_cells(low, above, place, unit)
    return above, lax.ppermute(edge, "c", SWAP)


def shifted_columns(x_ref, above_refs, beside_ref, land, left, out_ref, unit):
    cells, channels = x_ref.shape
    blocks = cells // unit + 4
    block = lax.broadcasted_iota(jnp.int32, (blocks, unit, 1), 0)
    cell = lax.broadcasted_iota(jnp.int32, (blocks, unit, 1), 1)
    for lane in range(0, channels, 128):
        at = slice(lane, lane + 128)
        if above_refs:
            top, bottom = above_refs[0][:, at], above_refs[1][:, at]
        else:
            top = bottom = jnp.zeros((2 * unit, 128), bf16)
        wide = jnp.concatenate([top, x_ref[:, at], bottom], axis=0)
        out_ref[1, :, at] = wide
        wide = wide.astype(f32)
        beside = beside_ref[:, at].astype(f32)[:, None, :]
        for j, edge, odd in ((0, 0, 0), (2, unit - 1, 1)):
            moved = pltpu.roll(wide, 1 if j == 0 else blocks * unit - 1, 0).reshape(blocks, unit, 128)
            outer_side = (cell == edge) & (jnp.logical_not(land) | (block % 2 == odd))
            fill = jnp.where(left if j == 2 else jnp.logical_not(left), beside, 0.0)
            out_ref[j, :, at] = jnp.where(outer_side, fill, moved).reshape(blocks * unit, 128).astype(bf16)


def rows_at(i, first, count, land, unit):
    if i == 1:
        return slice(2 * unit + first, 2 * unit + first + count)
    step = jnp.where(land, 2 * unit, unit)
    return pl.ds(pl.multiple_of(2 * unit + first + (i - 1) * step, unit), count)


def conv_forward(low, above, beside, place, unit, local_kernel, global_t):
    cells, channels = low.shape
    narrow = local_kernel.shape[1] // 9
    padded = cells + 4 * unit
    extra = () if above is None else above
    start = 4 + len(extra)

    def body(*refs):
        x_ref, beside_ref, l_ref, g_ref = refs[0], *refs[1 + len(extra) : 4 + len(extra)]
        place_ref, pre_ref, cols_ref, wide_ref = refs[start:]
        land, left = place_ref[0] == 0, place_ref[1] == 0
        shifted_columns(x_ref, refs[1 : 1 + len(extra)], beside_ref, land, left, wide_ref, unit)
        cols_ref[...] = wide_ref[:, :, :narrow]
        for at in blocks_of(cells, 512):
            count = at.stop - at.start
            local = jnp.zeros((count, narrow), f32)
            patches = []
            for t in range(9):
                block = wide_ref[t % 3, rows_at(t // 3, at.start, count, land, unit), :]
                local = local + dot(block, l_ref[:, t * narrow : (t + 1) * narrow])
                patches.append(block[:, :narrow])
            pre_ref[at, :narrow] = local
            pre_ref[at, narrow:] = dot_t(jnp.concatenate(patches, axis=1), g_ref[...])

    outs = [shape((cells, channels)), shape((3, padded, narrow), bf16)]
    ins = (low, *extra, beside, local_kernel, global_t, place)
    return run(body, outs, ins, "conv_forward", [pltpu.VMEM((3, padded, channels), bf16)], 12, 1)


def conv_backward(low, above, beside, place, unit, local_kernel, global_t, kind):
    cells, channels = low.shape
    narrow = local_kernel.shape[1] // 9
    padded = cells + 4 * unit
    extra = () if above is None else above
    start = 4 + len(extra)

    def body(*refs):
        x_ref, beside_ref, l_ref, g_ref = refs[0], *refs[1 + len(extra) : 4 + len(extra)]
        place_ref, grad_ref, patches_ref, wide_ref = refs[start:]
        land, left = place_ref[0] == 0, place_ref[1] == 0
        shifted_columns(x_ref, refs[1 : 1 + len(extra)], beside_ref, land, left, wide_ref, unit)
        for at in blocks_of(cells, 512):
            count = at.stop - at.start
            into = jnp.zeros((count, narrow), f32)
            for t in range(9):
                block = wide_ref[2 - t % 3, rows_at(2 - t // 3, at.start, count, land, unit), :]
                patches_ref[at, t * narrow : (t + 1) * narrow] = block[:, :narrow]
                into = into + dot(block[:, narrow:], g_ref[:, t * narrow : (t + 1) * narrow])
            grad = dot_t(patches_ref[at, :], l_ref[...])
            grad_ref[at, :narrow] = (grad[:, :narrow] + into).astype(kind)
            grad_ref[at, narrow:] = grad[:, narrow:].astype(kind)

    outs = [shape((cells, channels), kind), shape((cells, 9 * narrow), bf16)]
    ins = (low, *extra, beside, local_kernel, global_t, place)
    return run(body, outs, ins, "conv_backward", [pltpu.VMEM((3, padded, channels), bf16)], 12, 1)


def spaced(rows, own, pad):
    row = lax.broadcasted_iota(jnp.int32, (rows, rows // own * pad), 0)
    place = lax.broadcasted_iota(jnp.int32, (rows, rows // own * pad), 1)
    return jnp.where(place == row // own * pad + row % own, 1.0, 0.0).astype(bf16)


def copies(values, count):
    def body(in_ref, out_ref):
        for i in range(count):
            out_ref[i] = in_ref[...]

    return run(body, [shape((count,) + values.shape, values.dtype)], (values,), "copies")[0]


def unpack_small(blocks, own, half):
    pad, columns = blocks.shape[-2:]
    devices = math.prod(blocks.shape[:-2])
    wide = columns - 2 * half

    def body(full_ref, *out_refs):
        split_small(full_ref[...].reshape(devices * pad, columns), spaced(devices * own, own, pad), wide, half, out_refs)

    outs = [shape((devices * own, width), bf16) for width in (wide, half, half)]
    return run(body, outs, (blocks,), "unpack_small", limit=12)


def split_small(full, place, wide, half, out_refs):
    full = dot(place, full).astype(bf16)
    out_refs[0][...] = full[:, :wide]
    out_refs[1][...] = full[:, wide : wide + half]
    out_refs[2][...] = full[:, wide + half : wide + 2 * half]


def unpack_kernels(full, sections, own_in, pad_in, own_out, half):
    devices, rows, columns = full.shape
    pad = (rows - sections * pad_in) // (2 * sections - 1)
    plain = own_in == pad_in
    wide = devices * own_out
    each = pad_in + pad

    def body(full_ref, *refs):
        out_refs, small_refs = refs[: 2 * sections], refs[2 * sections : 5 * sections - 3]
        local_ref, global_ref, small_ref, sems = refs[5 * sections - 3 :]
        copies = []
        for s in range(sections):
            target = out_refs[2 * s] if plain else local_ref.at[s]
            sources = [(s * each, pad_in, target), (s * each + pad_in, pad, global_ref.at[s])]
            if s:
                sources.append((sections * each + (s - 1) * pad, pad, small_ref.at[s - 1]))
            for k, (first, count, target) in enumerate(sources):
                source = full_ref.at[:, pl.ds(first, count), :]
                copies.append(pltpu.make_async_copy(source, target, sems.at[s, k]))
        for copy in copies:
            copy.start()
        for copy in copies:
            copy.wait()
        place = spaced(devices * own_out, own_out, pad)
        for s in range(sections):
            if not plain:
                block = local_ref[s].reshape(devices * pad_in, columns)
                out_refs[2 * s][...] = dot(spaced(devices * own_in, own_in, pad_in), block).astype(bf16)
            out_refs[2 * s + 1][...] = dot(place, global_ref[s].reshape(devices * pad, columns)).astype(bf16)
            if s:
                block = small_ref[s - 1].reshape(devices * pad, columns)
                split_small(block, place, wide, half, small_refs[3 * s - 3 : 3 * s])

    local = (devices, pad_in, columns) if plain else (devices * own_in, columns)
    outs = [shape(dims, bf16) for dims in (local, (devices * own_out, columns))] * sections
    outs += [shape((devices * own_out, width), bf16) for width in (wide, half, half)] * (sections - 1)
    scratch = [
        pltpu.VMEM((8,) * 4 if plain else (sections, devices, pad_in, columns), bf16),
        pltpu.VMEM((sections, devices, pad, columns), bf16),
        pltpu.VMEM((max(sections - 1, 1), devices, pad, columns), bf16),
        pltpu.SemaphoreType.DMA((sections, 3)),
    ]
    limit = 44 if plain else 52
    out = run(body, outs, (InPlace(full),), "unpack_kernels", scratch, limit)
    kernels = [(out[2 * s].reshape(devices * own_in, columns), out[2 * s + 1]) for s in range(sections)]
    return kernels, out[2 * sections :]


def early_grads(x_low, patches, grad_low, shifted, summed, place, unit, own, pad, alike):
    cells, channels = x_low.shape
    narrow = shifted.shape[2]
    broad = channels - narrow
    half = summed.shape[1]
    wide = 9 * narrow

    def body(x_ref, p_ref, g_ref, s_ref, m_ref, place_ref, *out_refs):
        land = place_ref[0] == 0
        out_refs[-1][...] = jnp.zeros((8, 128), f32)
        local_ref, other_ref, first = (out_refs[0], out_refs[0], wide) if alike else (*out_refs[:2], 0)
        for i in range(3):
            at = slice(3 * i * narrow, 3 * (i + 1) * narrow)
            local_ref[:, at] = outer(x_ref[...], p_ref[:, at]).astype(bf16)
        grad = dot(g_ref[:, narrow:], spaced(broad, own, pad)).astype(bf16)
        for i in range(3):
            taps = [s_ref[j, rows_at(i, 0, cells, land, unit), :] for j in range(3)]
            at = slice(first + 3 * i * narrow, first + 3 * (i + 1) * narrow)
            other_ref[:, at] = outer(grad, jnp.concatenate(taps, axis=1)).astype(bf16)
        other_ref[:, first + wide :] = outer(grad, m_ref[...]).astype(bf16)

    padded = broad // own * pad
    if alike:
        outs = [shape((channels, 2 * wide + half), bf16)]
    else:
        outs = [shape((channels, wide), bf16), shape((padded, wide + half), bf16)]
    outs.append(shape((8, 128)))
    ins = (x_low, patches, grad_low, shifted, summed, place)
    return run(body, outs, ins, "early_grads", limit=12, scalars=1)[:-1]


def freq_grads(real, imag, mixed_low, own, pad):
    wide = mixed_low.shape[1]

    def body(real_ref, imag_ref, m_ref, out_ref):
        freq = jnp.concatenate([outer(real_ref[...], m_ref[...]), outer(imag_ref[...], m_ref[...])], axis=0)
        out_ref[...] = outer(spaced(wide, own, pad), freq.astype(bf16)).astype(bf16)

    return run(body, [shape((wide // own * pad, wide), bf16)], (real, imag, mixed_low), "freq_grads")[0]


def reduce_grads(x_low, reduced_low, narrow, own, pad):
    broad = x_low.shape[1] - narrow

    def body(x_ref, r_ref, out_ref):
        reduce = outer(x_ref[:, narrow:], r_ref[...])
        out_ref[...] = outer(spaced(broad, own, pad), reduce.astype(bf16)).astype(bf16)

    outs = [shape((broad // own * pad, reduced_low.shape[1]), bf16)]
    return run(body, outs, (x_low, reduced_low), "reduce_grads")[0]


def core_parts(shares, here, g_n):
    parts = [part.reshape((g_n, 2, -1) + part.shape[1:]) for part in shares]
    rows, widths = parts[0].shape[2], [part.shape[3] for part in parts]
    starts = [sum(widths[:i]) for i in range(len(widths) + 1)]

    def body(*refs):
        c = refs[len(parts)][0]
        theirs_ref, mine_ref = refs[len(parts) + 1 :]
        for i, ref in enumerate(refs[: len(parts)]):
            at = slice(starts[i], starts[i + 1])
            for g in range(g_n):
                theirs_ref[g, :, at] = ref[g, 1 - c]
                mine_ref[g, :, at] = ref[g, c]

    outs = [shape((g_n, rows, starts[-1]), bf16)] * 2
    return run(body, outs, (*parts, here[2]), "core_parts", scalars=1)


def add_parts(mine, theirs, here):
    g_n = mine.shape[0]

    def body(mine_ref, theirs_ref, *refs):
        for step in range(g_n):
            g = refs[0][0] ^ step
            total = mine_ref[g].astype(f32) + theirs_ref[g].astype(f32)
            refs[1 + step][...] = total if step == 0 else total.astype(bf16)

    outs = [shape(mine.shape[1:], f32 if step == 0 else bf16) for step in range(g_n)]
    return run(body, outs, (mine, theirs, here[1]), "add_parts", scalars=1)


def add_plane(pieces, here, line_n):
    rows, columns = pieces[0].shape
    block = rows // line_n

    def body(*refs):
        for i in range(line_n):
            at = slice(i * block, (i + 1) * block)
            total = refs[0][at, :].astype(f32)
            for ref in refs[1:-1]:
                total = total + ref[at, :].astype(f32)
            refs[-1][i] = total.astype(bf16)

    return run(body, [shape((line_n, block, columns), bf16)], pieces, "add_plane")[0]


def owned(shares, here):
    g_n = lax.axis_size("g")
    line = ("k", "z", "e")
    line_n = lax.axis_size(line)
    theirs, mine = core_parts(shares, here, g_n)
    theirs = lax.ppermute(theirs, "c", SWAP)
    yield
    pieces = over_plane(add_parts(mine, theirs, here))
    yield
    sums = add_plane(pieces, here, line_n)
    yield
    if line_n > 4:
        pieces = [lax.all_to_all(sums, line, 0, 0, tiled=True)]
    else:
        pieces = over_line(for_partners(sums, here[0]))
    yield
    return total_of(pieces)


def owned_apart(shares):
    for axes in (("g", "c"), ("k", "z", "e")):
        shares = shares.reshape(lax.axis_size(axes), -1, shares.shape[-1])
        shares = lax.psum_scatter(shares, axes, scatter_dimension=0, tiled=True).reshape(-1, shares.shape[-1])
        if "g" in axes:
            yield
            shares = copies(shares, 1)[0]
    return shares


def total_of(blocks):
    dims = blocks[0].shape[-2:]

    def body(*refs):
        total = jnp.zeros(dims, f32)
        for ref in refs[:-1]:
            for part in [ref[i] for i in range(ref.shape[0])] if len(ref.shape) == 3 else [ref[...]]:
                total = total + part.astype(f32)
        refs[-1][...] = total

    return run(body, [shape(dims)], blocks, "total_of")[0]


def pack_sums(sums):
    widths = [item.shape[1] for item in sums]

    def body(*refs):
        refs[-1][...] = jnp.concatenate([ref[...] for ref in refs[:-1]], axis=1)

    return run(body, [shape((2, sum(widths)))], sums, "pack_sums")[0]


def results(totals, sums, other_sums, own_in, own_out, narrow, half, channels, alike):
    sections = len(totals)
    wides = (9 * narrow, 9 * narrow + half, 2 * half, half)
    flat, where = [], {}
    for s in range(sections):
        if s == 0:
            rest = [(1, 0)] + ([(2, 1), (3, 1)] if sections > 1 else []) + [(2, 0)]
        else:
            rest = [(1, s)]
        parts = [[(0, s), *rest]] if alike else [[(0, s)], rest]
        if s != 1:
            parts.append([(3, s)] if s == 0 else [(2, s), (3, s)])
        assert len(parts) == len(totals[s])
        for group, item in zip(parts, totals[s]):
            start = 0
            for part in group:
                where[part] = (len(flat), start)
                start += wides[part[0]]
            flat.append(item)

    def body(*refs):
        sums_ref, other_ref, local_ref, global_ref, reduce_ref, freq_ref, expand_ref, *norm_refs = refs[len(flat) :]
        for s in range(sections):

            def columns(part, start, count, rows):
                index, first = where[part, s]
                return refs[index][:rows, first + start : first + start + count].astype(f32)

            for t in range(9):
                local_ref[s, t] = columns(0, t * narrow, narrow, own_in)
                global_ref[t, :, s, :] = columns(1, t * narrow, narrow, own_out)
            expand_ref[:, s, :] = columns(1, 9 * narrow, half, own_out)
            freq_ref[:, s, :] = columns(2, 0, 2 * half, own_out)
            reduce_ref[:, s, :] = columns(3, 0, half, own_out)
        both = sums_ref[...] + other_ref[...]
        at = 0
        for s in range(sections):
            for index, wide in enumerate((half, 2 * half, channels)):
                norm_refs[2 * index][s : s + 1, :] = both[1:2, at : at + wide]
                norm_refs[2 * index + 1][s : s + 1, :] = both[0:1, at : at + wide]
                at += wide

    outs = [
        shape((sections, 9, own_in, narrow)),
        shape((9, own_out, sections, narrow)),
        shape((own_out, sections, half)),
        shape((own_out, sections, 2 * half)),
        shape((own_out, sections, half)),
    ]
    outs += [shape((sections, wide)) for wide in (half, half, 2 * half, 2 * half, channels, channels)]
    out = run(body, outs, (*flat, sums, other_sums), "results")
    return (
        out[0],
        jnp.transpose(out[1], (2, 0, 3, 1)),
        jnp.transpose(out[2], (1, 0, 2)),
        jnp.transpose(out[3], (1, 0, 2)),
        jnp.transpose(out[4], (1, 2, 0)),
        *out[5:],
    )


def pick_tables(table, factors, variant, size):
    points, cells = factors.shape[1], size // lax.axis_size(PART)
    columns = -(-points * lax.axis_size(PART) // 128) * 128

    def body(table_ref, factor_ref, v_ref, forward_ref, inverse_ref, out_ref, sems):
        v = v_ref[0]
        copies = []
        for side in range(2):
            source = table_ref.at[v, pl.ds(side * points, points), pl.ds(0, size)]
            copies.append(pltpu.make_async_copy(source, forward_ref.at[side], sems.at[0, side]))
            source = table_ref.at[v, pl.ds(2 * points + side * cells, cells), pl.ds(0, columns)]
            copies.append(pltpu.make_async_copy(source, inverse_ref.at[side], sems.at[1, side]))
        for copy in copies:
            copy.start()
        out_ref[...] = factor_ref[v]
        for copy in copies:
            copy.wait()

    outs = [shape((2, points, size), bf16), shape((2, cells, columns), bf16), shape(factors.shape[1:])]
    ins = (InPlace(table), factors, variant)
    return run(body, outs, ins, "pick_tables", [pltpu.SemaphoreType.DMA((2, 2))], 12, 1)


def per_device(plan, *args):
    (
        land,
        port,
        to_local,
        to_global,
        reduce_weight,
        freq_weight,
        expand_weight,
        spec_gain,
        spec_bias,
        freq_gain,
        freq_bias,
        out_gain,
        out_bias,
        cot_land,
        cot_port,
    ) = args
    rounds, table, weight_table, point_counts = plan
    sections = to_local.shape[0]
    devices = lax.axis_size(ALL)
    own_in = to_local.shape[2]
    own_out = to_global.shape[3]
    pad = -(-own_out // 16) * 16
    narrow = to_local.shape[3]
    channels = own_in * devices
    half = reduce_weight.shape[2]
    unit = port.shape[2] // 2
    k, c, part = lax.axis_index("k"), lax.axis_index("c"), lax.axis_index(PART)
    line_here = lax.axis_index(("k", "z", "e"))
    place = jnp.stack([k, c, line_here]).astype(jnp.int32)
    here = tuple(index.astype(jnp.int32).reshape(1) for index in (line_here, lax.axis_index("g"), c))
    variant = k * lax.axis_size(PART) + part
    g_n, z_n, e_n = lax.axis_size("g"), lax.axis_size("z"), lax.axis_size("e")
    width = lax.axis_size(KIND)

    pad_in = -(-own_in // 16) * 16
    Order.last = ()

    grow = ((0, 0), (0, pad - own_out), (0, 0))
    taps_local = jnp.transpose(to_local, (0, 2, 1, 3)).reshape(sections, own_in, 9 * narrow)
    taps_local = jnp.pad(taps_local, ((0, 0), (0, pad_in - own_in), (0, 0)))
    taps_global = jnp.pad(jnp.transpose(to_global, (0, 3, 1, 2)).reshape(sections, own_out, 9 * narrow), grow)
    packed = jnp.concatenate([freq_weight, reduce_weight, jnp.transpose(expand_weight, (0, 2, 1))], axis=2)
    packed = jnp.pad(packed, grow)
    small = copies(packed[0], lax.axis_size(("k", "z", "e")))
    small = lax.all_to_all(small, ("k", "z", "e"), 0, 0, tiled=True)
    later = jnp.pad(packed[1:], ((0, 0), (0, 0), (0, 9 * narrow - packed.shape[2])))
    taps = jnp.concatenate([taps_local, taps_global], axis=1)
    taps = jnp.concatenate([item.reshape(-1, 9 * narrow) for item in (taps, later)], axis=0)
    taps = lax.all_gather(taps, ALL)
    x_steps = to_tile(land, port, rounds, place, here)
    advance(x_steps)
    advance(x_steps)
    small = copies(small, lax.axis_size(("g", "c")))
    small = lax.all_to_all(small, ("g", "c"), 0, 0, tiled=True)
    variant = variant.reshape(1)
    size = land.shape[1] * land.shape[2] * lax.axis_size(("k", "z", "e"))
    forward, inverse, factor = pick_tables(jnp.asarray(table), jnp.asarray(np.repeat(weight_table[..., None], 128, axis=2)), variant, size)
    small = unpack_small(small, own_out, half)
    x = finish(x_steps)

    cells = x.shape[0]
    scale = 1.0 / math.sqrt(size)
    cell_total = float(g_n * z_n * size)
    point_totals = [int(item.sum()) * g_n * z_n for item in point_counts]

    def exchange(stats):
        every = lax.all_to_all(stats, KIND, 0, 0, tiled=True)
        Order.last = (every,)
        return every

    kept = []
    for s in range(sections):
        freq_kernel, reduce_kernel, expand_t = small[3 * s : 3 * s + 3]
        if s == 0:
            low = x
            reduced, stats = reduce_first(x, reduce_kernel, width, narrow)
        else:
            low, reduced, stats, kept[-1]["mi_3"], edge = reduce_next(
                both, every, out_gain, out_bias, s - 1, reduce_kernel, narrow, place, unit
            )
        every = exchange(stats)
        if s == 1:
            gate(every)
            cot = finish(cot_steps)
        if s == 0:
            cot_steps = to_tile(cot_land, cot_port, rounds, place, here)
            advance(cot_steps)
        else:
            above, beside = surroundings(low, place, unit, edge)
        hidden_low, hidden, mi_1 = hidden_act(reduced, every, spec_gain, spec_bias, s)
        others = shared(hidden_low)
        if s > 0:
            pre, shifted = conv_forward(low, above, beside, place, unit, *kernels[s])
        real, imag, mixed, stats = spectrum_forward(forward, hidden_low, others, freq_kernel, factor, scale, width)
        every = exchange(stats)
        if s == 0:
            above, beside = surroundings(low, place, unit)
            kernels, more = unpack_kernels(taps, sections, own_in, pad_in, own_out, half)
            small = [*small, *more]
            hold(beside)
        freq_low, mi_2 = freq_act(mixed, every, freq_gain, freq_bias, s, factor, place, point_counts, e_n, z_n)
        others = shared(freq_low)
        if s == 0:
            pre, shifted = conv_forward(low, above, beside, place, unit, *kernels[s])
            advance(cot_steps)
        summed, both, stats = inverse_forward(inverse, freq_low, others, hidden, pre, expand_t, scale, width)
        every = exchange(stats)
        kept.append(
            dict(low=low, shifted=shifted, reduced=reduced, mi_1=mi_1, real=real, imag=imag, mixed=mixed, mi_2=mi_2, summed=summed, both=both)
        )
    if sections == 1:
        cot = finish(cot_steps)
    out, q_3, sums, kept[-1]["mi_3"] = turn(both, every, out_gain, out_bias, sections - 1, x, cot)

    alike = own_in == pad

    def late_grads(item):
        return (
            freq_grads(item["real"], item["imag"], mixed_low, own_out, pad),
            reduce_grads(item["low"], reduced_low, narrow, own_out, pad),
        )

    norm_sums = [None] * sections
    totals = [None] * sections
    last_steps = None
    for s in reversed(range(sections)):
        freq_kernel, reduce_kernel, expand_t = small[3 * s : 3 * s + 3]
        item = kept[s]
        every = exchange(sums)
        if s == sections - 2:
            gate(every)
            out_parts = finish(out_steps)
        low, summed, summed_low, sums_3, edge = grad_pre(
            q_3, item["both"], item["mi_3"], every, out_gain, s, expand_t, cell_total, place, unit
        )
        others = shared(summed_low)
        above, beside = surroundings(low, place, unit, edge)

        def kernel_grads():
            return early_grads(
                item["low"], patches, low, item["shifted"], item["summed"], place, unit, own_out, pad, alike
            )

        if s == 0:
            conv_back, patches = conv_backward(low, above, beside, place, unit, *kernels[s], f32 if s > 0 else bf16)
            conv_steps = from_tile(conv_back, rounds, place, here)
            advance(conv_steps)
            grads = kernel_grads()
            if sections > 1:
                grads = (*grads, *late_grads(kept[1]))
        else:
            hold(beside)
        q, sums, normed = spectrum_backward(
            forward, summed_low, others, item["mixed"], item["mi_2"], freq_gain, freq_bias, s, factor, scale, width
        )
        every = exchange(sums)
        if s == 0:
            gate(every)
            conv_parts = finish(conv_steps)
        mixed_low, back, sums_2 = grad_mixed(
            q, normed, item["mi_2"], every, freq_gain, s, freq_kernel, place, point_totals
        )
        others = shared(back)
        if s > 0:
            conv_back, patches = conv_backward(low, above, beside, place, unit, *kernels[s], f32 if s > 0 else bf16)
            grads = kernel_grads()
            totals[s] = [owned_apart(grad) for grad in grads]
            for steps in totals[s]:
                advance(steps)
        else:
            grads = (*grads, freq_grads(item["real"], item["imag"], mixed_low, own_out, pad))
            if alike:
                last_steps = [owned(grads, here)]
            else:
                last_steps = [owned(grads[:1], here), owned(grads[1:], here)]
            for steps in last_steps:
                advance(steps)
        if s == sections - 1:
            out_steps = from_tile(out, rounds, place, here)
            advance(out_steps)
        q, sums, normed = inverse_backward(
            inverse, back, others, summed, item["reduced"], item["mi_1"], spec_gain, spec_bias, s, scale, width
        )
        every = exchange(sums)
        if s > 0:
            below = kept[s - 1]
            reduced_low, q_3, sums, sums_1 = grad_reduced(
                q, normed, item["mi_1"], every, spec_gain, s, reduce_kernel, cell_total,
                conv_back, below["both"], below["mi_3"], out_gain, out_bias, width,
            )
            if s > 1:
                totals[s].append(owned_apart(jnp.concatenate(late_grads(item), axis=1)))
                advance(totals[s][-1])
        else:
            reduced_low, sums_1 = grad_last(q, normed, item["mi_1"], every, spec_gain, s, cell_total)
            for k in range(1, sections):
                totals[k] = [finish(steps) for steps in totals[k]]
            for steps in last_steps:
                advance(steps)
        norm_sums[s] = (sums_1, sums_2, sums_3)

    if sections == 1:
        out_parts = finish(out_steps)
    end = lax.all_to_all(reduced_low.reshape(4, -1, half), ("k", "z"), 0, 0, tiled=True) if e_n == 1 else None
    land_out, port_out = join_halves(*out_parts, (land, port), place)
    if e_n == 1:
        mine, theirs = from_line(end, place)
        end_parts = mine, lax.ppermute(theirs, "c", SWAP)
    else:
        end_parts = finish(from_tile(reduced_low, rounds, place, here))
    reduce_grad = reduce_grads(kept[0]["low"], reduced_low, narrow, own_out, pad)
    reduce_grad = lax.all_to_all(reduce_grad.reshape(devices, pad, half), ALL, 0, 0, tiled=True)
    for steps in last_steps:
        advance(steps)
    for steps in last_steps:
        advance(steps)
    packed_sums = pack_sums([item for s in range(sections) for item in norm_sums[s]])
    other_sums = lax.ppermute(packed_sums, "k", SWAP)
    land_grad, port_grad = input_grad((cot_land, cot_port), conv_parts, end_parts, small[1], place)
    totals[0] = [finish(steps) for steps in last_steps] + [total_of([reduce_grad])]
    rest = results(totals, packed_sums, other_sums, own_in, own_out, narrow, half, channels, alike)
    return (land_out, port_out, land_grad, port_grad, *rest)


def solution(mesh):
    f_n, s_n = mesh.shape["fsdp"], mesh.shape["sp"]
    e_n = s_n // 4
    fine = Mesh(np.asarray(mesh.devices).reshape(f_n // 2, 2, 2, 2, e_n), ALL)
    maps = P(("g", "c"), ("k", "z", "e"), None, None)
    split = ALL

    def whole(*args):
        land, port = args[0], args[1]
        plan = (
            routes(e_n),
            *transform_tables(e_n, land.shape[1:3], port.shape[1:3]),
        )
        weights = (
            P(None, None, split, None),
            P(None, None, None, split),
            P(None, split, None),
            P(None, split, None),
            P(None, None, split),
        )
        return jax.shard_map(
            lambda *local: per_device(plan, *local),
            mesh=fine,
            in_specs=(maps, maps, *weights, P(), P(), P(), P(), P(), P(), maps, maps),
            out_specs=(maps, maps, maps, maps, *weights, P(), P(), P(), P(), P(), P()),
            check_vma=False,
        )(*args)

    return whole
```

```python
import math

import jax
import jax.numpy as jnp
import numpy as np
from jax import lax
from jax.experimental import pallas as pl
from jax.experimental.pallas import tpu as pltpu
from jax.sharding import Mesh, PartitionSpec as P

EPS = 1e-05
LINE = ("c", "k", "z", "e")
KIND = ("g", "c", "z", "e")
PART = ("c", "e")
ALL = ("g", "c", "k", "z", "e")
f32 = jnp.float32
bf16 = jnp.bfloat16


def routes(e_n):
    s_n = 4 * e_n
    count = 2 * s_n
    left = []
    for c in range(2):
        for s in range(s_n):
            for unit in range(4):
                kind, half = unit // 2, unit % 2
                left.append((c * s_n + s, unit, half * s_n + (kind * 2 + c) * e_n + s // 4, s % 4))
    rounds = []
    for _ in range(4):
        owner = {}

        def augment(src, seen):
            for edge in left:
                if edge[0] == src and edge[2] not in seen:
                    seen.add(edge[2])
                    if edge[2] not in owner or augment(owner[edge[2]][0], seen):
                        owner[edge[2]] = edge
                        return True
            return False

        for src in range(count):
            assert augment(src, set())
        chosen = list(owner.values())
        for edge in chosen:
            left.remove(edge)
        sent = np.zeros(count, np.int32)
        slot = np.zeros(count, np.int32)
        for edge in chosen:
            sent[edge[0]] = edge[1]
            slot[edge[2]] = edge[3]
        rounds.append(([(edge[0], edge[2]) for edge in chosen], sent, slot))
    return rounds


def transform_tables(e_n, land_shape, port_shape):
    parts = 2 * e_n
    shapes = (land_shape, port_shape)
    most = max(rows * (cols // 2 + 1) for rows, cols in shapes)
    per_part = -(-most // (16 * parts)) * 16
    forward, inverse, weight, counts = [], [], [], []
    for rows, cols in shapes:
        half = cols // 2 + 1
        point = np.arange(per_part * parts)
        valid = point < rows * half
        kr, f = point // half, point % half
        tiles = []
        for part in range(parts):
            c, e = part // e_n, part % e_n
            h = np.arange(rows // e_n) + e * (rows // e_n)
            w = np.arange(cols // 2) + c * (cols // 2)
            tiles.append((np.repeat(h, len(w)), np.tile(w, len(h))))
        cell_h = np.concatenate([tile[0] for tile in tiles])
        cell_w = np.concatenate([tile[1] for tile in tiles])
        size = rows * cols
        phase = (kr[:, None] * cell_h[None, :] * cols + f[:, None] * cell_w[None, :] * rows) % size
        angle = phase * (2.0 * math.pi / size)
        table = np.stack([np.cos(angle), -np.sin(angle)]) * valid[None, :, None]
        table = table.astype(np.float32).astype(jnp.bfloat16)
        cells = size // parts
        factor = np.where((f == 0) | (2 * f == cols), 1.0, 2.0) * valid
        counts.append([int(valid[p * per_part : (p + 1) * per_part].sum()) for p in range(parts)])
        for part in range(parts):
            order = [(part + step) % parts for step in range(parts)]
            own_points = slice(part * per_part, (part + 1) * per_part)
            own_cells = slice(part * cells, (part + 1) * cells)
            forward.append(
                np.concatenate([table[:, own_points, q * cells : (q + 1) * cells] for q in order], axis=2)
            )
            back = np.concatenate([table[:, q * per_part : (q + 1) * per_part, own_cells] for q in order], axis=1)
            inverse.append(np.ascontiguousarray(back.transpose(0, 2, 1)))
            weight.append(factor[own_points].astype(np.float32))
    forward, inverse = (np.stack(item).reshape(len(item), -1, item[0].shape[2]) for item in (forward, inverse))
    wide = max(-(-forward.shape[2] // 128), -(-inverse.shape[2] // 128)) * 128
    forward, inverse = (np.pad(item, ((0, 0), (0, 0), (0, wide - item.shape[2]))) for item in (forward, inverse))
    return np.concatenate([forward, inverse], axis=1), np.stack(weight), np.asarray(counts, np.int32)


SWAP = [(0, 1), (1, 0)]


def pick(table, index):
    return lax.dynamic_index_in_dim(jnp.asarray(table), index, 0, keepdims=False)


def partners(pieces, axes, step):
    count = lax.axis_size(axes)
    return lax.ppermute(pieces, axes, [(i, i ^ step) for i in range(count)])


def split_halves(land, port, place):
    channels = land.shape[3]
    shapes = [maps.shape[1:3] for maps in (land, port)]
    cells = shapes[0][0] * shapes[0][1] // 2

    def body(land_ref, port_ref, place_ref, mine_ref, theirs_ref):
        c = place_ref[1]
        for kind, ref in enumerate((land_ref, port_ref)):
            half = shapes[kind][1] // 2
            for out_ref, core in ((mine_ref, c), (theirs_ref, 1 - c)):
                at = pl.ds(pl.multiple_of(core * half, half), half)
                out_ref[kind] = ref[0, :, at, :].reshape(cells, channels)

    outs = [shape((2, cells, channels), land.dtype)] * 2
    return run(body, outs, (land, port, place), "split_halves", scalars=1)


def join_halves(mine, theirs, like, place):
    def body(mine_ref, theirs_ref, place_ref, *out_refs):
        c = place_ref[1]
        for kind, out_ref in enumerate(out_refs):
            _, rows, cols, channels = out_ref.shape
            half = cols // 2
            for ref, core in ((mine_ref, c), (theirs_ref, 1 - c)):
                at = pl.ds(pl.multiple_of(core * half, half), half)
                out_ref[0, :, at, :] = ref[kind].reshape(rows, half, channels)

    return run(body, [shape(maps.shape, maps.dtype) for maps in like], (mine, theirs, place), "join_halves", scalars=1)


def to_slots(mine, theirs, place):
    def body(mine_ref, theirs_ref, place_ref, *out_refs):
        here, c = place_ref[2], place_ref[1]
        for step, out_ref in enumerate(out_refs):
            there = here ^ step
            kind, core = there // 2, there % 2

            @pl.when(core == c)
            def _():
                out_ref[...] = mine_ref[kind]

            @pl.when(core != c)
            def _():
                out_ref[...] = theirs_ref[kind]

    outs = [shape(mine.shape[1:], mine.dtype)] * 4
    return run(body, outs, (mine, theirs, place), "to_slots", scalars=1)


def from_slots(pieces, place):
    def body(*refs):
        place_ref, mine_ref, theirs_ref = refs[-3:]
        here, c = place_ref[2], place_ref[1]
        for step in range(4):
            there = here ^ step
            kind, core = there // 2, there % 2

            @pl.when(core == c)
            def _():
                mine_ref[kind] = refs[step][...]

            @pl.when(core != c)
            def _():
                theirs_ref[kind] = refs[step][...]

    outs = [shape((2,) + pieces[0].shape, pieces[0].dtype)] * 2
    return run(body, outs, (*pieces, place), "from_slots", scalars=1)


def from_line(blocks, place):
    def body(blocks_ref, place_ref, mine_ref, theirs_ref):
        c = place_ref[1]
        for kind in range(2):
            mine_ref[kind] = blocks_ref[2 * kind + c]
            theirs_ref[kind] = blocks_ref[2 * kind + 1 - c]

    outs = [shape((2,) + blocks.shape[1:], blocks.dtype)] * 2
    return run(body, outs, (blocks, place), "from_line", scalars=1)


def in_order(pieces, here):
    rows = pieces[0].shape[0]

    def body(*refs):
        here_ref, out_ref = refs[-2:]
        for step in range(len(pieces)):
            out_ref[here_ref[0] ^ step] = refs[step][...]

    outs = [shape((len(pieces),) + pieces[0].shape, pieces[0].dtype)]
    out = run(body, outs, (*pieces, here), "in_order", scalars=1)[0]
    return out.reshape((len(pieces) * rows,) + pieces[0].shape[1:])


def for_partners(blocks, here):
    count = blocks.shape[0]

    def body(blocks_ref, here_ref, *out_refs):
        for step in range(count):
            out_refs[step][...] = blocks_ref[here_ref[0] ^ step]

    outs = [shape(blocks.shape[1:], blocks.dtype)] * count
    return run(body, outs, (blocks, here), "for_partners", scalars=1)


def advance(steps):
    return next(steps)


def finish(steps):
    while True:
        try:
            next(steps)
        except StopIteration as stop:
            return stop.value


def over_line(pieces):
    axes = ("k", "z", "e")
    return [pieces[0]] + [partners(pieces[step], axes, step) for step in range(1, lax.axis_size(axes))]


def over_plane(pieces):
    return [pieces[0]] + [partners(pieces[step], "g", step) for step in range(1, lax.axis_size("g"))]


def to_tile(land, port, rounds, place, here):
    channels = land.shape[3]
    if lax.axis_size("e") == 1:
        mine, theirs = split_halves(land, port, place)
        theirs = lax.ppermute(theirs, "c", SWAP)
        yield
        pieces = over_line(to_slots(mine, theirs, place))
        yield
        return in_order(pieces, here[0])
    me = lax.axis_index(LINE)
    units = []
    for maps in (land, port):
        cols = maps.shape[2] // 2
        units += [maps[0, :, :cols].reshape(-1, channels), maps[0, :, cols:].reshape(-1, channels)]
    units = jnp.stack(units)
    got = [lax.ppermute(pick(units, pick(sent, me)), LINE, pairs) for pairs, sent, _ in rounds]
    yield
    slots = np.stack([slot for _, _, slot in rounds], axis=1)
    order = pick(np.argsort(slots, axis=1).astype(np.int32), me)
    yield
    return jnp.concatenate([pick(jnp.stack(got), order[i]) for i in range(4)], axis=0)


def from_tile(tile, rounds, place, here):
    units = tile.reshape(4, -1, tile.shape[1])
    if lax.axis_size("e") == 1:
        pieces = over_line(for_partners(units, here[0]))
        yield
        mine, theirs = from_slots(pieces, place)
        return mine, lax.ppermute(theirs, "c", SWAP)
    me = lax.axis_index(LINE)
    got = [lax.ppermute(pick(units, pick(slot, me)), LINE, [(b, a) for a, b in pairs]) for pairs, _, slot in rounds]
    yield
    sents = np.stack([sent for _, sent, _ in rounds], axis=1)
    order = pick(np.argsort(sents, axis=1).astype(np.int32), me)
    both = jnp.stack([pick(jnp.stack(got), order[i]) for i in range(4)]).reshape((2, 2) + units.shape[1:])
    c = lax.axis_index("c")
    return (
        lax.dynamic_index_in_dim(both, c, 1, keepdims=False),
        lax.dynamic_index_in_dim(both, 1 - c, 1, keepdims=False),
    )


def shared(block):
    parts = lax.axis_size(PART)
    pieces = [
        lax.ppermute(block, PART, [((p + step) % parts, p) for p in range(parts)]) for step in range(1, parts)
    ]
    return pieces[0] if parts == 2 else jnp.concatenate(pieces, axis=0)


def gelu_parts(v):
    k = math.sqrt(2.0 / math.pi)
    square = v * v
    t = jnp.tanh(k * v * (1.0 + 0.044715 * square))
    half = 0.5 * (1.0 + t)
    return v * half, half + 0.5 * v * (1.0 - t * t) * (k * (1.0 + 3.0 * 0.044715 * square))


def gelu(v):
    return 0.5 * v * (1.0 + jnp.tanh(math.sqrt(2.0 / math.pi) * v * (1.0 + 0.044715 * (v * v))))


def dot(a, b):
    return lax.dot_general(a, b, (((1,), (0,)), ((), ())), preferred_element_type=f32)


def dot_t(a, b):
    return lax.dot_general(a, b, (((1,), (1,)), ((), ())), preferred_element_type=f32)


def outer(a, b):
    return lax.dot_general(a, b, (((0,), (0,)), ((), ())), preferred_element_type=f32)


def device_counts(counts, kind, width, e_n, z_n):
    row = lax.broadcasted_iota(jnp.int32, (width, 1), 0)
    part = row // (e_n * z_n) % 2 * e_n + row % e_n
    out = jnp.zeros((width, 1), f32)
    for p in range(len(counts[0])):
        out = jnp.where(part == p, jnp.where(kind == 0, float(counts[0][p]), float(counts[1][p])), out)
    return out


def moments(every, counts, total):
    sums, squares = every[:, 0, :], every[:, 1, :]
    mean = jnp.sum(sums, axis=0, keepdims=True) / total
    apart = sums / counts - mean
    square = jnp.sum(squares + counts * apart * apart, axis=0, keepdims=True)
    return mean, lax.rsqrt(square / total + EPS)


def emit(out_ref, first, second):
    both = jnp.concatenate([first, second], axis=0)
    out_ref[...] = jnp.broadcast_to(both[None], out_ref.shape)


def row_step(rows):
    return next(step for step in (64, 32, 16, 8) if rows % step == 0)


def sweep(rows, body, carry=0, step=None):
    step = step or row_step(rows)
    if rows == step:
        return body(slice(0, rows), carry)
    return lax.fori_loop(0, rows // step, lambda i, carry: body(pl.ds(pl.multiple_of(i * step, step), step), carry), carry)


def folded(values):
    return jnp.sum(values.reshape(values.shape[0] // 8, 8, values.shape[1]), axis=0)


def column(values):
    return jnp.sum(values, axis=0, keepdims=True)


def lanes_of(values, columns):
    return jnp.concatenate([values] * (columns // 128), axis=1)


def emit_moments(out_ref, ref, count, factor_ref=None):
    rows, columns = ref.shape
    zero = jnp.zeros((8, columns), f32)
    local_sum = column(sweep(rows, lambda at, acc: acc + folded(ref[at, :]), zero))
    mean = local_sum / count

    def squares(at, acc):
        centered = ref[at, :] - mean
        if factor_ref is not None:
            centered = jnp.where(lanes_of(factor_ref[at, :], columns) > 0.0, centered, 0.0)
        return acc + folded(centered * centered)

    emit(out_ref, local_sum, column(sweep(rows, squares, zero)))


def pair(columns):
    return jnp.zeros((8, columns), f32), jnp.zeros((8, columns), f32)


def add_sums(sums, q, normed):
    return sums[0] + folded(q), sums[1] + folded(q * normed)


def emit_sums(out_ref, sums):
    emit(out_ref, column(sums[0]), column(sums[1]))


def back_terms(every_ref, total):
    sums = jnp.sum(every_ref[...], axis=0)
    return sums, sums[0:1] / total, sums[1:2] / total


VMEM = pl.BlockSpec(memory_space=pltpu.VMEM)
SMEM = pl.BlockSpec(memory_space=pltpu.SMEM)
ANY = pl.BlockSpec(memory_space=pl.ANY)
HBM = pl.BlockSpec(memory_space=pltpu.HBM)


class Order:
    last = ()


def run(body, outs, ins, name, scratch=(), limit=8, scalars=0):
    vectors = len(ins) - scalars
    waits = len(Order.last)

    def ordered(*refs):
        body(*refs[:vectors], *refs[vectors + waits :])

    result = pl.pallas_call(
        ordered,
        out_shape=outs,
        in_specs=[HBM if item is None else VMEM for item in _spaces(ins[:vectors])] + [ANY] * waits + [SMEM] * scalars,
        out_specs=[VMEM] * len(outs),
        scratch_shapes=list(scratch),
        compiler_params=pltpu.CompilerParams(vmem_limit_bytes=limit * 1024 * 1024),
        name=name,
    )(*[item.array if isinstance(item, InPlace) else item for item in ins[:vectors]], *Order.last, *ins[vectors:])
    Order.last = (min(result, key=lambda item: math.prod(item.shape)),)
    return result


def hold(*arrays):
    Order.last = (*Order.last, *arrays)


def gate(every):
    def body(in_ref, out_ref):
        out_ref[...] = in_ref[0]

    run(body, [shape(every.shape[1:])], (every,), "gate")


class InPlace:
    def __init__(self, array):
        self.array = array


def _spaces(items):
    return [None if isinstance(item, InPlace) else item for item in items]


def shape(dims, kind=f32):
    return jax.ShapeDtypeStruct(tuple(dims), kind)


def reduce_first(x, reduce_kernel, width, narrow):
    cells = x.shape[0]
    half = reduce_kernel.shape[1]

    def body(x_ref, r_ref, reduced_ref, stats_ref):
        reduced_ref[...] = dot(x_ref[:, narrow:], r_ref[...])
        emit_moments(stats_ref, reduced_ref, float(cells))

    return run(body, [shape((cells, half)), shape((width, 2, half))], (x, reduce_kernel), "reduce_first")


def reduce_next(both, every, gain, bias, s, reduce_kernel, narrow, place, unit):
    cells, channels = both.shape
    half = reduce_kernel.shape[1]
    width = every.shape[0]

    def body(both_ref, every_ref, g_ref, b_ref, r_ref, place_ref, low_ref, reduced_ref, stats_ref, mi_ref, edge_ref):
        mean, inv = moments(every_ref[...], float(cells), float(cells * width))
        mi_ref[...] = jnp.concatenate([mean, inv], axis=0)
        gain_row, bias_row = g_ref[s : s + 1], b_ref[s : s + 1]

        def apply(at, carry):
            low_ref[at, :] = gelu((both_ref[at, :] - mean) * inv * gain_row + bias_row).astype(bf16)
            return carry

        sweep(cells, apply, step=32)
        reduced_ref[...] = dot(low_ref[:, narrow:], r_ref[...])
        emit_moments(stats_ref, reduced_ref, float(cells))
        edge_ref[...] = edge_rows(low_ref[...].astype(f32).reshape(-1, unit, channels), (), place_ref, unit)

    outs = [shape((cells, channels), bf16), shape((cells, half)), shape((width, 2, half)), shape((2, channels))]
    outs.append(shape((cells // unit + 4, channels), bf16))
    return run(body, outs, (both, every, gain, bias, reduce_kernel, place), "reduce_next", scalars=1)


def hidden_act(reduced, every, gain, bias, s):
    cells, channels = reduced.shape
    width = every.shape[0]

    def body(v_ref, every_ref, g_ref, b_ref, low_ref, hidden_ref, mi_ref):
        mean, inv = moments(every_ref[...], float(cells), float(cells * width))
        mi_ref[...] = jnp.concatenate([mean, inv], axis=0)
        gain_row, bias_row = g_ref[s : s + 1], b_ref[s : s + 1]

        def apply(at, carry):
            act = gelu((v_ref[at, :] - mean) * inv * gain_row + bias_row)
            hidden_ref[at, :] = act
            low_ref[at, :] = act.astype(bf16)
            return carry

        sweep(cells, apply)

    outs = [shape((cells, channels), bf16), shape((cells, channels)), shape((2, channels))]
    return run(body, outs, (reduced, every, gain, bias), "hidden_act")


def freq_act(mixed, every, gain, bias, s, factor, place, counts, e_n, z_n):
    points, channels = mixed.shape
    width = every.shape[0]

    def body(v_ref, every_ref, g_ref, b_ref, factor_ref, place_ref, low_ref, mi_ref):
        by_device = device_counts(counts, place_ref[0], width, e_n, z_n)
        mean, inv = moments(every_ref[...], by_device, jnp.sum(by_device))
        mi_ref[...] = jnp.concatenate([mean, inv], axis=0)
        gain_row, bias_row = g_ref[s : s + 1], b_ref[s : s + 1]

        def apply(at, carry):
            act = gelu((v_ref[at, :] - mean) * inv * gain_row + bias_row)
            low_ref[at, :] = (act * lanes_of(factor_ref[at, :], channels)).astype(bf16)
            return carry

        sweep(points, apply)

    outs = [shape((points, channels), bf16), shape((2, channels))]
    return run(body, outs, (mixed, every, gain, bias, factor, place), "freq_act", scalars=1)


def blocks_of(rows, most):
    count = -(-rows // most)
    while rows % (16 * count):
        count += 1
    return [slice(i * rows // count, (i + 1) * rows // count) for i in range(count)]


def spectrum_forward(table, own, others, freq_kernel, factor, scale, width):
    points = table.shape[1]
    cells, half = own.shape
    wide = freq_kernel.shape[1]

    def body(t_ref, own_ref, others_ref, w_ref, factor_ref, real_ref, imag_ref, mixed_ref, stats_ref):
        for side, out_ref in enumerate((real_ref, imag_ref)):
            for at in blocks_of(points, 272):
                z = dot(t_ref[side, at, :cells], own_ref[...]) + dot(t_ref[side, at, cells:], others_ref[...])
                out_ref[at, :] = (z * scale).astype(bf16)
        mixed_ref[...] = dot(real_ref[...], w_ref[:half]) + dot(imag_ref[...], w_ref[half:])
        count = jnp.sum(jnp.where(factor_ref[:, :1] > 0.0, 1.0, 0.0))
        emit_moments(stats_ref, mixed_ref, count, factor_ref)

    outs = [shape((points, half), bf16), shape((points, half), bf16), shape((points, wide)), shape((width, 2, wide))]
    return run(body, outs, (table, own, others, freq_kernel, factor), "spectrum_forward")


def inverse_forward(table, own, others, hidden, pre, expand_t, scale, width):
    cells = table.shape[1]
    half = hidden.shape[1]
    channels = pre.shape[1]
    narrow = channels - expand_t.shape[0]

    def body(t_ref, own_ref, others_ref, hidden_ref, pre_ref, e_ref, summed_ref, both_ref, stats_ref):
        freq = jnp.concatenate([own_ref[...], others_ref[...]], axis=0)
        real, imag = freq[:, :half], freq[:, half:]
        total = freq.shape[0]
        for at in blocks_of(cells, 256):
            returned = dot(t_ref[0, at, :total], real) + dot(t_ref[1, at, :total], imag)
            summed_ref[at, :] = (hidden_ref[at, :] + returned * scale).astype(bf16)
        both_ref[:, :narrow] = pre_ref[:, :narrow]
        for at in blocks_of(cells, 256):
            both_ref[at, narrow:] = pre_ref[at, narrow:] + dot_t(summed_ref[at, :], e_ref[...])
        emit_moments(stats_ref, both_ref, float(cells))

    outs = [shape((cells, half), bf16), shape((cells, channels)), shape((width, 2, channels))]
    return run(body, outs, (table, own, others, hidden, pre, expand_t), "inverse_forward")


def turn(both, every, gain, bias, s, x, cot):
    cells, channels = both.shape

    width = every.shape[0]

    def body(both_ref, every_ref, g_ref, b_ref, x_ref, cot_ref, out_ref, q_ref, sums_ref, mi_ref):
        mean, inv = moments(every_ref[...], float(cells), float(cells * width))
        mi_ref[...] = jnp.concatenate([mean, inv], axis=0)
        gain_row, bias_row = g_ref[s : s + 1], b_ref[s : s + 1]

        def apply(at, sums):
            normed = (both_ref[at, :] - mean) * inv
            state, slope = gelu_parts(normed * gain_row + bias_row)
            out_ref[at, :] = (x_ref[at, :].astype(f32) + state).astype(bf16)
            q = slope * cot_ref[at, :].astype(f32)
            q_ref[at, :] = q
            return add_sums(sums, q, normed)

        emit_sums(sums_ref, sweep(cells, apply, pair(channels), step=32))

    outs = [shape((cells, channels), bf16), shape((cells, channels)), shape((width, 2, channels)), shape((2, channels))]
    return run(body, outs, (both, every, gain, bias, x, cot), "turn")


def grad_pre(q, both, mi, every, gain, s, expand_t, total, place, unit):
    cells, channels = both.shape
    broad, half = expand_t.shape
    narrow = channels - broad

    def body(q_ref, both_ref, mi_ref, every_ref, g_ref, e_ref, place_ref, *refs):
        low_ref, summed_ref, summed_low_ref, sums_ref, edge_ref = refs
        sums, bias_term, gain_term = back_terms(every_ref, total)
        sums_ref[...] = sums
        mean, inv = mi_ref[0:1], mi_ref[1:2]
        gain_row = g_ref[s : s + 1] * inv

        def apply(at, carry):
            normed = (both_ref[at, :] - mean) * inv
            low_ref[at, :] = (gain_row * (q_ref[at, :] - bias_term - normed * gain_term)).astype(bf16)
            return carry

        sweep(cells, apply, step=32)
        summed_ref[...] = dot(low_ref[:, narrow:], e_ref[...])
        summed_low_ref[...] = summed_ref[...].astype(bf16)
        edge_ref[...] = edge_rows(low_ref[...].astype(f32).reshape(-1, unit, channels), (), place_ref, unit)

    outs = [shape((cells, channels), bf16), shape((cells, half)), shape((cells, half), bf16), shape((2, channels))]
    outs.append(shape((cells // unit + 4, channels), bf16))
    return run(body, outs, (q, both, mi, every, gain, expand_t, place), "grad_pre", scalars=1)


def spectrum_backward(table, own, others, mixed, mi, gain, bias, s, factor, scale, width):
    points, wide = mixed.shape
    cells, half = own.shape

    def body(t_ref, own_ref, others_ref, mixed_ref, mi_ref, g_ref, b_ref, factor_ref, *refs):
        q_ref, sums_ref, n_ref = refs
        mean, inv = mi_ref[0:1], mi_ref[1:2]
        gain_row, bias_row = g_ref[s : s + 1], b_ref[s : s + 1]
        for side in range(2):
            for at in blocks_of(points, 272):
                z = dot(t_ref[side, at, :cells], own_ref[...]) + dot(t_ref[side, at, cells:], others_ref[...])
                q_ref[at, side * half : (side + 1) * half] = z * scale

        def apply(at, sums):
            normed = (mixed_ref[at, :] - mean) * inv
            q = gelu_parts(normed * gain_row + bias_row)[1] * (q_ref[at, :] * lanes_of(factor_ref[at, :], wide))
            q_ref[at, :] = q
            n_ref[at, :] = normed
            return add_sums(sums, q, normed)

        emit_sums(sums_ref, sweep(points, apply, pair(wide)))

    outs = [shape((points, wide)), shape((width, 2, wide)), shape((points, wide))]
    return run(body, outs, (table, own, others, mixed, mi, gain, bias, factor), "spectrum_backward")


def norm_low(low_ref, q_ref, n_ref, mi_ref, gain_row, bias_term, gain_term):
    gain_row = gain_row * mi_ref[1:2]

    def apply(at, carry):
        low_ref[at, :] = (gain_row * (q_ref[at, :] - bias_term - n_ref[at, :] * gain_term)).astype(bf16)
        return carry

    sweep(q_ref.shape[0], apply)


def grad_mixed(q, normed, mi, every, gain, s, freq_kernel, place, totals):
    points, wide = q.shape

    def body(q_ref, n_ref, mi_ref, every_ref, g_ref, w_ref, place_ref, low_ref, back_ref, sums_ref):
        total = jnp.where(place_ref[0] == 0, float(totals[0]), float(totals[1]))
        sums, bias_term, gain_term = back_terms(every_ref, total)
        sums_ref[...] = sums
        norm_low(low_ref, q_ref, n_ref, mi_ref, g_ref[s : s + 1], bias_term, gain_term)
        back_ref[...] = dot_t(low_ref[...], w_ref[...]).astype(bf16)

    outs = [shape((points, wide), bf16), shape((points, wide), bf16), shape((2, wide))]
    return run(body, outs, (q, normed, mi, every, gain, freq_kernel, place), "grad_mixed", scalars=1)


def inverse_backward(table, own, others, summed, reduced, mi, gain, bias, s, scale, width):
    cells = table.shape[1]
    half = summed.shape[1]

    def body(t_ref, own_ref, others_ref, summed_ref, reduced_ref, mi_ref, g_ref, b_ref, *refs):
        q_ref, sums_ref, n_ref = refs
        mean, inv = mi_ref[0:1], mi_ref[1:2]
        gain_row, bias_row = g_ref[s : s + 1], b_ref[s : s + 1]
        freq = jnp.concatenate([own_ref[...], others_ref[...]], axis=0)
        real, imag = freq[:, :half], freq[:, half:]
        total = freq.shape[0]
        for at in blocks_of(cells, 256):
            back = dot(t_ref[0, at, :total], real) + dot(t_ref[1, at, :total], imag)
            q_ref[at, :] = summed_ref[at, :] + back * scale

        def apply(at, sums):
            normed = (reduced_ref[at, :] - mean) * inv
            q = gelu_parts(normed * gain_row + bias_row)[1] * q_ref[at, :]
            q_ref[at, :] = q
            n_ref[at, :] = normed
            return add_sums(sums, q, normed)

        emit_sums(sums_ref, sweep(cells, apply, pair(half)))

    outs = [shape((cells, half)), shape((width, 2, half)), shape((cells, half))]
    return run(body, outs, (table, own, others, summed, reduced, mi, gain, bias), "inverse_backward")


def grad_reduced(q, normed, mi, every, gain, s, reduce_kernel, total, conv_back, both, mi_3, gain_3, bias_3, width):
    cells, half = q.shape
    channels = both.shape[1]
    narrow = channels - reduce_kernel.shape[0]

    def body(q_ref, n_ref, mi_ref, every_ref, g_ref, r_ref, conv_ref, both_ref, mi3_ref, g3_ref, b3_ref, *refs):
        low_ref, out_ref, sums3_ref, sums_ref = refs
        sums, bias_term, gain_term = back_terms(every_ref, total)
        sums_ref[...] = sums
        norm_low(low_ref, q_ref, n_ref, mi_ref, g_ref[s : s + 1], bias_term, gain_term)
        out_ref[:, :narrow] = conv_ref[:, :narrow]
        for at in blocks_of(cells, 256):
            out_ref[at, narrow:] = conv_ref[at, narrow:] + dot_t(low_ref[at, :], r_ref[...])
        mean, inv = mi3_ref[0:1], mi3_ref[1:2]
        gain_row, bias_row = g3_ref[s - 1 : s], b3_ref[s - 1 : s]

        def apply(at, sums):
            normed_3 = (both_ref[at, :] - mean) * inv
            grad = gelu_parts(normed_3 * gain_row + bias_row)[1] * out_ref[at, :]
            out_ref[at, :] = grad
            return add_sums(sums, grad, normed_3)

        emit_sums(sums3_ref, sweep(cells, apply, pair(channels), step=32))

    outs = [shape((cells, half), bf16), shape((cells, channels)), shape((width, 2, channels)), shape((2, half))]
    ins = (q, normed, mi, every, gain, reduce_kernel, conv_back, both, mi_3, gain_3, bias_3)
    return run(body, outs, ins, "grad_reduced")


def grad_last(q, normed, mi, every, gain, s, total):
    cells, half = q.shape

    def body(q_ref, n_ref, mi_ref, every_ref, g_ref, *refs):
        low_ref, sums_ref = refs
        sums, bias_term, gain_term = back_terms(every_ref, total)
        sums_ref[...] = sums
        norm_low(low_ref, q_ref, n_ref, mi_ref, g_ref[s : s + 1], bias_term, gain_term)

    outs = [shape((cells, half), bf16), shape((2, half))]
    return run(body, outs, (q, normed, mi, every, gain), "grad_last")


def input_grad(cots, conv, late, reduce_kernel, place):
    channels = cots[0].shape[3]
    narrow = channels - reduce_kernel.shape[0]

    def body(cot0_ref, cot1_ref, *refs):
        conv_refs, late_refs, (r_ref, place_ref), out_refs = refs[:2], refs[2:4], refs[4:6], refs[6:]
        c = place_ref[1]
        for kind, (cot_ref, out_ref) in enumerate(zip((cot0_ref, cot1_ref), out_refs)):
            _, rows, cols, _ = cot_ref.shape
            half = cols // 2
            for side, core in enumerate((c, 1 - c)):
                at = pl.ds(pl.multiple_of(core * half, half), half)
                into = dot_t(late_refs[side][kind], r_ref[...]).reshape(rows, half, channels - narrow)
                base = conv_refs[side][kind].astype(f32).reshape(rows, half, channels) + cot_ref[0, :, at, :].astype(f32)
                out_ref[0, :, at, :narrow] = base[..., :narrow].astype(bf16)
                out_ref[0, :, at, narrow:] = (base[..., narrow:] + into).astype(bf16)

    outs = [shape(cot.shape, bf16) for cot in cots]
    ins = (*cots, *conv, *late, reduce_kernel, place)
    return run(body, outs, ins, "input_grad", limit=12, scalars=1)


def edge_rows(ends, above, place_ref, unit):
    first, last = ends[:, 0], ends[:, unit - 1]
    if not above:
        zeros = jnp.zeros((2, ends.shape[2]), f32)
        first, last = (jnp.concatenate([zeros, item, zeros], axis=0) for item in (first, last))
    land, left = place_ref[0] == 0, place_ref[1] == 0
    last = jnp.where(land, jnp.concatenate([last[1:], last[:1]], axis=0), last)
    first = jnp.where(land, jnp.concatenate([first[-1:], first[:-1]], axis=0), first)
    return jnp.where(left, last, first).astype(bf16)


def edge_cells(low, above, place, unit):
    channels = low.shape[1]
    blocks = low.shape[0] // unit + 4
    above = above or ()

    def body(*refs):
        *tile_refs, place_ref, out_ref = refs
        if above:
            wide = jnp.concatenate([tile_refs[1][...], tile_refs[0][...], tile_refs[2][...]], axis=0)
        else:
            wide = tile_refs[0][...]
        out_ref[...] = edge_rows(wide.astype(f32).reshape(-1, unit, channels), above, place_ref, unit)

    return run(body, [shape((blocks, channels), bf16)], (low, *above, place), "edge_cells", scalars=1)[0]


def surroundings(low, place, unit, edge=None):
    e_n = lax.axis_size("e")
    above = None
    if e_n > 1:
        ahead = [(e, e + 1) for e in range(e_n - 1)]
        above = (
            lax.ppermute(low[-2 * unit :], "e", ahead),
            lax.ppermute(low[: 2 * unit], "e", [(b, a) for a, b in ahead]),
        )
    if edge is None or above:
        edge = edge_cells(low, above, place, unit)
    return above, lax.ppermute(edge, "c", SWAP)


def shifted_columns(x_ref, above_refs, beside_ref, land, left, out_ref, unit):
    cells, channels = x_ref.shape
    blocks = cells // unit + 4
    block = lax.broadcasted_iota(jnp.int32, (blocks, unit, 1), 0)
    cell = lax.broadcasted_iota(jnp.int32, (blocks, unit, 1), 1)
    for lane in range(0, channels, 128):
        at = slice(lane, lane + 128)
        if above_refs:
            top, bottom = above_refs[0][:, at], above_refs[1][:, at]
        else:
            top = bottom = jnp.zeros((2 * unit, 128), bf16)
        wide = jnp.concatenate([top, x_ref[:, at], bottom], axis=0)
        out_ref[1, :, at] = wide
        wide = wide.astype(f32)
        beside = beside_ref[:, at].astype(f32)[:, None, :]
        for j, edge, odd in ((0, 0, 0), (2, unit - 1, 1)):
            moved = pltpu.roll(wide, 1 if j == 0 else blocks * unit - 1, 0).reshape(blocks, unit, 128)
            outer_side = (cell == edge) & (jnp.logical_not(land) | (block % 2 == odd))
            fill = jnp.where(left if j == 2 else jnp.logical_not(left), beside, 0.0)
            out_ref[j, :, at] = jnp.where(outer_side, fill, moved).reshape(blocks * unit, 128).astype(bf16)


def rows_at(i, first, count, land, unit):
    if i == 1:
        return slice(2 * unit + first, 2 * unit + first + count)
    step = jnp.where(land, 2 * unit, unit)
    return pl.ds(pl.multiple_of(2 * unit + first + (i - 1) * step, unit), count)


def conv_forward(low, above, beside, place, unit, local_kernel, global_t):
    cells, channels = low.shape
    narrow = local_kernel.shape[1] // 9
    padded = cells + 4 * unit
    extra = () if above is None else above
    start = 4 + len(extra)

    def body(*refs):
        x_ref, beside_ref, l_ref, g_ref = refs[0], *refs[1 + len(extra) : 4 + len(extra)]
        place_ref, pre_ref, cols_ref, wide_ref = refs[start:]
        land, left = place_ref[0] == 0, place_ref[1] == 0
        shifted_columns(x_ref, refs[1 : 1 + len(extra)], beside_ref, land, left, wide_ref, unit)
        cols_ref[...] = wide_ref[:, :, :narrow]
        for at in blocks_of(cells, 512):
            count = at.stop - at.start
            local = jnp.zeros((count, narrow), f32)
            patches = []
            for t in range(9):
                block = wide_ref[t % 3, rows_at(t // 3, at.start, count, land, unit), :]
                local = local + dot(block, l_ref[:, t * narrow : (t + 1) * narrow])
                patches.append(block[:, :narrow])
            pre_ref[at, :narrow] = local
            pre_ref[at, narrow:] = dot_t(jnp.concatenate(patches, axis=1), g_ref[...])

    outs = [shape((cells, channels)), shape((3, padded, narrow), bf16)]
    ins = (low, *extra, beside, local_kernel, global_t, place)
    return run(body, outs, ins, "conv_forward", [pltpu.VMEM((3, padded, channels), bf16)], 12, 1)


def conv_backward(low, above, beside, place, unit, local_kernel, global_t, kind):
    cells, channels = low.shape
    narrow = local_kernel.shape[1] // 9
    padded = cells + 4 * unit
    extra = () if above is None else above
    start = 4 + len(extra)

    def body(*refs):
        x_ref, beside_ref, l_ref, g_ref = refs[0], *refs[1 + len(extra) : 4 + len(extra)]
        place_ref, grad_ref, patches_ref, wide_ref = refs[start:]
        land, left = place_ref[0] == 0, place_ref[1] == 0
        shifted_columns(x_ref, refs[1 : 1 + len(extra)], beside_ref, land, left, wide_ref, unit)
        for at in blocks_of(cells, 512):
            count = at.stop - at.start
            into = jnp.zeros((count, narrow), f32)
            for t in range(9):
                block = wide_ref[2 - t % 3, rows_at(2 - t // 3, at.start, count, land, unit), :]
                patches_ref[at, t * narrow : (t + 1) * narrow] = block[:, :narrow]
                into = into + dot(block[:, narrow:], g_ref[:, t * narrow : (t + 1) * narrow])
            grad = dot_t(patches_ref[at, :], l_ref[...])
            grad_ref[at, :narrow] = (grad[:, :narrow] + into).astype(kind)
            grad_ref[at, narrow:] = grad[:, narrow:].astype(kind)

    outs = [shape((cells, channels), kind), shape((cells, 9 * narrow), bf16)]
    ins = (low, *extra, beside, local_kernel, global_t, place)
    return run(body, outs, ins, "conv_backward", [pltpu.VMEM((3, padded, channels), bf16)], 12, 1)


def spaced(rows, own, pad):
    row = lax.broadcasted_iota(jnp.int32, (rows, rows // own * pad), 0)
    place = lax.broadcasted_iota(jnp.int32, (rows, rows // own * pad), 1)
    return jnp.where(place == row // own * pad + row % own, 1.0, 0.0).astype(bf16)


def copies(values, count):
    def body(in_ref, out_ref):
        for i in range(count):
            out_ref[i] = in_ref[...]

    return run(body, [shape((count,) + values.shape, values.dtype)], (values,), "copies")[0]


def unpack_small(blocks, own, half):
    pad, columns = blocks.shape[-2:]
    devices = math.prod(blocks.shape[:-2])
    wide = columns - 2 * half

    def body(full_ref, *out_refs):
        split_small(full_ref[...].reshape(devices * pad, columns), spaced(devices * own, own, pad), wide, half, out_refs)

    outs = [shape((devices * own, width), bf16) for width in (wide, half, half)]
    return run(body, outs, (blocks,), "unpack_small", limit=12)


def split_small(full, place, wide, half, out_refs):
    full = dot(place, full).astype(bf16)
    out_refs[0][...] = full[:, :wide]
    out_refs[1][...] = full[:, wide : wide + half]
    out_refs[2][...] = full[:, wide + half : wide + 2 * half]


def unpack_kernels(full, sections, own_in, pad_in, own_out, half):
    devices, rows, columns = full.shape
    pad = (rows - sections * pad_in) // (2 * sections - 1)
    plain = own_in == pad_in
    wide = devices * own_out
    each = pad_in + pad

    def body(full_ref, *refs):
        out_refs, small_refs = refs[: 2 * sections], refs[2 * sections : 5 * sections - 3]
        local_ref, global_ref, small_ref, sems = refs[5 * sections - 3 :]
        copies = []
        for s in range(sections):
            target = out_refs[2 * s] if plain else local_ref.at[s]
            sources = [(s * each, pad_in, target), (s * each + pad_in, pad, global_ref.at[s])]
            if s:
                sources.append((sections * each + (s - 1) * pad, pad, small_ref.at[s - 1]))
            for k, (first, count, target) in enumerate(sources):
                source = full_ref.at[:, pl.ds(first, count), :]
                copies.append(pltpu.make_async_copy(source, target, sems.at[s, k]))
        for copy in copies:
            copy.start()
        for copy in copies:
            copy.wait()
        place = spaced(devices * own_out, own_out, pad)
        for s in range(sections):
            if not plain:
                block = local_ref[s].reshape(devices * pad_in, columns)
                out_refs[2 * s][...] = dot(spaced(devices * own_in, own_in, pad_in), block).astype(bf16)
            out_refs[2 * s + 1][...] = dot(place, global_ref[s].reshape(devices * pad, columns)).astype(bf16)
            if s:
                block = small_ref[s - 1].reshape(devices * pad, columns)
                split_small(block, place, wide, half, small_refs[3 * s - 3 : 3 * s])

    local = (devices, pad_in, columns) if plain else (devices * own_in, columns)
    outs = [shape(dims, bf16) for dims in (local, (devices * own_out, columns))] * sections
    outs += [shape((devices * own_out, width), bf16) for width in (wide, half, half)] * (sections - 1)
    scratch = [
        pltpu.VMEM((8,) * 4 if plain else (sections, devices, pad_in, columns), bf16),
        pltpu.VMEM((sections, devices, pad, columns), bf16),
        pltpu.VMEM((max(sections - 1, 1), devices, pad, columns), bf16),
        pltpu.SemaphoreType.DMA((sections, 3)),
    ]
    limit = 44 if plain else 52
    out = run(body, outs, (InPlace(full),), "unpack_kernels", scratch, limit)
    kernels = [(out[2 * s].reshape(devices * own_in, columns), out[2 * s + 1]) for s in range(sections)]
    return kernels, out[2 * sections :]


def early_grads(x_low, patches, grad_low, shifted, summed, place, unit, own, pad, alike):
    cells, channels = x_low.shape
    narrow = shifted.shape[2]
    broad = channels - narrow
    half = summed.shape[1]
    wide = 9 * narrow

    def body(x_ref, p_ref, g_ref, s_ref, m_ref, place_ref, *out_refs):
        land = place_ref[0] == 0
        out_refs[-1][...] = jnp.zeros((8, 128), f32)
        local_ref, other_ref, first = (out_refs[0], out_refs[0], wide) if alike else (*out_refs[:2], 0)
        x_t = x_ref[...].T
        for i in range(3):
            at = slice(3 * i * narrow, 3 * (i + 1) * narrow)
            local_ref[:, at] = dot(x_t, p_ref[:, at]).astype(bf16)
        grad_t = outer(spaced(broad, own, pad), g_ref[:, narrow:].T).astype(bf16)
        for i in range(3):
            taps = [s_ref[j, rows_at(i, 0, cells, land, unit), :] for j in range(3)]
            at = slice(first + 3 * i * narrow, first + 3 * (i + 1) * narrow)
            other_ref[:, at] = dot(grad_t, jnp.concatenate(taps, axis=1)).astype(bf16)
        other_ref[:, first + wide :] = dot(grad_t, m_ref[...]).astype(bf16)

    padded = broad // own * pad
    if alike:
        outs = [shape((channels, 2 * wide + half), bf16)]
    else:
        outs = [shape((channels, wide), bf16), shape((padded, wide + half), bf16)]
    outs.append(shape((8, 128)))
    ins = (x_low, patches, grad_low, shifted, summed, place)
    return run(body, outs, ins, "early_grads", limit=12, scalars=1)[:-1]


def freq_grads(real, imag, mixed_low, own, pad):
    wide = mixed_low.shape[1]

    def body(real_ref, imag_ref, m_ref, out_ref):
        freq = jnp.concatenate([outer(real_ref[...], m_ref[...]), outer(imag_ref[...], m_ref[...])], axis=0)
        out_ref[...] = outer(spaced(wide, own, pad), freq.astype(bf16)).astype(bf16)

    return run(body, [shape((wide // own * pad, wide), bf16)], (real, imag, mixed_low), "freq_grads")[0]


def reduce_grads(x_low, reduced_low, narrow, own, pad):
    broad = x_low.shape[1] - narrow

    def body(x_ref, r_ref, out_ref):
        reduce = outer(x_ref[:, narrow:], r_ref[...])
        out_ref[...] = outer(spaced(broad, own, pad), reduce.astype(bf16)).astype(bf16)

    outs = [shape((broad // own * pad, reduced_low.shape[1]), bf16)]
    return run(body, outs, (x_low, reduced_low), "reduce_grads")[0]


def core_parts(shares, here, g_n):
    parts = [part.reshape((g_n, 2, -1) + part.shape[1:]) for part in shares]
    rows, widths = parts[0].shape[2], [part.shape[3] for part in parts]
    starts = [sum(widths[:i]) for i in range(len(widths) + 1)]

    def body(*refs):
        c = refs[len(parts)][0]
        theirs_ref, mine_ref = refs[len(parts) + 1 :]
        for i, ref in enumerate(refs[: len(parts)]):
            at = slice(starts[i], starts[i + 1])
            for g in range(g_n):
                theirs_ref[g, :, at] = ref[g, 1 - c]
                mine_ref[g, :, at] = ref[g, c]

    outs = [shape((g_n, rows, starts[-1]), bf16)] * 2
    return run(body, outs, (*parts, here[2]), "core_parts", scalars=1)


def add_parts(mine, theirs, here):
    g_n = mine.shape[0]

    def body(mine_ref, theirs_ref, *refs):
        for step in range(g_n):
            g = refs[0][0] ^ step
            total = mine_ref[g].astype(f32) + theirs_ref[g].astype(f32)
            refs[1 + step][...] = total if step == 0 else total.astype(bf16)

    outs = [shape(mine.shape[1:], f32 if step == 0 else bf16) for step in range(g_n)]
    return run(body, outs, (mine, theirs, here[1]), "add_parts", scalars=1)


def add_plane(pieces, here, line_n):
    rows, columns = pieces[0].shape
    block = rows // line_n

    def body(*refs):
        for i in range(line_n):
            at = slice(i * block, (i + 1) * block)
            total = refs[0][at, :].astype(f32)
            for ref in refs[1:-1]:
                total = total + ref[at, :].astype(f32)
            refs[-1][i] = total.astype(bf16)

    return run(body, [shape((line_n, block, columns), bf16)], pieces, "add_plane")[0]


def owned(shares, here):
    g_n = lax.axis_size("g")
    line = ("k", "z", "e")
    line_n = lax.axis_size(line)
    theirs, mine = core_parts(shares, here, g_n)
    theirs = lax.ppermute(theirs, "c", SWAP)
    yield
    pieces = over_plane(add_parts(mine, theirs, here))
    yield
    sums = add_plane(pieces, here, line_n)
    yield
    if line_n > 4:
        pieces = [lax.all_to_all(sums, line, 0, 0, tiled=True)]
    else:
        pieces = over_line(for_partners(sums, here[0]))
    yield
    return total_of(pieces)


def owned_apart(shares):
    for axes in (("g", "c"), ("k", "z", "e")):
        shares = shares.reshape(lax.axis_size(axes), -1, shares.shape[-1])
        shares = lax.psum_scatter(shares, axes, scatter_dimension=0, tiled=True).reshape(-1, shares.shape[-1])
        if "g" in axes:
            yield
            shares = copies(shares, 1)[0]
    return shares


def total_of(blocks):
    dims = blocks[0].shape[-2:]

    def body(*refs):
        total = jnp.zeros(dims, f32)
        for ref in refs[:-1]:
            for part in [ref[i] for i in range(ref.shape[0])] if len(ref.shape) == 3 else [ref[...]]:
                total = total + part.astype(f32)
        refs[-1][...] = total

    return run(body, [shape(dims)], blocks, "total_of")[0]


def pack_sums(sums):
    widths = [item.shape[1] for item in sums]

    def body(*refs):
        refs[-1][...] = jnp.concatenate([ref[...] for ref in refs[:-1]], axis=1)

    return run(body, [shape((2, sum(widths)))], sums, "pack_sums")[0]


def results(totals, sums, other_sums, own_in, own_out, narrow, half, channels, alike):
    sections = len(totals)
    wides = (9 * narrow, 9 * narrow + half, 2 * half, half)
    flat, where = [], {}
    for s in range(sections):
        if s == 0:
            rest = [(1, 0)] + ([(2, 1), (3, 1)] if sections > 1 else []) + [(2, 0)]
        else:
            rest = [(1, s)]
        parts = [[(0, s), *rest]] if alike else [[(0, s)], rest]
        if s != 1:
            parts.append([(3, s)] if s == 0 else [(2, s), (3, s)])
        assert len(parts) == len(totals[s])
        for group, item in zip(parts, totals[s]):
            start = 0
            for part in group:
                where[part] = (len(flat), start)
                start += wides[part[0]]
            flat.append(item)

    def body(*refs):
        sums_ref, other_ref, local_ref, global_ref, reduce_ref, freq_ref, expand_ref, *norm_refs = refs[len(flat) :]
        for s in range(sections):

            def columns(part, start, count, rows):
                index, first = where[part, s]
                return refs[index][:rows, first + start : first + start + count].astype(f32)

            for t in range(9):
                local_ref[s, t] = columns(0, t * narrow, narrow, own_in)
                global_ref[t, :, s, :] = columns(1, t * narrow, narrow, own_out)
            expand_ref[:, s, :] = columns(1, 9 * narrow, half, own_out)
            freq_ref[:, s, :] = columns(2, 0, 2 * half, own_out)
            reduce_ref[:, s, :] = columns(3, 0, half, own_out)
        both = sums_ref[...] + other_ref[...]
        at = 0
        for s in range(sections):
            for index, wide in enumerate((half, 2 * half, channels)):
                norm_refs[2 * index][s : s + 1, :] = both[1:2, at : at + wide]
                norm_refs[2 * index + 1][s : s + 1, :] = both[0:1, at : at + wide]
                at += wide

    outs = [
        shape((sections, 9, own_in, narrow)),
        shape((9, own_out, sections, narrow)),
        shape((own_out, sections, half)),
        shape((own_out, sections, 2 * half)),
        shape((own_out, sections, half)),
    ]
    outs += [shape((sections, wide)) for wide in (half, half, 2 * half, 2 * half, channels, channels)]
    out = run(body, outs, (*flat, sums, other_sums), "results")
    return (
        out[0],
        jnp.transpose(out[1], (2, 0, 3, 1)),
        jnp.transpose(out[2], (1, 0, 2)),
        jnp.transpose(out[3], (1, 0, 2)),
        jnp.transpose(out[4], (1, 2, 0)),
        *out[5:],
    )


def pick_tables(table, factors, variant, size):
    points, cells = factors.shape[1], size // lax.axis_size(PART)
    columns = -(-points * lax.axis_size(PART) // 128) * 128

    def body(table_ref, factor_ref, v_ref, forward_ref, inverse_ref, out_ref, sems):
        v = v_ref[0]
        copies = []
        for side in range(2):
            source = table_ref.at[v, pl.ds(side * points, points), pl.ds(0, size)]
            copies.append(pltpu.make_async_copy(source, forward_ref.at[side], sems.at[0, side]))
            source = table_ref.at[v, pl.ds(2 * points + side * cells, cells), pl.ds(0, columns)]
            copies.append(pltpu.make_async_copy(source, inverse_ref.at[side], sems.at[1, side]))
        for copy in copies:
            copy.start()
        out_ref[...] = factor_ref[v]
        for copy in copies:
            copy.wait()

    outs = [shape((2, points, size), bf16), shape((2, cells, columns), bf16), shape(factors.shape[1:])]
    ins = (InPlace(table), factors, variant)
    return run(body, outs, ins, "pick_tables", [pltpu.SemaphoreType.DMA((2, 2))], 12, 1)


def per_device(plan, *args):
    (
        land,
        port,
        to_local,
        to_global,
        reduce_weight,
        freq_weight,
        expand_weight,
        spec_gain,
        spec_bias,
        freq_gain,
        freq_bias,
        out_gain,
        out_bias,
        cot_land,
        cot_port,
    ) = args
    rounds, table, weight_table, point_counts = plan
    sections = to_local.shape[0]
    devices = lax.axis_size(ALL)
    own_in = to_local.shape[2]
    own_out = to_global.shape[3]
    pad = -(-own_out // 16) * 16
    narrow = to_local.shape[3]
    channels = own_in * devices
    half = reduce_weight.shape[2]
    unit = port.shape[2] // 2
    k, c, part = lax.axis_index("k"), lax.axis_index("c"), lax.axis_index(PART)
    line_here = lax.axis_index(("k", "z", "e"))
    place = jnp.stack([k, c, line_here]).astype(jnp.int32)
    here = tuple(index.astype(jnp.int32).reshape(1) for index in (line_here, lax.axis_index("g"), c))
    variant = k * lax.axis_size(PART) + part
    g_n, z_n, e_n = lax.axis_size("g"), lax.axis_size("z"), lax.axis_size("e")
    width = lax.axis_size(KIND)

    pad_in = -(-own_in // 16) * 16
    Order.last = ()

    grow = ((0, 0), (0, pad - own_out), (0, 0))
    taps_local = jnp.transpose(to_local, (0, 2, 1, 3)).reshape(sections, own_in, 9 * narrow)
    taps_local = jnp.pad(taps_local, ((0, 0), (0, pad_in - own_in), (0, 0)))
    taps_global = jnp.pad(jnp.transpose(to_global, (0, 3, 1, 2)).reshape(sections, own_out, 9 * narrow), grow)
    packed = jnp.concatenate([freq_weight, reduce_weight, jnp.transpose(expand_weight, (0, 2, 1))], axis=2)
    packed = jnp.pad(packed, grow)
    small = copies(packed[0], lax.axis_size(("k", "z", "e")))
    small = lax.all_to_all(small, ("k", "z", "e"), 0, 0, tiled=True)
    later = jnp.pad(packed[1:], ((0, 0), (0, 0), (0, 9 * narrow - packed.shape[2])))
    taps = jnp.concatenate([taps_local, taps_global], axis=1)
    taps = jnp.concatenate([item.reshape(-1, 9 * narrow) for item in (taps, later)], axis=0)
    taps = lax.all_gather(taps, ALL)
    x_steps = to_tile(land, port, rounds, place, here)
    advance(x_steps)
    advance(x_steps)
    small = copies(small, lax.axis_size(("g", "c")))
    small = lax.all_to_all(small, ("g", "c"), 0, 0, tiled=True)
    variant = variant.reshape(1)
    size = land.shape[1] * land.shape[2] * lax.axis_size(("k", "z", "e"))
    forward, inverse, factor = pick_tables(jnp.asarray(table), jnp.asarray(np.repeat(weight_table[..., None], 128, axis=2)), variant, size)
    small = unpack_small(small, own_out, half)
    x = finish(x_steps)

    cells = x.shape[0]
    scale = 1.0 / math.sqrt(size)
    cell_total = float(g_n * z_n * size)
    point_totals = [int(item.sum()) * g_n * z_n for item in point_counts]

    def exchange(stats):
        every = lax.all_to_all(stats, KIND, 0, 0, tiled=True)
        Order.last = (every,)
        return every

    kept = []
    for s in range(sections):
        freq_kernel, reduce_kernel, expand_t = small[3 * s : 3 * s + 3]
        if s == 0:
            low = x
            reduced, stats = reduce_first(x, reduce_kernel, width, narrow)
        else:
            low, reduced, stats, kept[-1]["mi_3"], edge = reduce_next(
                both, every, out_gain, out_bias, s - 1, reduce_kernel, narrow, place, unit
            )
        every = exchange(stats)
        if s == 1:
            gate(every)
            cot = finish(cot_steps)
        if s == 0:
            cot_steps = to_tile(cot_land, cot_port, rounds, place, here)
            advance(cot_steps)
        else:
            above, beside = surroundings(low, place, unit, edge)
        hidden_low, hidden, mi_1 = hidden_act(reduced, every, spec_gain, spec_bias, s)
        others = shared(hidden_low)
        if s > 0:
            pre, shifted = conv_forward(low, above, beside, place, unit, *kernels[s])
        real, imag, mixed, stats = spectrum_forward(forward, hidden_low, others, freq_kernel, factor, scale, width)
        every = exchange(stats)
        if s == 0:
            above, beside = surroundings(low, place, unit)
            kernels, more = unpack_kernels(taps, sections, own_in, pad_in, own_out, half)
            small = [*small, *more]
            hold(beside)
        freq_low, mi_2 = freq_act(mixed, every, freq_gain, freq_bias, s, factor, place, point_counts, e_n, z_n)
        others = shared(freq_low)
        if s == 0:
            pre, shifted = conv_forward(low, above, beside, place, unit, *kernels[s])
            advance(cot_steps)
        summed, both, stats = inverse_forward(inverse, freq_low, others, hidden, pre, expand_t, scale, width)
        every = exchange(stats)
        kept.append(
            dict(low=low, shifted=shifted, reduced=reduced, mi_1=mi_1, real=real, imag=imag, mixed=mixed, mi_2=mi_2, summed=summed, both=both)
        )
    if sections == 1:
        cot = finish(cot_steps)
    out, q_3, sums, kept[-1]["mi_3"] = turn(both, every, out_gain, out_bias, sections - 1, x, cot)

    alike = own_in == pad

    def late_grads(item):
        return (
            freq_grads(item["real"], item["imag"], mixed_low, own_out, pad),
            reduce_grads(item["low"], reduced_low, narrow, own_out, pad),
        )

    norm_sums = [None] * sections
    totals = [None] * sections
    last_steps = None
    for s in reversed(range(sections)):
        freq_kernel, reduce_kernel, expand_t = small[3 * s : 3 * s + 3]
        item = kept[s]
        every = exchange(sums)
        if s == sections - 2:
            gate(every)
            out_parts = finish(out_steps)
        low, summed, summed_low, sums_3, edge = grad_pre(
            q_3, item["both"], item["mi_3"], every, out_gain, s, expand_t, cell_total, place, unit
        )
        others = shared(summed_low)
        above, beside = surroundings(low, place, unit, edge)

        def kernel_grads():
            return early_grads(
                item["low"], patches, low, item["shifted"], item["summed"], place, unit, own_out, pad, alike
            )

        if s == 0:
            conv_back, patches = conv_backward(low, above, beside, place, unit, *kernels[s], f32 if s > 0 else bf16)
            conv_steps = from_tile(conv_back, rounds, place, here)
            advance(conv_steps)
            grads = kernel_grads()
            if sections > 1:
                grads = (*grads, *late_grads(kept[1]))
        else:
            hold(beside)
        q, sums, normed = spectrum_backward(
            forward, summed_low, others, item["mixed"], item["mi_2"], freq_gain, freq_bias, s, factor, scale, width
        )
        every = exchange(sums)
        if s == 0:
            gate(every)
            conv_parts = finish(conv_steps)
        mixed_low, back, sums_2 = grad_mixed(
            q, normed, item["mi_2"], every, freq_gain, s, freq_kernel, place, point_totals
        )
        others = shared(back)
        if s > 0:
            conv_back, patches = conv_backward(low, above, beside, place, unit, *kernels[s], f32 if s > 0 else bf16)
            grads = kernel_grads()
            totals[s] = [owned_apart(grad) for grad in grads]
            for steps in totals[s]:
                advance(steps)
        else:
            grads = (*grads, freq_grads(item["real"], item["imag"], mixed_low, own_out, pad))
            if alike:
                last_steps = [owned(grads, here)]
            else:
                last_steps = [owned(grads[:1], here), owned(grads[1:], here)]
            for steps in last_steps:
                advance(steps)
        if s == sections - 1:
            out_steps = from_tile(out, rounds, place, here)
            advance(out_steps)
        q, sums, normed = inverse_backward(
            inverse, back, others, summed, item["reduced"], item["mi_1"], spec_gain, spec_bias, s, scale, width
        )
        every = exchange(sums)
        if s > 0:
            below = kept[s - 1]
            reduced_low, q_3, sums, sums_1 = grad_reduced(
                q, normed, item["mi_1"], every, spec_gain, s, reduce_kernel, cell_total,
                conv_back, below["both"], below["mi_3"], out_gain, out_bias, width,
            )
            if s > 1:
                totals[s].append(owned_apart(jnp.concatenate(late_grads(item), axis=1)))
                advance(totals[s][-1])
        else:
            reduced_low, sums_1 = grad_last(q, normed, item["mi_1"], every, spec_gain, s, cell_total)
            for k in range(1, sections):
                totals[k] = [finish(steps) for steps in totals[k]]
            for steps in last_steps:
                advance(steps)
        norm_sums[s] = (sums_1, sums_2, sums_3)

    if sections == 1:
        out_parts = finish(out_steps)
    end = lax.all_to_all(reduced_low.reshape(4, -1, half), ("k", "z"), 0, 0, tiled=True) if e_n == 1 else None
    land_out, port_out = join_halves(*out_parts, (land, port), place)
    if e_n == 1:
        mine, theirs = from_line(end, place)
        end_parts = mine, lax.ppermute(theirs, "c", SWAP)
    else:
        end_parts = finish(from_tile(reduced_low, rounds, place, here))
    reduce_grad = reduce_grads(kept[0]["low"], reduced_low, narrow, own_out, pad)
    reduce_grad = lax.all_to_all(reduce_grad.reshape(devices, pad, half), ALL, 0, 0, tiled=True)
    for steps in last_steps:
        advance(steps)
    for steps in last_steps:
        advance(steps)
    packed_sums = pack_sums([item for s in range(sections) for item in norm_sums[s]])
    other_sums = lax.ppermute(packed_sums, "k", SWAP)
    land_grad, port_grad = input_grad((cot_land, cot_port), conv_parts, end_parts, small[1], place)
    totals[0] = [finish(steps) for steps in last_steps] + [total_of([reduce_grad])]
    rest = results(totals, packed_sums, other_sums, own_in, own_out, narrow, half, channels, alike)
    return (land_out, port_out, land_grad, port_grad, *rest)


def solution(mesh):
    f_n, s_n = mesh.shape["fsdp"], mesh.shape["sp"]
    e_n = s_n // 4
    fine = Mesh(np.asarray(mesh.devices).reshape(f_n // 2, 2, 2, 2, e_n), ALL)
    maps = P(("g", "c"), ("k", "z", "e"), None, None)
    split = ALL

    def whole(*args):
        land, port = args[0], args[1]
        plan = (
            routes(e_n),
            *transform_tables(e_n, land.shape[1:3], port.shape[1:3]),
        )
        weights = (
            P(None, None, split, None),
            P(None, None, None, split),
            P(None, split, None),
            P(None, split, None),
            P(None, None, split),
        )
        return jax.shard_map(
            lambda *local: per_device(plan, *local),
            mesh=fine,
            in_specs=(maps, maps, *weights, P(), P(), P(), P(), P(), P(), maps, maps),
            out_specs=(maps, maps, maps, maps, *weights, P(), P(), P(), P(), P(), P()),
            check_vma=False,
        )(*args)

    return whole
```
